256 devices in a mesh: frame: 32 (over z_hi, y, core), mlp: 8 (over z_lo, x).
Axes of the slice: x: 4, y: 4, z: 8 (z_hi: 4, z_lo: 2; z = z_hi * 2 + z_lo), core: 2. Of those that a mesh axis runs over, the one named last changes fastest.
Arguments:
- tokens: bfloat16 [6, 64, 256, 1024], P(None, 'frame'), may hold values from -8 to 8
- output_gradient: bfloat16 [6, 64, 256, 1024], P(None, 'frame'), may hold values from -6 to 6
- gain: float32 [1024], replicated, may hold values from 0.25 to 1.75
- qkv_weight: bfloat16 [1024, 3, 1024], P(None, None, 'mlp'), may hold values from -1 to 1
- out_weight: bfloat16 [1024, 1024], P('mlp'), may hold values from -0.1875 to 0.1875
Outputs:
- token_gradient: bfloat16 [6, 64, 256, 1024], P(None, 'frame')
- grad_qkv: float32 [1024, 3, 1024], P('frame', None, 'mlp')
- grad_out_weight: float32 [1024, 1024], P('mlp', 'frame')
- gain_gradient: float32 [1024], P('frame')
The draws below stay inside these ranges and needn't reach their ends.
All inputs are finite; a program needn't handle non-finite values.
Results may differ from the reference program's by a relative error of at most 0.035.
The reference program's roundings to bfloat16 on the way count: a program that leaves them out, or rounds other values in their place, can miss the bound.
Values may be sent and summed in bfloat16 or wider, within the bound.
A program may use at most 128 MiB of HBM per device.

```python
import jax
import jax.numpy as jnp
from jax import lax

D = 1024
HEADS = 16
HD = 64
PATCHES = 256
CLIPS = 6
FRAMES = 64
N_MLP = 8


def draw_tokens(key, part):
    key = jax.random.fold_in(key, 11)
    first = jax.random.fold_in(key, 0)
    shape = (CLIPS, FRAMES, PATCHES, D)
    values = jax.random.normal(first, shape, jnp.float32)
    return jnp.clip(values, -8.0, 8.0).astype(jnp.bfloat16)


def draw_qkv_weight(key, part):
    key = jax.random.fold_in(key, 23)
    first = jax.random.fold_in(key, 0)
    values = jax.random.normal(first, (D, 3, D), jnp.float32) / jnp.sqrt(jnp.float32(D))
    return jnp.clip(values, -1.0, 1.0).astype(jnp.bfloat16)


def level_of(stream_key, shape, cuts, smallest, high):
    level, own = 1.0, jax.random.fold_in(stream_key, 6)
    for dim, parts in cuts:
        heights = jnp.exp(jax.random.uniform(jax.random.fold_in(own, dim), (parts,), jnp.float32, smallest / len(cuts), high / len(cuts)))
        level = level * jnp.repeat(heights, shape[dim] // parts).reshape([-1 if axis == dim else 1 for axis in range(len(shape))])
    return level


def gaussian(key, dims, scale, bound, cuts=(), kind=jnp.bfloat16):
    result = scale * jax.random.normal(key, dims, jnp.float32)
    if cuts:
        result = result * level_of(key, dims, cuts, -0.22, 0.18)
    return jnp.clip(result, -bound, bound).astype(kind)


def setup_inputs(seed: int = 0) -> dict:
    key_of = jax.random.split(jax.random.key(seed), 6)
    return {
        "tokens": draw_tokens(jax.random.fold_in(key_of[5], 71), 0),
        "output_gradient": gaussian(key_of[1], (CLIPS, FRAMES, PATCHES, D), 1.0, 6.0, ((1, 32),)),
        "gain": jnp.clip(1.0 + 0.15 * jax.random.normal(key_of[2], (D,), jnp.float32), 0.25, 1.75),
        "qkv_weight": draw_qkv_weight(jax.random.fold_in(key_of[5], 71), 0),
        "out_weight": gaussian(key_of[4], (D, D), D ** -0.5, 0.1875, ((0, 8),)),
    }


def apply_norm(tokens, gain):
    values = tokens.astype(jnp.float32)
    centered_rows = values - lax.optimization_barrier(jnp.mean(values, axis=-1, keepdims=True))
    inverse_deviation = lax.rsqrt(lax.optimization_barrier(jnp.mean(centered_rows * centered_rows, axis=-1, keepdims=True)) + 1e-05)
    standardized_input = centered_rows * inverse_deviation
    return (standardized_input, inverse_deviation, (standardized_input * gain).astype(jnp.bfloat16))

def round_keep(value):
    return lax.optimization_barrier(value.astype(jnp.bfloat16)).astype(jnp.float32)

def temporal(query, keys, values, d_out, factor):
    qf = query.astype(jnp.float32)
    kf = keys.astype(jnp.float32)
    vf = values.astype(jnp.float32)
    df = d_out.astype(jnp.float32)
    scores = jnp.einsum('nfphe,ngphe->nphfg', qf, kf) * factor
    top = lax.optimization_barrier(jnp.max(scores, axis=-1, keepdims=True))
    expo = jnp.exp(scores - top)
    probs = expo / lax.optimization_barrier(jnp.sum(expo, axis=-1, keepdims=True))
    probs_b = round_keep(probs)
    attn_out = jnp.einsum('nphfg,ngphe->nfphe', probs_b, vf).astype(jnp.bfloat16)
    dprob = jnp.einsum('nfphe,ngphe->nphfg', df, vf)
    d_value = jnp.einsum('nphfg,nfphe->ngphe', probs_b, df).astype(jnp.bfloat16)
    delta = lax.optimization_barrier(jnp.sum(probs * dprob, axis=-1, keepdims=True))
    dscore = round_keep(probs * (dprob - delta) * factor)
    d_query = jnp.einsum('nphfg,ngphe->nfphe', dscore, kf).astype(jnp.bfloat16)
    d_key = jnp.einsum('nphfg,nfphe->ngphe', dscore, qf).astype(jnp.bfloat16)
    return (attn_out, d_query, d_key, d_value)

def reference(tokens, output_gradient, gain, qkv_weight, out_weight):
    clips, frames, patches, width = tokens.shape
    standardized_input, inverse_deviation, normalized_rows = apply_norm(tokens, gain)
    rows2 = normalized_rows.reshape(-1, width)
    weight2 = qkv_weight.reshape(width, 3 * width)
    proj = jnp.dot(rows2, weight2, preferred_element_type=jnp.float32).astype(jnp.bfloat16)
    proj = proj.reshape(clips, frames, patches, 3, HEADS, HD)
    grad2 = output_gradient.reshape(-1, width)
    d_attn = jnp.dot(grad2, out_weight.T, preferred_element_type=jnp.float32).astype(jnp.bfloat16)
    d_attn = d_attn.reshape(clips, frames, patches, HEADS, HD)
    attn_out, d_query, d_key, d_value = temporal(proj[:, :, :, 0], proj[:, :, :, 1], proj[:, :, :, 2], d_attn, HD ** (-0.5))
    grad_out_weight = jnp.dot(attn_out.reshape(-1, width).T, grad2, preferred_element_type=jnp.float32)
    dstack = jnp.stack([d_query, d_key, d_value], axis=3).reshape(-1, 3 * width)
    group_cols = width // N_MLP
    dgroups = dstack.reshape(-1, 3, N_MLP, group_cols)
    wgroups = qkv_weight.reshape(width, 3, N_MLP, group_cols)
    normalized_gradient = jnp.zeros((dstack.shape[0], width), jnp.float32)
    for group in range(N_MLP):
        dpart = dgroups[:, :, group, :].reshape(-1, 3 * group_cols)
        wpart = wgroups[:, :, group, :].reshape(width, 3 * group_cols)
        partial_value = jnp.dot(dpart, wpart.T, preferred_element_type=jnp.float32)
        normalized_gradient = normalized_gradient + round_keep(partial_value)
    normalized_gradient = normalized_gradient.reshape(clips, frames, patches, width)
    grad_qkv = jnp.dot(rows2.T, dstack, preferred_element_type=jnp.float32).reshape(width, 3, width)
    gain_gradient = lax.optimization_barrier(jnp.sum(normalized_gradient * standardized_input, axis=(0, 1, 2)))
    backward_pass = normalized_gradient * gain
    inner_product = backward_pass - lax.optimization_barrier(jnp.mean(backward_pass, axis=-1, keepdims=True)) - standardized_input * lax.optimization_barrier(jnp.mean(backward_pass * standardized_input, axis=-1, keepdims=True))
    token_gradient = (output_gradient.astype(jnp.float32) + inverse_deviation * inner_product).astype(jnp.bfloat16)
    return (token_gradient, grad_qkv, grad_out_weight, gain_gradient)
```

```python
import functools

import numpy as np

import jax
import jax.numpy as jnp
from jax import lax
from jax.experimental import pallas as pl
from jax.experimental.pallas import tpu as pltpu
from jax.sharding import PartitionSpec as P

MESH = pl.DeviceIdType.MESH
BF = jnp.bfloat16
F32 = jnp.float32
D = 1024
FACTOR = 64 ** (-0.5)
NEG = -1e30


def one_hot(shape, perm):
    index = np.arange(384).reshape(shape).transpose(perm).reshape(-1)
    return np.eye(384, dtype=np.float32)[index]


PACK = one_hot((2, 12, 8, 2), (2, 0, 3, 1))
GROUP = one_hot((8, 2, 12, 2), (1, 2, 0, 3))
REPACK = one_hot((2, 12, 8, 2), (2, 0, 1, 3))
UNPACK = one_hot((8, 2, 2, 12), (1, 3, 0, 2))


def place():
    f, m = lax.axis_index("frame"), lax.axis_index("mlp")
    return f, m, f // 2, f % 2, m // 4, m % 4


def remote(src, dst, send, recv, f, m):
    return pltpu.make_async_remote_copy(
        src_ref=src, dst_ref=dst, send_sem=send, recv_sem=recv, device_id=(f, m), device_id_type=MESH
    )


def greet(barrier, f, m):
    pl.semaphore_signal(barrier, inc=1, device_id=(f, m), device_id_type=MESH)


def scatter_kernel(
    tok, og, wc, perm, recv, wout, xin, sbuf, loc, wloc, asend, arecv, fsend, frecv, ssend, srecv, rsend, rrecv
):
    f, m, g, c, z, x = place()
    sib = g * 2 + 1 - c
    pf, pm = g * 2 + 1 - c, (1 - z) * 4 + x
    mr, ml = z * 4 + (x + 1) % 4, z * 4 + (x + 3) % 4
    xl, xr, xf = (x + 3) % 4, (x + 1) % 4, (x + 2) % 4
    rows = pl.ds(pl.multiple_of(m * 32, 32), 32)
    in_tok = pltpu.make_async_copy(tok.at[:, rows, :], xin.at[0], loc.at[0])
    in_og = pltpu.make_async_copy(og.at[:, rows, :], xin.at[1], loc.at[1])
    in_tok.start()
    in_og.start()

    barrier = pltpu.get_barrier_semaphore()

    def hello(k, _):
        greet(barrier, ((g + k) % 16) * 2 + c, m)
        return 0

    lax.fori_loop(1, 16, hello, 0)
    greet(barrier, sib, m)
    greet(barrier, pf, pm)
    greet(barrier, f, mr)
    greet(barrier, f, ml)
    pl.semaphore_wait(barrier, 19)

    halves = (pl.ds(0, 512), pl.ds(512, 512))

    def ring(src, slot, h, i, mm):
        return remote(src, wout.at[slot, halves[h]], rsend.at[i], rrecv.at[i], f, mm)

    own = c == z
    own_copy = pltpu.make_async_copy(wc, wout.at[x], wloc)

    def swap(h):
        return remote(wc.at[halves[h]], wout.at[x, halves[h]], ssend.at[h], srecv.at[h], pf, pm)

    @pl.when(own)
    def _():
        ring(wc.at[halves[0]], x, 0, 0, mr).start()
        ring(wc.at[halves[1]], x, 1, 2, ml).start()
        ring(wc.at[halves[1]], x, 1, 1, mr).start()
        ring(wc.at[halves[0]], x, 0, 3, ml).start()
        own_copy.start()

    @pl.when(jnp.logical_not(own))
    def _():
        swap(0).start()
        swap(1).start()

    in_tok.wait()
    in_og.wait()
    for gh in range(2):
        block = xin[:, :, 16 * gh : 16 * gh + 16, :].reshape(384, D)
        packed = jnp.dot(perm[...], block, preferred_element_type=F32).astype(BF)
        sbuf[8 * gh : 8 * gh + 8] = packed.reshape(8, 48, D)

    def a2a(k):
        return remote(sbuf.at[(g + k) % 16], recv.at[c, g], asend.at[k], arecv.at[k], ((g + k) % 16) * 2 + c, m)

    def send(k, _):
        a2a(k).start()
        return 0

    lax.fori_loop(1, 16, send, 0)
    keep = pltpu.make_async_copy(sbuf.at[g], recv.at[c, g], loc.at[2])
    keep.start()

    def forward(k, src):
        slot = (g + 16 - k) % 16
        return remote(src, recv.at[c, slot], fsend.at[k], frecv.at[k], sib, m)

    forward(0, sbuf.at[g]).start()

    @pl.when(jnp.logical_not(own))
    def _():
        swap(0).wait_recv()
        ring(wout.at[x, halves[0]], x, 0, 0, mr).start()
        ring(wout.at[x, halves[0]], x, 0, 3, ml).start()
        swap(1).wait_recv()
        ring(wout.at[x, halves[1]], x, 1, 2, ml).start()
        ring(wout.at[x, halves[1]], x, 1, 1, mr).start()

    def relay(k, _):
        slot = (g + 16 - k) % 16
        remote(sbuf.at[0], recv.at[c, slot], asend.at[k], arecv.at[k], f, m).wait_recv()
        forward(k, recv.at[c, slot]).start()
        return 0

    def arrived(slot, h, i):
        ring(wout.at[slot, halves[h]], slot, h, i, mr).wait_recv()

    lax.fori_loop(1, 9, relay, 0)
    arrived(xl, 0, 0)
    ring(wout.at[xl, halves[0]], xl, 0, 4, mr).start()
    arrived(xr, 1, 2)
    ring(wout.at[xr, halves[1]], xr, 1, 5, ml).start()
    lax.fori_loop(9, 16, relay, 0)
    arrived(xl, 1, 1)
    arrived(xr, 0, 3)
    arrived(xf, 0, 4)
    arrived(xf, 1, 5)

    def finish(k, _):
        slot = (g + 16 - k) % 16
        a2a(k).wait_send()
        forward(k, recv.at[c, slot]).wait_send()
        remote(sbuf.at[0], recv.at[1 - c, slot], fsend.at[k], frecv.at[k], sib, m).wait_recv()
        return 0

    lax.fori_loop(1, 16, finish, 0)
    forward(0, sbuf.at[g]).wait_send()
    remote(sbuf.at[0], recv.at[1 - c, g], fsend.at[0], frecv.at[0], sib, m).wait_recv()
    keep.wait()
    for i, (slot, h) in enumerate(((x, 0), (x, 1), (x, 1), (x, 0), (xl, 0), (xr, 1))):
        ring(wout.at[slot, halves[h]], slot, h, i, mr).wait_send()

    @pl.when(own)
    def _():
        own_copy.wait()

    @pl.when(jnp.logical_not(own))
    def _():
        swap(0).wait_send()
        swap(1).wait_send()


def scatter(tok, og, wc, perm):
    any_spec = pl.BlockSpec(memory_space=pl.ANY)
    dma = pltpu.SemaphoreType.DMA
    return pl.pallas_call(
        scatter_kernel,
        out_shape=(jax.ShapeDtypeStruct((2, 16, 48, D), BF), jax.ShapeDtypeStruct((4, D, 512), BF)),
        in_specs=[any_spec, any_spec, any_spec, pl.BlockSpec(memory_space=pltpu.VMEM)],
        out_specs=(any_spec, any_spec),
        scratch_shapes=[
            pltpu.VMEM((2, 12, 32, D), BF),
            pltpu.VMEM((16, 48, D), BF),
            dma((3,)),
            dma,
            dma((16,)),
            dma((16,)),
            dma((16,)),
            dma((16,)),
            dma((2,)),
            dma((2,)),
            dma((6,)),
            dma((6,)),
        ],
        compiler_params=pltpu.CompilerParams(
            collective_id=0, has_side_effects=True, vmem_limit_bytes=32 * 2**20
        ),
        name="scatter",
    )(tok, og, wc, perm)


def standardize(values):
    centered = values - jnp.mean(values, axis=-1, keepdims=True)
    rstd = lax.rsqrt(jnp.mean(centered * centered, axis=-1, keepdims=True) + 1e-05)
    return centered * rstd, rstd


def dot_t(a, b):
    return lax.dot_general(a, b, (((1,), (1,)), ((), ())), preferred_element_type=F32)


def t_dot(a, b):
    return lax.dot_general(a, b, (((0,), (0,)), ((), ())), preferred_element_type=F32)


def attend(q, k, v, d, allowed, first):
    zero = jnp.zeros_like(k)
    k2 = jnp.concatenate([jnp.where(first, k, zero), jnp.where(first, zero, k)], axis=0)
    v2 = jnp.concatenate([jnp.where(first, v, zero), jnp.where(first, zero, v)], axis=0)
    scores = dot_t(q, k2) * FACTOR
    dprob = dot_t(d, v2)
    probs, dscore = [], []
    for h in range(2):
        s = jnp.where(allowed, scores[:, 128 * h : 128 * h + 128], NEG)
        e = jnp.exp(s - jnp.max(s, axis=-1, keepdims=True))
        p = e * (1.0 / jnp.sum(e, axis=-1, keepdims=True))
        dp = dprob[:, 128 * h : 128 * h + 128]
        delta = jnp.sum(p * dp, axis=-1, keepdims=True)
        probs.append(p.astype(BF))
        dscore.append((p * (dp - delta) * FACTOR).astype(BF))
    probs = jnp.concatenate(probs, axis=1)
    dscore = jnp.concatenate(dscore, axis=1)
    out = jnp.dot(probs, v2, preferred_element_type=F32)
    dq = jnp.dot(dscore, k2, preferred_element_type=F32)
    dv = t_dot(probs, d)
    dk = t_dot(dscore, q)
    dv = jnp.where(first, dv[:128], dv[128:])
    dk = jnp.where(first, dk[:128], dk[128:])
    return out, dq, dk, dv


def core_kernel(recv, w, gain, perm, grads, mine, other, xown, xs, normed, norm_t, og_t, acc, proj, back):
    _, _, _, c, _, _ = place()
    for s in range(2):
        for gh in range(2):
            block = recv[s, 8 * gh : 8 * gh + 8].reshape(384, D)
            rows = jnp.dot(perm[...], block, preferred_element_type=F32).astype(BF)
            xs[:, :, s, 16 * gh : 16 * gh + 16, :] = rows.reshape(2, 12, 16, D)

    xown[...] = xs[:, :, c]

    def norm(u, _):
        values = xs[0, u].reshape(64, D).astype(F32)
        xhat, _ = standardize(values)
        normed[pl.ds(pl.multiple_of(u * 64, 64), 64), :] = (xhat * gain[...]).astype(BF)
        return 0

    lax.fori_loop(0, 12, norm, 0)

    for i in range(6):
        norm_t[:, 128 * i : 128 * i + 128] = normed[128 * i : 128 * i + 128, :].T
        og_t[:, 128 * i : 128 * i + 128] = xs[1, 2 * i : 2 * i + 2].reshape(128, D).T

    acc[...] = jnp.zeros_like(acc)
    lane = lax.broadcasted_iota(jnp.int32, (128, 128), 1)
    line = lax.broadcasted_iota(jnp.int32, (128, 128), 0)
    first = lane < 64
    allowed = (lane < 64) == (line < 64)

    def group(j, _):
        def project(i, _):
            rows = pl.ds(pl.multiple_of(i * 256, 256), 256)
            proj[rows, 0:384] = jnp.dot(normed[rows, :], w[j, :, 0:384], preferred_element_type=F32).astype(BF)
            cot = xs[1, pl.ds(i * 4, 4)].reshape(256, D)
            proj[rows, 384:512] = jnp.dot(cot, w[j, :, 384:512], preferred_element_type=F32).astype(BF)
            return 0

        lax.fori_loop(0, 3, project, 0)

        def pair(i, _):
            for e in range(2):
                rows = pl.ds(pl.multiple_of(i * 256 + e * 128, 128), 128)
                out, dq, dk, dv = attend(
                    proj[rows, 0:128], proj[rows, 128:256], proj[rows, 256:384], proj[rows, 384:512], allowed, first
                )
                back[rows, 0:128] = dq.astype(BF)
                back[rows, 128:256] = dk.astype(BF)
                back[rows, 256:384] = dv.astype(BF)
                back[rows, 384:512] = out.astype(BF)
            return 0

        lax.fori_loop(0, 3, pair, 0)

        def partial(i, _):
            rows = pl.ds(pl.multiple_of(i * 128, 128), 128)
            term = dot_t(back[rows, 0:384], w[j, :, 0:384])
            acc[pl.ds(i * 2, 2)] += term.astype(BF).astype(F32).reshape(2, 2, 32, D)
            return 0

        lax.fori_loop(0, 6, partial, 0)

        def weight(i, _):
            rows = pl.ds(pl.multiple_of(i * 256, 256), 256)
            grads[j, rows, 0:384] = jnp.dot(norm_t[rows, :], back[:, 0:384], preferred_element_type=F32).astype(BF)
            grads[j, rows, 384:512] = jnp.dot(og_t[rows, :], back[:, 384:512], preferred_element_type=F32).astype(BF)
            return 0

        lax.fori_loop(0, 4, weight, 0)
        return 0

    lax.fori_loop(0, 4, group, 0)
    mine[...] = acc[:, c]
    other[...] = acc[:, 1 - c].astype(BF)


def core(recv, w, gain, perm):
    vm = pl.BlockSpec(memory_space=pltpu.VMEM)
    return pl.pallas_call(
        core_kernel,
        out_shape=(
            jax.ShapeDtypeStruct((4, D, 512), BF),
            jax.ShapeDtypeStruct((12, 32, D), F32),
            jax.ShapeDtypeStruct((12, 32, D), BF),
            jax.ShapeDtypeStruct((2, 12, 32, D), BF),
        ),
        in_specs=[vm] * 4,
        out_specs=(vm,) * 4,
        scratch_shapes=[
            pltpu.VMEM((2, 12, 2, 32, D), BF),
            pltpu.VMEM((768, D), BF),
            pltpu.VMEM((D, 768), BF),
            pltpu.VMEM((D, 768), BF),
            pltpu.VMEM((12, 2, 32, D), F32),
            pltpu.VMEM((768, 512), BF),
            pltpu.VMEM((768, 512), BF),
        ],
        compiler_params=pltpu.CompilerParams(vmem_limit_bytes=52 * 2**20),
        name="core",
    )(recv, w, gain, perm)


def gather_kernel(
    mine, other, xown, gain, grads, repack, unpack, tgrad, wgrad,
    rsib, tg, gvec, gvecr, gcol, sbuf, rbuf, blk, gyr, ggr, gz, gzr, gxs, gxr,
    loc, bsend, brecv, vsend, vrecv, ysend, yrecv, gsend, grecv, asend, arecv,
    psend, precv, rsend, rrecv, zsend, zrecv, xsend, xrecv,
):
    f, m, g, c, z, x = place()
    zh, y = f // 8, (f // 2) % 4
    zi = zh * 2 + z
    sib = g * 2 + 1 - c
    pm = (1 - z) * 4 + x
    mr, ml = z * 4 + (x + 1) % 4, z * 4 + (x + 3) % 4
    xl, xr, xf = (x + 3) % 4, (x + 1) % 4, (x + 2) % 4
    barrier = pltpu.get_barrier_semaphore()

    def hello_frame(k, _):
        greet(barrier, ((g + k) % 16) * 2 + c, m)
        return 0

    def hello_column(k, _):
        dz = (zi + k // 2) % 8
        dc = (c + k) % 2
        greet(barrier, ((dz // 2) * 4 + y) * 2 + dc, (dz % 2) * 4 + x)
        return 0

    lax.fori_loop(1, 16, hello_frame, 0)
    lax.fori_loop(1, 16, hello_column, 0)
    for k in range(1, 4):
        greet(barrier, f, z * 4 + (x + k) % 4)
    pl.semaphore_wait(barrier, 33)

    to_sib = remote(other, rsib, bsend, brecv, sib, m)
    to_sib.start()

    def y_copy(k):
        yk = (y + k) % 4
        return remote(
            grads.at[:, :, yk], gyr.at[k], ysend.at[k], yrecv.at[k], (zh * 4 + yk) * 2 + c, m
        )

    for k in (1, 3, 2):
        y_copy(k).start()
    own_y = pltpu.make_async_copy(grads.at[:, :, y], gyr.at[0], loc.at[0])
    own_y.start()

    to_sib.wait_recv()

    def token(u, total):
        xhat, rstd = standardize(xown[0, u].astype(F32))
        dn = mine[u] + rsib[u].astype(F32)
        bp = dn * gain[...]
        inner = bp - jnp.mean(bp, axis=-1, keepdims=True) - xhat * jnp.mean(bp * xhat, axis=-1, keepdims=True)
        tg[u] = (xown[1, u].astype(F32) + rstd * inner).astype(BF)
        return total + jnp.sum((dn * xhat).reshape(4, 8, D), axis=0)

    total = lax.fori_loop(0, 12, token, jnp.zeros((8, D), F32))
    gvec[...] = jnp.broadcast_to(jnp.sum(total, axis=0, keepdims=True), (8, D))
    to_sib_gain = remote(gvec, gvecr, vsend, vrecv, sib, m)
    to_sib_gain.start()

    for gh in range(2):
        halves = [tg[:, 16 * gh : 16 * gh + 16, 512 * h : 512 * h + 512].reshape(192, 512) for h in range(2)]
        packed = jnp.dot(repack[...], jnp.concatenate(halves, axis=0), preferred_element_type=F32)
        sbuf[8 * gh : 8 * gh + 8] = packed.astype(BF).reshape(8, 48, 512)

    def a2a(k):
        return remote(sbuf.at[(g + k) % 16], rbuf.at[g], asend.at[k], arecv.at[k], ((g + k) % 16) * 2 + c, m)

    def send(k, _):
        a2a(k).start()
        return 0

    lax.fori_loop(1, 16, send, 0)
    keep = pltpu.make_async_copy(sbuf.at[g], rbuf.at[g], loc.at[1])
    keep.start()

    to_sib_gain.wait_recv()
    column = jnp.broadcast_to(gvec[0:1] + gvecr[0:1], (128, D)).T
    gcol[...] = column.astype(BF).reshape(4, 4, 2, 32, 128)

    def gain_copy(k):
        yk = (y + k) % 4
        return remote(gcol.at[:, yk], ggr.at[k], gsend.at[k], grecv.at[k], (zh * 4 + yk) * 2 + c, m)

    for k in range(1, 4):
        gain_copy(k).start()
    own_gain = pltpu.make_async_copy(gcol.at[:, y], ggr.at[0], loc.at[2])
    own_gain.start()

    keep.wait()

    def received(k, _):
        remote(sbuf.at[0], rbuf.at[(g + 16 - k) % 16], asend.at[k], arecv.at[k], f, m).wait_recv()
        return 0

    lax.fori_loop(1, 16, received, 0)
    for gh in range(2):
        rows = jnp.dot(unpack[...], rbuf[8 * gh : 8 * gh + 8].reshape(384, 512), preferred_element_type=F32)
        rows = rows.astype(BF).reshape(2, 12, 16, 512)
        for h in range(2):
            blk[:, 16 * gh : 16 * gh + 16, 512 * h : 512 * h + 512] = rows[h]

    def span(mm):
        return pl.ds(pl.multiple_of(mm * 32, 32), 32)

    six = (pl.ds(0, 6), pl.ds(6, 6))

    def part(mm, h):
        return tgrad.at[six[h], span(mm), :]

    def pair(h):
        return remote(blk.at[six[h]], part(m, h), psend.at[h], precv.at[h], f, pm)

    def ring(r, src, mm, h, i, to):
        return remote(src, part(mm, h), rsend.at[r, i], rrecv.at[r, i], f, to)

    pair(0).start()
    pair(1).start()
    ring(0, blk.at[six[0]], m, 0, 0, mr).start()
    ring(0, blk.at[six[1]], m, 1, 2, ml).start()
    ring(0, blk.at[six[1]], m, 1, 1, mr).start()
    ring(0, blk.at[six[0]], m, 0, 3, ml).start()
    own_out = pltpu.make_async_copy(blk, tgrad.at[:, span(m), :], loc.at[3])
    own_out.start()

    def pair_arrived(h):
        remote(blk.at[six[h]], part(pm, h), psend.at[h], precv.at[h], f, pm).wait_recv()

    pair_arrived(0)
    ring(1, part(pm, 0), pm, 0, 0, mr).start()
    ring(1, part(pm, 0), pm, 0, 3, ml).start()
    pair_arrived(1)
    ring(1, part(pm, 1), pm, 1, 2, ml).start()
    ring(1, part(pm, 1), pm, 1, 1, mr).start()

    def arrived(r, mm, h, i):
        ring(r, part(mm, h), mm, h, i, mr).wait_recv()

    def base(r):
        return (z if r == 0 else 1 - z) * 4

    def relay(r):
        arrived(r, base(r) + xl, 0, 0)
        ring(r, part(base(r) + xl, 0), base(r) + xl, 0, 4, mr).start()
        arrived(r, base(r) + xr, 1, 2)
        ring(r, part(base(r) + xr, 1), base(r) + xr, 1, 5, ml).start()

    relay(0)

    own_y.wait()
    own_gain.wait()
    for k in range(1, 4):
        remote(gyr.at[0], gyr.at[k], ysend.at[k], yrecv.at[k], f, m).wait_recv()
        remote(ggr.at[0], ggr.at[k], gsend.at[k], grecv.at[k], f, m).wait_recv()

    def sum_y(n, _):
        a, b = n // 2, n % 2
        for j in range(4):
            terms = [gyr[k, j, a, b].astype(F32) for k in range(4)]
            gz[a, b, :, 512 * j : 512 * j + 512] = ((terms[0] + terms[1]) + (terms[2] + terms[3])).astype(BF)
        terms = [ggr[k, a, b].astype(F32) for k in range(4)]
        gz[a, b, :, 2048:2176] = ((terms[0] + terms[1]) + (terms[2] + terms[3])).astype(BF)
        return 0

    lax.fori_loop(0, 8, sum_y, 0)

    def z_copy(n):
        return remote(
            gz.at[n // 2, n % 2], gzr.at[zi], zsend.at[n], zrecv.at[zi], ((n // 2) * 4 + y) * 2 + n % 2, c * 4 + x
        )

    def z_self(n):
        return jnp.logical_and(n == zh * 2 + c, c == z)

    def z_send(n, _):
        @pl.when(jnp.logical_not(z_self(n)))
        def _():
            z_copy(n).start()

        return 0

    lax.fori_loop(0, 8, z_send, 0)
    own_z = pltpu.make_async_copy(gz.at[zh, c], gzr.at[zi], loc.at[4])

    @pl.when(c == z)
    def _():
        own_z.start()

    relay(1)

    def z_wait(n, _):
        @pl.when(jnp.logical_not(jnp.logical_and(n == zi, c == z)))
        def _():
            remote(gz.at[0, 0], gzr.at[n], zsend.at[0], zrecv.at[n], f, m).wait_recv()

        return 0

    lax.fori_loop(0, 8, z_wait, 0)

    @pl.when(c == z)
    def _():
        own_z.wait()

    for j in range(5):
        cols = slice(512 * j, 512 * j + (512 if j < 4 else 128))
        terms = [gzr[k, :, cols].astype(F32) for k in range(8)]
        while len(terms) > 1:
            terms = [a + b for a, b in zip(terms[::2], terms[1::2])]
        if j < 4:
            gxs[j, :, 0:512] = terms[0].astype(BF)
        else:
            for i in range(4):
                gxs[i, :, 512:640] = terms[0].astype(BF)

    def x_copy(k):
        xk = (x + k) % 4
        return remote(gxs.at[xk], gxr.at[k], xsend.at[k], xrecv.at[k], f, z * 4 + xk)

    for k in range(1, 4):
        x_copy(k).start()
    for k in range(1, 4):
        remote(gxs.at[0], gxr.at[k], xsend.at[k], xrecv.at[k], f, m).wait_recv()
    wgrad[...] = (gxs[x].astype(F32) + gxr[1].astype(F32)) + (gxr[2].astype(F32) + gxr[3].astype(F32))

    for r in range(2):
        arrived(r, base(r) + xl, 1, 1)
        arrived(r, base(r) + xr, 0, 3)
        arrived(r, base(r) + xf, 0, 4)
        arrived(r, base(r) + xf, 1, 5)
        for i, (mm, h) in enumerate(((x, 0), (x, 1), (x, 1), (x, 0), (xl, 0), (xr, 1))):
            ring(r, part(base(r) + mm, h), base(r) + mm, h, i, mr).wait_send()
    pair(0).wait_send()
    pair(1).wait_send()
    own_out.wait()
    to_sib.wait_send()
    to_sib_gain.wait_send()

    def a2a_sent(k, _):
        a2a(k).wait_send()
        return 0

    lax.fori_loop(1, 16, a2a_sent, 0)
    for k in range(1, 4):
        y_copy(k).wait_send()
        gain_copy(k).wait_send()
        x_copy(k).wait_send()

    def z_sent(n, _):
        @pl.when(jnp.logical_not(z_self(n)))
        def _():
            z_copy(n).wait_send()

        return 0

    lax.fori_loop(0, 8, z_sent, 0)


def gather(mine, other, xown, gain, grads, repack, unpack):
    vm = pl.BlockSpec(memory_space=pltpu.VMEM)
    any_spec = pl.BlockSpec(memory_space=pl.ANY)
    dma = pltpu.SemaphoreType.DMA
    return pl.pallas_call(
        gather_kernel,
        out_shape=(jax.ShapeDtypeStruct((12, 256, D), BF), jax.ShapeDtypeStruct((32, 640), F32)),
        in_specs=[vm, any_spec, vm, vm, any_spec, vm, vm],
        out_specs=(any_spec, vm),
        scratch_shapes=[
            pltpu.VMEM((12, 32, D), BF),
            pltpu.VMEM((12, 32, D), BF),
            pltpu.VMEM((8, D), F32),
            pltpu.VMEM((8, D), F32),
            pltpu.VMEM((4, 4, 2, 32, 128), BF),
            pltpu.VMEM((16, 48, 512), BF),
            pltpu.VMEM((16, 48, 512), BF),
            pltpu.VMEM((12, 32, D), BF),
            pltpu.VMEM((4, 4, 4, 2, 32, 512), BF),
            pltpu.VMEM((4, 4, 2, 32, 128), BF),
            pltpu.VMEM((4, 2, 32, 2176), BF),
            pltpu.VMEM((8, 32, 2176), BF),
            pltpu.VMEM((4, 32, 640), BF),
            pltpu.VMEM((4, 32, 640), BF),
            dma((5,)),
            dma,
            dma,
            dma,
            dma,
            dma((4,)),
            dma((4,)),
            dma((4,)),
            dma((4,)),
            dma((16,)),
            dma((16,)),
            dma((2,)),
            dma((2,)),
            dma((2, 6)),
            dma((2, 6)),
            dma((8,)),
            dma((8,)),
            dma((4,)),
            dma((4,)),
        ],
        compiler_params=pltpu.CompilerParams(
            collective_id=1, has_side_effects=True, vmem_limit_bytes=48 * 2**20
        ),
        name="gather",
    )(mine, other, xown, gain, grads, repack, unpack)


def shards(tokens, output_gradient, gain, qkv_weight, out_weight):
    clips, frames, patches, width = tokens.shape
    tok = tokens.reshape(12, 256, D)
    og = output_gradient.reshape(12, 256, D)
    wc = jnp.concatenate([qkv_weight.reshape(D, 384), out_weight.T], axis=1)
    gain_row = gain.reshape(1, D)
    recv, w = scatter(tok, og, wc, jnp.asarray(PACK, BF))
    grads, mine, other, xown = core(recv, w, gain_row, jnp.asarray(GROUP, BF))
    tgrad, wgrad = gather(
        mine,
        other,
        xown,
        gain_row,
        grads.reshape(4, 4, 4, 2, 32, 512),
        jnp.asarray(REPACK, BF),
        jnp.asarray(UNPACK, BF),
    )
    return (
        tgrad.reshape(clips, frames, patches, width),
        wgrad[:, 0:384].reshape(32, 3, 128),
        wgrad[:, 384:512].T,
        wgrad[:, 512],
    )


def solution(mesh):
    in_specs = (
        P(None, "frame", None, None),
        P(None, "frame", None, None),
        P(),
        P(None, None, "mlp"),
        P("mlp", None),
    )
    out_specs = (
        P(None, "frame", None, None),
        P("frame", None, "mlp"),
        P("mlp", "frame"),
        P("frame"),
    )
    return jax.shard_map(shards, mesh=mesh, in_specs=in_specs, out_specs=out_specs, check_vma=False)
```

```python
import numpy as np

import jax
import jax.numpy as jnp
from jax import lax
from jax.experimental import pallas as pl
from jax.experimental.pallas import tpu as pltpu
from jax.sharding import PartitionSpec as P

MESH = pl.DeviceIdType.MESH
BF = jnp.bfloat16
F32 = jnp.float32
D = 1024
FACTOR = 64 ** (-0.5)
NEG = -1e30


def one_hot(shape, perm):
    index = np.arange(384).reshape(shape).transpose(perm).reshape(-1)
    return np.eye(384, dtype=np.float32)[index]


PACK = one_hot((2, 2, 6, 8, 2), (3, 0, 1, 4, 2))
GROUP = one_hot((8, 2, 2, 6, 2), (1, 2, 3, 0, 4))
REPACK = one_hot((4, 6, 8, 2), (2, 0, 1, 3))
UNPACK = one_hot((8, 4, 2, 6), (1, 3, 0, 2))


def remote(src, dst, send, recv, f, m):
    return pltpu.make_async_remote_copy(
        src_ref=src, dst_ref=dst, send_sem=send, recv_sem=recv, device_id=(f, m), device_id_type=MESH
    )


def greet(barrier, f, m):
    pl.semaphore_signal(barrier, inc=1, device_id=(f, m), device_id_type=MESH)


def standardize(values):
    centered = values - jnp.mean(values, axis=-1, keepdims=True)
    rstd = lax.rsqrt(jnp.mean(centered * centered, axis=-1, keepdims=True) + 1e-05)
    return centered * rstd, rstd


def dot_t(a, b):
    return lax.dot_general(a, b, (((1,), (1,)), ((), ())), preferred_element_type=F32)


def t_dot(a, b):
    return lax.dot_general(a, b, (((0,), (0,)), ((), ())), preferred_element_type=F32)


def attend(q, k, v, d, allowed, first):
    zero = jnp.zeros_like(k)
    k2 = jnp.concatenate([jnp.where(first, k, zero), jnp.where(first, zero, k)], axis=0)
    v2 = jnp.concatenate([jnp.where(first, v, zero), jnp.where(first, zero, v)], axis=0)
    scores = dot_t(q, k2) * FACTOR
    dprob = dot_t(d, v2)
    probs, dscore = [], []
    for h in range(2):
        s = jnp.where(allowed, scores[:, 128 * h : 128 * h + 128], NEG)
        e = jnp.exp(s - jnp.max(s, axis=-1, keepdims=True))
        p = e * (1.0 / jnp.sum(e, axis=-1, keepdims=True))
        dp = dprob[:, 128 * h : 128 * h + 128]
        delta = jnp.sum(p * dp, axis=-1, keepdims=True)
        probs.append(p.astype(BF))
        dscore.append((p * (dp - delta) * FACTOR).astype(BF))
    probs = jnp.concatenate(probs, axis=1)
    dscore = jnp.concatenate(dscore, axis=1)
    out = jnp.dot(probs, v2, preferred_element_type=F32)
    dq = jnp.dot(dscore, k2, preferred_element_type=F32)
    dv = t_dot(probs, d)
    dk = t_dot(dscore, q)
    dv = jnp.where(first, dv[:128], dv[128:])
    dk = jnp.where(first, dk[:128], dk[128:])
    return out, dq, dk, dv


def sublayer_kernel(
    tok, og, qkvw, outw, gain, pack_p, group_p, repack_p, unpack_p,
    tgrad, gq, go, gg,
    xin, sbuf, recv, wown, wout, wt, ow, xs, normed, norm_t, og_t, proj, back, ao, part, other, rsib,
    tg, gacc, gvec, gvecr, gcol, sret, rret, blk, grads, gf, gn, ggr, gz, gzr, gzg, gzgr, gxs, gxr, gxg, gxgr,
    loc, kloc, wloc, oloc, zloc, gloc,
    asend, arecv, fsend, frecv, ssend, srecv, wsend, wrecv, bsend, brecv, vsend, vrecv,
    csend, crecv, psend, precv, rsend, rrecv, y1send, y1recv, y2send, y2recv, gsend, grecv,
    zsend, zrecv, xsend, xrecv, hsend, hrecv,
):
    f, m = lax.axis_index("frame"), lax.axis_index("mlp")
    g, c, z, x = f // 2, f % 2, m // 4, m % 4
    zh, y = f // 8, (f // 2) % 4
    zi = zh * 2 + z
    sib = g * 2 + 1 - c
    mz = (1 - z) * 4 + x
    xl, xr, xf = (x + 3) % 4, (x + 1) % 4, (x + 2) % 4
    mr, ml = z * 4 + xr, z * 4 + xl
    yl, yr, yf = (y + 3) % 4, (y + 1) % 4, (y + 2) % 4
    fr, fl = (zh * 4 + yr) * 2 + c, (zh * 4 + yl) * 2 + c
    own = c == z
    rows32 = pl.ds(pl.multiple_of(m * 32, 32), 32)

    w_in = [pltpu.make_async_copy(qkvw.at[j], wown.at[:, pl.ds(128 * j, 128)], loc.at[4 + j]) for j in range(3)]
    w_in.append(pltpu.make_async_copy(outw, ow, loc.at[7]))
    for copy in w_in:
        copy.start()
    x_in = []
    for ch in range(2):
        for t, ref in enumerate((tok, og)):
            x_in.append(
                pltpu.make_async_copy(ref.at[pl.ds(6 * ch, 6), rows32, :], xin.at[ch, t], loc.at[2 * ch + t])
            )
            x_in[-1].start()

    barrier = pltpu.get_barrier_semaphore()

    def hello_frame(k, _):
        greet(barrier, ((g + k) % 16) * 2 + c, m)
        return 0

    def hello_column(k, _):
        dz = (zi + k // 2) % 8
        greet(barrier, ((dz // 2) * 4 + y) * 2 + (c + k) % 2, (dz % 2) * 4 + x)
        return 0

    lax.fori_loop(1, 16, hello_frame, 0)
    lax.fori_loop(1, 16, hello_column, 0)
    for k in range(1, 4):
        greet(barrier, f, z * 4 + (x + k) % 4)

    for copy in w_in:
        copy.wait()
    wown[:, 384:512] = ow[...].T
    pl.semaphore_wait(barrier, 33)

    half = (pl.ds(0, 512), pl.ds(512, 512))
    w_pairs = ((1, 0), (1, 1), (2, 1), (2, 0), (3, 0), (3, 1))

    def w_ring(src, slot, n, to):
        i, h = w_pairs[n]
        return remote(src, wout.at[slot, half[h]], wsend.at[n], wrecv.at[i, h], f, to)

    def w_spread(src, h):
        if h == 0:
            w_ring(src.at[half[0]], x, 0, mr).start()
            w_ring(src.at[half[0]], x, 3, ml).start()
        else:
            w_ring(src.at[half[1]], x, 2, ml).start()
            w_ring(src.at[half[1]], x, 1, mr).start()

    far = (zi + 7 + 2 * z) % 8
    near_id = (g * 2 + 1 - c, mz)
    far_id = (((far // 2) * 4 + y) * 2 + 1 - c, (far % 2) * 4 + x)

    def swap(h):
        return remote(
            wown.at[half[h]], wout.at[x, half[h]], ssend.at[h], srecv.at[h], *(near_id if h == 0 else far_id)
        )

    own_w = pltpu.make_async_copy(wown, wout.at[x], wloc)

    @pl.when(own)
    def _():
        w_spread(wown, 0)
        w_spread(wown, 1)
        own_w.start()

    @pl.when(jnp.logical_not(own))
    def _():
        swap(0).start()
        swap(1).start()

    def a2a(ch, k):
        to = (g + k) % 16
        return remote(sbuf.at[ch, to], recv.at[ch, c, g], asend.at[ch, k], arecv.at[ch, k], to * 2 + c, m)

    def forward(ch, k, src):
        slot = (g + 16 - k) % 16
        return remote(src, recv.at[ch, c, slot], fsend.at[ch, k], frecv.at[ch, k], sib, m)

    def keep(ch):
        return pltpu.make_async_copy(sbuf.at[ch, g], recv.at[ch, c, g], kloc.at[ch])

    for ch in range(2):
        x_in[2 * ch].wait()
        x_in[2 * ch + 1].wait()
        for gh in range(2):
            rows = slice(16 * gh, 16 * gh + 16)
            parts = [xin[ch, t, :, rows, 512 * h : 512 * h + 512].reshape(96, 512) for h in range(2) for t in range(2)]
            packed = jnp.dot(pack_p[...], jnp.concatenate(parts, axis=0), preferred_element_type=F32)
            sbuf[ch, 8 * gh : 8 * gh + 8] = packed.astype(BF).reshape(8, 48, 512)

        def send(k, _, ch=ch):
            a2a(ch, k).start()
            return 0

        lax.fori_loop(1, 16, send, 0)
        keep(ch).start()
        forward(ch, 0, sbuf.at[ch, g]).start()

    @pl.when(jnp.logical_not(own))
    def _():
        swap(0).wait_recv()
        w_spread(wout.at[x], 0)
        swap(1).wait_recv()
        w_spread(wout.at[x], 1)

    def w_arrived(n):
        i, h = w_pairs[n]
        slot = (x, xl, xr, xf)[i]
        remote(wown.at[half[h]], wout.at[slot, half[h]], wsend.at[n], wrecv.at[i, h], f, mr).wait_recv()

    def relay_tokens(ch):
        def relay(k, _):
            slot = (g + 16 - k) % 16
            remote(sbuf.at[ch, 0], recv.at[ch, c, slot], asend.at[ch, k], arecv.at[ch, k], f, m).wait_recv()
            forward(ch, k, recv.at[ch, c, slot]).start()
            return 0

        lax.fori_loop(1, 16, relay, 0)

    def tokens_arrived(ch):
        keep(ch).wait()

        def wait(k, _):
            slot = (g + 16 - k) % 16
            remote(sbuf.at[ch, 0], recv.at[ch, 1 - c, slot], fsend.at[ch, k], frecv.at[ch, k], f, m).wait_recv()
            return 0

        lax.fori_loop(0, 16, wait, 0)

    relay_tokens(0)
    w_arrived(0)
    w_ring(wout.at[xl, half[0]], xl, 4, mr).start()
    w_arrived(2)
    w_ring(wout.at[xr, half[1]], xr, 5, ml).start()

    lane = lax.broadcasted_iota(jnp.int32, (128, 128), 1)
    line = lax.broadcasted_iota(jnp.int32, (128, 128), 0)
    first = lane < 64
    allowed = (lane < 64) == (line < 64)

    def shard_of(i):
        return (x + (i % 2) * 3 + (i // 2) * (1 + (i % 2) * 2)) % 4

    def prepare(ch):
        for s in range(2):
            for gh in range(2):
                block = recv[ch, s, 8 * gh : 8 * gh + 8].reshape(384, 512)
                rows = jnp.dot(group_p[...], block, preferred_element_type=F32).astype(BF).reshape(2, 2, 6, 16, 512)
                for h in range(2):
                    xs[ch, :, :, s, 16 * gh : 16 * gh + 16, 512 * h : 512 * h + 512] = rows[h]

        def norm(u, _):
            xhat, _ = standardize(xs[ch, 0, u].reshape(64, D).astype(F32))
            normed[pl.ds(pl.multiple_of(ch * 384 + u * 64, 64), 64), :] = (xhat * gain[...]).astype(BF)
            return 0

        lax.fori_loop(0, 6, norm, 0)
        for i in range(3):
            at = 384 * ch + 128 * i
            norm_t[:, at : at + 128] = normed[at : at + 128, :].T
            og_t[:, at : at + 128] = xs[ch, 1, 2 * i : 2 * i + 2].reshape(128, D).T

    def heads(ch, i):
        j = shard_of(i)
        at = 384 * ch
        if ch == 0:
            wt[i] = wout[j, :, 0:384].T
        proj[:, 0:384] = jnp.dot(normed[at : at + 384, :], wout[j, :, 0:384], preferred_element_type=F32).astype(BF)
        proj[:, 384:512] = jnp.dot(
            xs[ch, 1].reshape(384, D), wout[j, :, 384:512], preferred_element_type=F32
        ).astype(BF)
        for n in range(3):
            rows = slice(128 * n, 128 * n + 128)
            out, dq, dk, dv = attend(
                proj[rows, 0:128], proj[rows, 128:256], proj[rows, 256:384], proj[rows, 384:512], allowed, first
            )
            rows = slice(at + 128 * n, at + 128 * n + 128)
            back[i, rows, 0:128] = dq.astype(BF)
            back[i, rows, 128:256] = dk.astype(BF)
            back[i, rows, 256:384] = dv.astype(BF)
            ao[i, rows, :] = out.astype(BF)

    def to_sibling(ch):
        return remote(other.at[ch], rsib.at[ch], bsend.at[ch], brecv.at[ch], sib, m)

    def partial(ch):
        for n in range(3):
            rows = slice(384 * ch + 128 * n, 384 * ch + 128 * n + 128)
            term = jnp.dot(back[0, rows, :], wt[0], preferred_element_type=F32)
            for i in range(1, 4):
                term += jnp.dot(back[i, rows, :], wt[i], preferred_element_type=F32)
            part[2 * n : 2 * n + 2] = term.reshape(2, 2, 32, D)
        other[ch] = part[:, 1 - c].astype(BF)
        to_sibling(ch).start()

    def back_to(ch, k):
        to = (g + k) % 16
        return remote(sret.at[ch, to], rret.at[ch, g], csend.at[ch, k], crecv.at[ch, k], to * 2 + c, m)

    def keep_back(ch):
        return pltpu.make_async_copy(sret.at[ch, g], rret.at[ch, g], kloc.at[2 + ch])

    def token_gradient(ch):
        to_sibling(ch).wait_recv()

        def token(u, total):
            xhat, rstd = standardize(xs[ch, 0, u, c].astype(F32))
            dn = part[u, c] + rsib[ch, u].astype(F32)
            bp = dn * gain[...]
            inner = bp - jnp.mean(bp, axis=-1, keepdims=True) - xhat * jnp.mean(bp * xhat, axis=-1, keepdims=True)
            tg[u] = (xs[ch, 1, u, c].astype(F32) + rstd * inner).astype(BF)
            return total + jnp.sum((dn * xhat).reshape(4, 8, D), axis=0)

        total = lax.fori_loop(0, 6, token, jnp.zeros((8, D), F32))
        if ch == 0:
            gacc[...] = total
        else:
            gacc[...] += total
        for gh in range(2):
            rows = slice(16 * gh, 16 * gh + 16)
            parts = [tg[:, rows, 256 * h : 256 * h + 256].reshape(96, 256) for h in range(4)]
            packed = jnp.dot(repack_p[...], jnp.concatenate(parts, axis=0), preferred_element_type=F32)
            sret[ch, 8 * gh : 8 * gh + 8] = packed.astype(BF).reshape(8, 48, 256)

        def send(k, _):
            back_to(ch, k).start()
            return 0

        lax.fori_loop(1, 16, send, 0)
        keep_back(ch).start()

    def span(mm):
        return pl.ds(pl.multiple_of(mm * 32, 32), 32)

    def piece(ch, h, mm):
        return tgrad.at[pl.ds(6 * ch + 3 * h, 3), span(mm), :]

    def pair(ch, h):
        return remote(
            blk.at[ch, pl.ds(3 * h, 3)], piece(ch, h, m), psend.at[ch, h], precv.at[ch, h], f, mz
        )

    def ring(ch, r, src, mm, h, n, to):
        return remote(src, piece(ch, h, mm), rsend.at[ch, r, n], rrecv.at[ch, r, n], f, to)

    def own_out(ch):
        return pltpu.make_async_copy(blk.at[ch], tgrad.at[pl.ds(6 * ch, 6), span(m), :], oloc.at[ch])

    def gather_own(ch):
        keep_back(ch).wait()

        def received(k, _):
            slot = (g + 16 - k) % 16
            remote(sret.at[ch, 0], rret.at[ch, slot], csend.at[ch, k], crecv.at[ch, k], f, m).wait_recv()
            return 0

        lax.fori_loop(1, 16, received, 0)
        for gh in range(2):
            block = rret[ch, 8 * gh : 8 * gh + 8].reshape(384, 256)
            rows = jnp.dot(unpack_p[...], block, preferred_element_type=F32).astype(BF).reshape(4, 6, 16, 256)
            for h in range(4):
                blk[ch, :, 16 * gh : 16 * gh + 16, 256 * h : 256 * h + 256] = rows[h]
        pair(ch, 0).start()
        pair(ch, 1).start()
        mine = [blk.at[ch, pl.ds(3 * h, 3)] for h in range(2)]
        ring(ch, 0, mine[0], m, 0, 0, mr).start()
        ring(ch, 0, mine[1], m, 1, 2, ml).start()
        ring(ch, 0, mine[1], m, 1, 1, mr).start()
        ring(ch, 0, mine[0], m, 0, 3, ml).start()
        own_out(ch).start()

    def gather_pair(ch):
        def arrived(h):
            remote(
                blk.at[ch, pl.ds(3 * h, 3)], piece(ch, h, mz), psend.at[ch, h], precv.at[ch, h], f, mz
            ).wait_recv()

        arrived(0)
        ring(ch, 1, piece(ch, 0, mz), mz, 0, 0, mr).start()
        ring(ch, 1, piece(ch, 0, mz), mz, 0, 3, ml).start()
        arrived(1)
        ring(ch, 1, piece(ch, 1, mz), mz, 1, 2, ml).start()
        ring(ch, 1, piece(ch, 1, mz), mz, 1, 1, mr).start()

    def base(r):
        return (z if r == 0 else 1 - z) * 4

    def arrived(ch, r, mm, h, n):
        ring(ch, r, piece(ch, h, base(r) + mm), base(r) + mm, h, n, mr).wait_recv()

    def gather_relay(ch, r):
        arrived(ch, r, xl, 0, 0)
        ring(ch, r, piece(ch, 0, base(r) + xl), base(r) + xl, 0, 4, mr).start()
        arrived(ch, r, xr, 1, 2)
        ring(ch, r, piece(ch, 1, base(r) + xr), base(r) + xr, 1, 5, ml).start()

    def weights(i):
        j = shard_of(i)

        def block(a, _):
            rows = pl.ds(pl.multiple_of(a * 256, 256), 256)
            left = jnp.dot(norm_t[rows, :], back[i], preferred_element_type=F32).astype(BF)
            grads[j, a, :, :, :, 0:384] = left.reshape(4, 2, 32, 384)
            left = jnp.dot(og_t[rows, :], ao[i], preferred_element_type=F32).astype(BF)
            grads[j, a, :, :, :, 384:512] = left.reshape(4, 2, 32, 128)
            return 0

        lax.fori_loop(0, 4, block, 0)
        y_far(i, 0).start()
        y_far(i, 1).start()

    def y_far(i, h):
        src = grads.at[shard_of(i), pl.ds(2 * h, 2), yf]
        return remote(src, gf.at[i, h], y1send.at[i, h], y1recv.at[i, h], fr if h == 0 else fl, m)

    def y_near(i, h):
        src = grads.at[shard_of(i), :, yr if h == 0 else yl]
        return remote(src, gn.at[i, h], y2send.at[i, h], y2recv.at[i, h], fr if h == 0 else fl, m)

    def y_step(i, _):
        j = shard_of(i)
        for h in range(2):
            y_far(i, h).wait_recv()
            to = yr if h == 0 else yl
            for a in range(2):
                total = grads[j, 2 * h + a, to].astype(F32) + gf[i, h, a].astype(F32)
                grads[j, 2 * h + a, to] = total.astype(BF)
            y_near(i, h).start()
        return 0

    def z_copy(i, n):
        to = ((n // 2) * 4 + y) * 2 + n % 2
        return remote(gz.at[i, n], gzr.at[i, zi], zsend.at[i, n], zrecv.at[i, zi], to, c * 4 + x)

    def zg_copy(n):
        to = ((n // 2) * 4 + y) * 2 + n % 2
        return remote(gzg.at[n], gzgr.at[zi], zsend.at[4, n], zrecv.at[4, zi], to, c * 4 + x)

    def z_self(n):
        return jnp.logical_and(n == zh * 2 + c, own)

    def own_z(i):
        return pltpu.make_async_copy(gz.at[i, zh * 2 + c], gzr.at[i, zi], zloc.at[i])

    def own_zg():
        return pltpu.make_async_copy(gzg.at[zh * 2 + c], gzgr.at[zi], zloc.at[4])

    def z_step(i, _):
        j = shard_of(i)
        for h in range(2):
            y_near(i, h).wait_recv()
        for a in range(4):
            total = grads[j, a, y].astype(F32) + (gn[i, 0, a].astype(F32) + gn[i, 1, a].astype(F32))
            gz[i, 2 * a : 2 * a + 2] = total.astype(BF)

        def z_send(n, _):
            @pl.when(jnp.logical_not(z_self(n)))
            def _():
                z_copy(i, n).start()

            return 0

        lax.fori_loop(0, 8, z_send, 0)

        @pl.when(own)
        def _():
            own_z(i).start()

        return 0

    def z_wait(i, src, dst):
        def wait(n, _):
            @pl.when(jnp.logical_not(jnp.logical_and(n == zi, own)))
            def _():
                remote(src, dst(n), zsend.at[i, 0], zrecv.at[i, n], f, m).wait_recv()

            return 0

        lax.fori_loop(0, 8, wait, 0)

    def sum8(terms):
        while len(terms) > 1:
            terms = [a + b for a, b in zip(terms[::2], terms[1::2])]
        return terms[0]

    def x_copy(i):
        return remote(gxs.at[i], gxr.at[i], xsend.at[i], xrecv.at[i], f, z * 4 + shard_of(i))

    def x_step(i, _):
        z_wait(i, gz.at[0, 0], lambda n: gzr.at[i, n])

        @pl.when(own)
        def _():
            own_z(i).wait()

        gxs[i] = sum8([gzr[i, k].astype(F32) for k in range(8)]).astype(BF)

        @pl.when(i > 0)
        def _():
            x_copy(i).start()

        return 0

    def gain_y(k):
        yk = (y + k) % 4
        return remote(gcol.at[:, yk], ggr.at[k], gsend.at[k], grecv.at[k], (zh * 4 + yk) * 2 + c, m)

    own_gain = pltpu.make_async_copy(gcol.at[:, y], ggr.at[0], gloc)

    def gain_x(k):
        return remote(gxg, gxgr.at[k], hsend.at[k], hrecv.at[k], f, z * 4 + (x + k) % 4)

    to_sib_gain = remote(gvec, gvecr, vsend, vrecv, sib, m)

    tokens_arrived(0)
    prepare(0)

    @pl.when(own)
    def _():
        own_w.wait()

    def first_heads(i, _):
        @pl.when(i > 0)
        def _():
            slot = shard_of(i)

            @pl.when(i != 2)
            def _():
                for h in range(2):
                    @pl.when(jnp.logical_or(h == 1, i == 3))
                    def _():
                        remote(wown.at[half[h]], wout.at[slot, half[h]], wsend.at[0], wrecv.at[i, h], f, mr).wait_recv()

            @pl.when(i == 2)
            def _():
                remote(wown.at[half[0]], wout.at[slot, half[0]], wsend.at[0], wrecv.at[i, 0], f, mr).wait_recv()

        heads(0, i)
        return 0

    lax.fori_loop(0, 4, first_heads, 0)
    partial(0)
    relay_tokens(1)
    token_gradient(0)

    tokens_arrived(1)
    prepare(1)

    def second_heads(i, _):
        @pl.when(i == 2)
        def _():
            gather_own(0)

        heads(1, i)
        return 0

    lax.fori_loop(0, 4, second_heads, 0)
    partial(1)
    gather_pair(0)
    token_gradient(1)
    gvec[...] = jnp.broadcast_to(jnp.sum(gacc[...], axis=0, keepdims=True), (8, D))
    to_sib_gain.start()
    gather_relay(0, 0)

    def all_weights(i, _):
        weights(i)

        @pl.when(i == 2)
        def _():
            gather_relay(0, 1)

        return 0

    lax.fori_loop(0, 4, all_weights, 0)
    gather_own(1)
    to_sib_gain.wait_recv()
    gcol[...] = jnp.broadcast_to(gvec[0:1] + gvecr[0:1], (128, D)).T.astype(BF).reshape(4, 4, 2, 32, 128)
    for k in range(1, 4):
        gain_y(k).start()
    own_gain.start()
    lax.fori_loop(0, 4, y_step, 0)
    gather_pair(1)
    lax.fori_loop(0, 4, z_step, 0)
    gather_relay(1, 0)

    own_gain.wait()
    for k in range(1, 4):
        remote(ggr.at[0], ggr.at[k], gsend.at[k], grecv.at[k], f, m).wait_recv()
    total = sum8([ggr[k].astype(F32) for k in range(4)])
    gzg[...] = total.astype(BF).reshape(8, 32, 128)

    def zg_send(n, _):
        @pl.when(jnp.logical_not(z_self(n)))
        def _():
            zg_copy(n).start()

        return 0

    lax.fori_loop(0, 8, zg_send, 0)

    @pl.when(own)
    def _():
        own_zg().start()

    lax.fori_loop(0, 4, x_step, 0)
    z_wait(4, gzg.at[0], lambda n: gzgr.at[n])

    @pl.when(own)
    def _():
        own_zg().wait()

    gxg[...] = sum8([gzgr[k].astype(F32) for k in range(8)]).astype(BF)
    for k in range(1, 4):
        gain_x(k).start()
    gather_relay(1, 1)

    for i in range(1, 4):
        x_copy(i).wait_recv()
    total = sum8([gxs[0].astype(F32)] + [gxr[i].astype(F32) for i in range(1, 4)])
    for j in range(3):
        gq[j] = total[:, 128 * j : 128 * j + 128]
    go[...] = total[:, 384:512]
    for k in range(1, 4):
        gain_x(k).wait_recv()
    total = sum8([gxg[...].astype(F32)] + [gxgr[k].astype(F32) for k in range(1, 4)])
    gg[...] = jnp.broadcast_to(total[0:32, 0:1], (32, 128))

    for ch in range(2):
        for r in range(2):
            arrived(ch, r, xl, 1, 1)
            arrived(ch, r, xr, 0, 3)
            arrived(ch, r, xf, 0, 4)
            arrived(ch, r, xf, 1, 5)
            for n, (mm, h) in enumerate(((x, 0), (x, 1), (x, 1), (x, 0), (xl, 0), (xr, 1))):
                ring(ch, r, piece(ch, h, base(r) + mm), base(r) + mm, h, n, mr).wait_send()
        pair(ch, 0).wait_send()
        pair(ch, 1).wait_send()
        own_out(ch).wait()
        to_sibling(ch).wait_send()

        def sent(k, _, ch=ch):
            a2a(ch, k).wait_send()
            back_to(ch, k).wait_send()
            forward(ch, k, recv.at[ch, c, (g + 16 - k) % 16]).wait_send()
            return 0

        lax.fori_loop(1, 16, sent, 0)
        forward(ch, 0, sbuf.at[ch, g]).wait_send()
    to_sib_gain.wait_send()
    for n in range(6):
        i, h = w_pairs[n]
        w_ring(wown.at[half[h]], x, n, mr).wait_send()

    @pl.when(jnp.logical_not(own))
    def _():
        swap(0).wait_send()
        swap(1).wait_send()

    for k in range(1, 4):
        gain_y(k).wait_send()
        gain_x(k).wait_send()
        x_copy(k).wait_send()

    def y_sent(i, _):
        for h in range(2):
            y_far(i, h).wait_send()
            y_near(i, h).wait_send()
        return 0

    lax.fori_loop(0, 4, y_sent, 0)

    def z_sent(n, _):
        @pl.when(jnp.logical_not(z_self(n)))
        def _():
            for i in range(4):
                z_copy(i, n).wait_send()
            zg_copy(n).wait_send()

        return 0

    lax.fori_loop(0, 8, z_sent, 0)


def sublayer(tok, og, qkvw, outw, gain):
    vm = pl.BlockSpec(memory_space=pltpu.VMEM)
    hbm = pl.BlockSpec(memory_space=pltpu.HBM)
    dma = pltpu.SemaphoreType.DMA
    perms = [jnp.asarray(p, BF) for p in (PACK, GROUP, REPACK, UNPACK)]
    bf = lambda *shape: pltpu.VMEM(shape, BF)
    return pl.pallas_call(
        sublayer_kernel,
        out_shape=(
            jax.ShapeDtypeStruct((12, 256, D), BF),
            jax.ShapeDtypeStruct((3, 32, 128), F32),
            jax.ShapeDtypeStruct((32, 128), F32),
            jax.ShapeDtypeStruct((32, 128), F32),
        ),
        in_specs=[hbm] * 4 + [vm] * 5,
        out_specs=(hbm, vm, vm, vm),
        scratch_shapes=[
            bf(2, 2, 6, 32, D),
            bf(2, 16, 48, 512),
            bf(2, 2, 16, 48, 512),
            bf(D, 512),
            bf(4, D, 512),
            bf(4, 384, D),
            bf(128, D),
            bf(2, 2, 6, 2, 32, D),
            bf(768, D),
            bf(D, 768),
            bf(D, 768),
            bf(384, 512),
            bf(4, 768, 384),
            bf(4, 768, 128),
            pltpu.VMEM((6, 2, 32, D), F32),
            bf(2, 6, 32, D),
            bf(2, 6, 32, D),
            bf(6, 32, D),
            pltpu.VMEM((8, D), F32),
            pltpu.VMEM((8, D), F32),
            pltpu.VMEM((8, D), F32),
            bf(4, 4, 2, 32, 128),
            bf(2, 16, 48, 256),
            bf(2, 16, 48, 256),
            bf(2, 6, 32, D),
            bf(4, 4, 4, 2, 32, 512),
            bf(4, 2, 2, 2, 32, 512),
            bf(4, 2, 4, 2, 32, 512),
            bf(4, 4, 2, 32, 128),
            bf(4, 8, 32, 512),
            bf(4, 8, 32, 512),
            bf(8, 32, 128),
            bf(8, 32, 128),
            bf(4, 32, 512),
            bf(4, 32, 512),
            bf(32, 128),
            bf(4, 32, 128),
            dma((8,)),
            dma((4,)),
            dma,
            dma((2,)),
            dma((5,)),
            dma,
            dma((2, 16)),
            dma((2, 16)),
            dma((2, 16)),
            dma((2, 16)),
            dma((2,)),
            dma((2,)),
            dma((6,)),
            dma((4, 2)),
            dma((2,)),
            dma((2,)),
            dma,
            dma,
            dma((2, 16)),
            dma((2, 16)),
            dma((2, 2)),
            dma((2, 2)),
            dma((2, 2, 6)),
            dma((2, 2, 6)),
            dma((4, 2)),
            dma((4, 2)),
            dma((4, 2)),
            dma((4, 2)),
            dma((4,)),
            dma((4,)),
            dma((5, 8)),
            dma((5, 8)),
            dma((4,)),
            dma((4,)),
            dma((4,)),
            dma((4,)),
        ],
        compiler_params=pltpu.CompilerParams(
            collective_id=0, has_side_effects=True, vmem_limit_bytes=57 * 2**20
        ),
        name="sublayer",
    )(tok, og, qkvw, outw, gain, *perms)


def shards(tokens, output_gradient, gain, qkv_weight, out_weight):
    clips, frames, patches, width = tokens.shape
    tgrad, gq, go, gg = sublayer(
        tokens.reshape(12, 256, D),
        output_gradient.reshape(12, 256, D),
        jnp.transpose(qkv_weight, (1, 0, 2)),
        out_weight,
        gain.reshape(1, D),
    )
    return (
        tgrad.reshape(clips, frames, patches, width),
        jnp.transpose(gq, (1, 0, 2)),
        go.T,
        gg[:, 0],
    )


def solution(mesh):
    in_specs = (
        P(None, "frame", None, None),
        P(None, "frame", None, None),
        P(),
        P(None, None, "mlp"),
        P("mlp", None),
    )
    out_specs = (
        P(None, "frame", None, None),
        P("frame", None, "mlp"),
        P("mlp", "frame"),
        P("frame"),
    )
    return jax.shard_map(shards, mesh=mesh, in_specs=in_specs, out_specs=out_specs, check_vma=False)
```

```python
import numpy as np

import jax
import jax.numpy as jnp
from jax import lax
from jax.experimental import pallas as pl
from jax.experimental.pallas import tpu as pltpu
from jax.sharding import PartitionSpec as P

MESH = pl.DeviceIdType.MESH
BF = jnp.bfloat16
F32 = jnp.float32
D = 1024
FACTOR = 64 ** (-0.5)
NEG = -1e30


def one_hot(shape, perm):
    index = np.arange(384).reshape(shape).transpose(perm).reshape(-1)
    return np.eye(384, dtype=np.float32)[index]


PACK = one_hot((2, 2, 6, 8, 2), (3, 0, 1, 4, 2))
GROUP = one_hot((8, 2, 2, 6, 2), (1, 2, 3, 0, 4))
REPACK = one_hot((4, 6, 8, 2), (2, 0, 1, 3))
UNPACK = one_hot((8, 4, 2, 6), (1, 3, 0, 2))


def remote(src, dst, send, recv, f, m):
    return pltpu.make_async_remote_copy(
        src_ref=src, dst_ref=dst, send_sem=send, recv_sem=recv, device_id=(f, m), device_id_type=MESH
    )


def greet(barrier, f, m):
    pl.semaphore_signal(barrier, inc=1, device_id=(f, m), device_id_type=MESH)


def standardize(values):
    centered = values - jnp.mean(values, axis=-1, keepdims=True)
    rstd = lax.rsqrt(jnp.mean(centered * centered, axis=-1, keepdims=True) + 1e-05)
    return centered * rstd, rstd


def dot_t(a, b):
    return lax.dot_general(a, b, (((1,), (1,)), ((), ())), preferred_element_type=F32)


def t_dot(a, b):
    return lax.dot_general(a, b, (((0,), (0,)), ((), ())), preferred_element_type=F32)


def attend(q, k, v, d, allowed, first):
    zero = jnp.zeros_like(k)
    k2 = jnp.concatenate([jnp.where(first, k, zero), jnp.where(first, zero, k)], axis=0)
    v2 = jnp.concatenate([jnp.where(first, v, zero), jnp.where(first, zero, v)], axis=0)
    scores = dot_t(q, k2) * FACTOR
    dprob = dot_t(d, v2)
    probs, dscore = [], []
    for h in range(2):
        s = jnp.where(allowed, scores[:, 128 * h : 128 * h + 128], NEG)
        e = jnp.exp(s - jnp.max(s, axis=-1, keepdims=True))
        p = e * (1.0 / jnp.sum(e, axis=-1, keepdims=True))
        dp = dprob[:, 128 * h : 128 * h + 128]
        delta = jnp.sum(p * dp, axis=-1, keepdims=True)
        probs.append(p.astype(BF))
        dscore.append((p * (dp - delta) * FACTOR).astype(BF))
    probs = jnp.concatenate(probs, axis=1)
    dscore = jnp.concatenate(dscore, axis=1)
    out = jnp.dot(probs, v2, preferred_element_type=F32)
    dq = jnp.dot(dscore, k2, preferred_element_type=F32)
    dv = t_dot(probs, d)
    dk = t_dot(dscore, q)
    dv = jnp.where(first, dv[:128], dv[128:])
    dk = jnp.where(first, dk[:128], dk[128:])
    return out, dq, dk, dv


def sublayer_kernel(
    tok, og, qkvw, outw, gain, pack_p, group_p, repack_p, unpack_p,
    tgrad, gq, go, gg,
    xin, sbuf, recv, wown, wout, wt, ow, xs, normed, norm_t, og_t, proj, back, ao, part, other, rsib,
    tg, gacc, gvec, gvecr, gcol, sret, rret, blk, grads, gf, gn, ggr, gz, gzr, gzg, gzgr, gxs, gxr, gxg, gxgr,
    loc, kloc, wloc, oloc, zloc, gloc,
    asend, arecv, fsend, frecv, ssend, srecv, wsend, wrecv, bsend, brecv, vsend, vrecv,
    csend, crecv, psend, precv, rsend, rrecv, y1send, y1recv, y2send, y2recv, gsend, grecv,
    zsend, zrecv, xsend, xrecv, hsend, hrecv,
):
    f, m = lax.axis_index("frame"), lax.axis_index("mlp")
    g, c, z, x = f // 2, f % 2, m // 4, m % 4
    zh, y = f // 8, (f // 2) % 4
    zi = zh * 2 + z
    sib = g * 2 + 1 - c
    mz = (1 - z) * 4 + x
    xl, xr, xf = (x + 3) % 4, (x + 1) % 4, (x + 2) % 4
    mr, ml = z * 4 + xr, z * 4 + xl
    yl, yr, yf = (y + 3) % 4, (y + 1) % 4, (y + 2) % 4
    fr, fl = (zh * 4 + yr) * 2 + c, (zh * 4 + yl) * 2 + c
    own = c == z
    start = (zi + 5 + 3 * z) % 8
    me = (3 - 3 * z) * 4 + y

    def window(lo, h):
        return (zh + 3 - 2 * lo + h) % 4

    def owner(slot):
        to = (start + slot // 4) % 8
        return ((to // 2) * 4 + slot % 4) * 2 + c, (to % 2) * 4 + x

    def source(n):
        there = n // 4
        d = (there + 4 - zh) % 4
        lo = (d % 2) * (d // 2) + (1 - d % 2) * ((d // 2) * (1 - z) + (1 - d // 2) * z)
        place = (zi + 16 - (there * 2 + lo + 5 + 3 * lo)) % 8
        return n * 2 + c, lo * 4 + x, place * 4 + y

    w_in = [pltpu.make_async_copy(qkvw.at[j], wown.at[:, pl.ds(128 * j, 128)], loc.at[j]) for j in range(3)]
    w_in.append(pltpu.make_async_copy(outw, ow, loc.at[3]))
    for copy in w_in:
        copy.start()
    x_in = []
    for ch in range(2):
        for t, ref in enumerate((tok, og)):
            for h in range(2):
                rows = pl.ds(pl.multiple_of(x * 64 + window(z, h) * 16, 16), 16)
                x_in.append(
                    pltpu.make_async_copy(
                        ref.at[pl.ds(6 * ch, 6), rows, :],
                        xin.at[ch, t, :, pl.ds(16 * h, 16), :],
                        loc.at[4 + 4 * ch + 2 * t + h],
                    )
                )
                x_in[-1].start()

    barrier = pltpu.get_barrier_semaphore()

    def hello_plane(k, _):
        n = (zi * 4 + y + k) % 32
        greet(barrier, ((n // 8) * 4 + n % 4) * 2 + c, ((n // 4) % 2) * 4 + x)
        return 0

    def hello_other(k, _):
        greet(barrier, ((k // 2) * 4 + y) * 2 + 1 - c, (k % 2) * 4 + x)
        return 0

    lax.fori_loop(1, 32, hello_plane, 0)
    lax.fori_loop(0, 8, hello_other, 0)
    for k in range(1, 4):
        greet(barrier, f, z * 4 + (x + k) % 4)

    for copy in w_in:
        copy.wait()
    wown[:, 384:512] = ow[...].T
    pl.semaphore_wait(barrier, 42)

    half = (pl.ds(0, 512), pl.ds(512, 512))
    w_pairs = ((1, 0), (1, 1), (2, 1), (2, 0), (3, 0), (3, 1))

    def w_ring(src, slot, n, to):
        i, h = w_pairs[n]
        return remote(src, wout.at[slot, half[h]], wsend.at[n], wrecv.at[i, h], f, to)

    def w_spread(src, h):
        if h == 0:
            w_ring(src.at[half[0]], x, 0, mr).start()
            w_ring(src.at[half[0]], x, 3, ml).start()
        else:
            w_ring(src.at[half[1]], x, 2, ml).start()
            w_ring(src.at[half[1]], x, 1, mr).start()

    far = (zi + 7 + 2 * z) % 8
    near_id = (g * 2 + 1 - c, mz)
    far_id = (((far // 2) * 4 + y) * 2 + 1 - c, (far % 2) * 4 + x)

    def swap(h):
        return remote(
            wown.at[half[h]], wout.at[x, half[h]], ssend.at[h], srecv.at[h], *(near_id if h == 0 else far_id)
        )

    own_w = pltpu.make_async_copy(wown, wout.at[x], wloc)

    @pl.when(own)
    def _():
        w_spread(wown, 0)
        w_spread(wown, 1)
        own_w.start()

    @pl.when(jnp.logical_not(own))
    def _():
        swap(0).start()
        swap(1).start()

    def a2a(ch, k):
        slot = (me + k) % 16
        return remote(sbuf.at[ch, slot], recv.at[ch, c, g], asend.at[ch, k], arecv.at[ch, g], *owner(slot))

    def forward(ch, k, src):
        slot = (g + 16 - k) % 16
        return remote(src, recv.at[ch, c, slot], fsend.at[ch, k], frecv.at[ch, k], sib, m)

    def keep(ch):
        return pltpu.make_async_copy(sbuf.at[ch, me], recv.at[ch, c, g], kloc.at[ch])

    for ch in range(2):
        for copy in x_in[4 * ch : 4 * ch + 4]:
            copy.wait()
        for gh in range(2):
            rows = slice(16 * gh, 16 * gh + 16)
            parts = [xin[ch, t, :, rows, 512 * h : 512 * h + 512].reshape(96, 512) for h in range(2) for t in range(2)]
            packed = jnp.dot(pack_p[...], jnp.concatenate(parts, axis=0), preferred_element_type=F32)
            sbuf[ch, 8 * gh : 8 * gh + 8] = packed.astype(BF).reshape(8, 48, 512)

        def send(k, _, ch=ch):
            a2a(ch, k).start()
            return 0

        lax.fori_loop(1, 16, send, 0)
        keep(ch).start()
        forward(ch, 0, sbuf.at[ch, me]).start()

    @pl.when(jnp.logical_not(own))
    def _():
        swap(0).wait_recv()
        w_spread(wout.at[x], 0)
        swap(1).wait_recv()
        w_spread(wout.at[x], 1)

    def w_arrived(n):
        i, h = w_pairs[n]
        slot = (x, xl, xr, xf)[i]
        remote(wown.at[half[h]], wout.at[slot, half[h]], wsend.at[n], wrecv.at[i, h], f, mr).wait_recv()

    def relay_tokens(ch):
        def relay(k, _):
            slot = (g + 16 - k) % 16
            remote(sbuf.at[ch, 0], recv.at[ch, c, slot], asend.at[ch, k], arecv.at[ch, slot], f, m).wait_recv()
            forward(ch, k, recv.at[ch, c, slot]).start()
            return 0

        lax.fori_loop(1, 16, relay, 0)

    def tokens_arrived(ch):
        keep(ch).wait()

        def wait(k, _):
            slot = (g + 16 - k) % 16
            remote(sbuf.at[ch, 0], recv.at[ch, 1 - c, slot], fsend.at[ch, k], frecv.at[ch, k], f, m).wait_recv()
            return 0

        lax.fori_loop(0, 16, wait, 0)

    relay_tokens(0)
    w_arrived(0)
    w_ring(wout.at[xl, half[0]], xl, 4, mr).start()
    w_arrived(2)
    w_ring(wout.at[xr, half[1]], xr, 5, ml).start()

    lane = lax.broadcasted_iota(jnp.int32, (128, 128), 1)
    line = lax.broadcasted_iota(jnp.int32, (128, 128), 0)
    first = lane < 64
    allowed = (lane < 64) == (line < 64)

    def shard_of(i):
        return (x + (i % 2) * 3 + (i // 2) * (1 + (i % 2) * 2)) % 4

    def prepare(ch):
        for s in range(2):
            for gh in range(2):
                block = recv[ch, s, 8 * gh : 8 * gh + 8].reshape(384, 512)
                rows = jnp.dot(group_p[...], block, preferred_element_type=F32).astype(BF).reshape(2, 2, 6, 16, 512)
                for h in range(2):
                    xs[ch, :, :, s, 16 * gh : 16 * gh + 16, 512 * h : 512 * h + 512] = rows[h]

        def norm(u, _):
            xhat, _ = standardize(xs[ch, 0, u].reshape(64, D).astype(F32))
            normed[pl.ds(pl.multiple_of(ch * 384 + u * 64, 64), 64), :] = (xhat * gain[...]).astype(BF)
            return 0

        lax.fori_loop(0, 6, norm, 0)
        for i in range(3):
            at = 384 * ch + 128 * i
            norm_t[:, at : at + 128] = normed[at : at + 128, :].T
            og_t[:, at : at + 128] = xs[ch, 1, 2 * i : 2 * i + 2].reshape(128, D).T

    def heads(ch, i):
        j = shard_of(i)
        at = 384 * ch
        if ch == 0:
            wt[i] = wout[j, :, 0:384].T
        proj[:, 0:384] = jnp.dot(normed[at : at + 384, :], wout[j, :, 0:384], preferred_element_type=F32).astype(BF)
        proj[:, 384:512] = jnp.dot(
            xs[ch, 1].reshape(384, D), wout[j, :, 384:512], preferred_element_type=F32
        ).astype(BF)
        for n in range(3):
            rows = slice(128 * n, 128 * n + 128)
            out, dq, dk, dv = attend(
                proj[rows, 0:128], proj[rows, 128:256], proj[rows, 256:384], proj[rows, 384:512], allowed, first
            )
            rows = slice(at + 128 * n, at + 128 * n + 128)
            back[i, rows, 0:128] = dq.astype(BF)
            back[i, rows, 128:256] = dk.astype(BF)
            back[i, rows, 256:384] = dv.astype(BF)
            ao[i, rows, :] = out.astype(BF)

    def to_sibling(ch):
        return remote(other.at[ch], rsib.at[ch], bsend.at[ch], brecv.at[ch], sib, m)

    def partial(ch):
        for n in range(3):
            rows = slice(384 * ch + 128 * n, 384 * ch + 128 * n + 128)
            term = jnp.dot(back[0, rows, :], wt[0], preferred_element_type=F32)
            for i in range(1, 4):
                term += jnp.dot(back[i, rows, :], wt[i], preferred_element_type=F32)
            part[2 * n : 2 * n + 2] = term.reshape(2, 2, 32, D)
        other[ch] = part[:, 1 - c].astype(BF)
        to_sibling(ch).start()

    def back_to(ch, k):
        n = (g + k) % 16
        fs, ms, slot = source(n)
        return remote(sret.at[ch, n], rret.at[ch, slot], csend.at[ch, k], crecv.at[ch, slot], fs, ms)

    def keep_back(ch):
        return pltpu.make_async_copy(sret.at[ch, g], rret.at[ch, me], kloc.at[2 + ch])

    def token_gradient(ch):
        to_sibling(ch).wait_recv()

        def token(u, total):
            xhat, rstd = standardize(xs[ch, 0, u, c].astype(F32))
            dn = part[u, c] + rsib[ch, u].astype(F32)
            bp = dn * gain[...]
            inner = bp - jnp.mean(bp, axis=-1, keepdims=True) - xhat * jnp.mean(bp * xhat, axis=-1, keepdims=True)
            tg[u] = (xs[ch, 1, u, c].astype(F32) + rstd * inner).astype(BF)
            return total + jnp.sum((dn * xhat).reshape(4, 8, D), axis=0)

        total = lax.fori_loop(0, 6, token, jnp.zeros((8, D), F32))
        if ch == 0:
            gacc[...] = total
        else:
            gacc[...] += total
        for gh in range(2):
            rows = slice(16 * gh, 16 * gh + 16)
            parts = [tg[:, rows, 256 * h : 256 * h + 256].reshape(96, 256) for h in range(4)]
            packed = jnp.dot(repack_p[...], jnp.concatenate(parts, axis=0), preferred_element_type=F32)
            sret[ch, 8 * gh : 8 * gh + 8] = packed.astype(BF).reshape(8, 48, 256)

        def send(k, _):
            back_to(ch, k).start()
            return 0

        lax.fori_loop(1, 16, send, 0)
        keep_back(ch).start()

    def piece(ch, h, mm):
        rows = pl.ds(pl.multiple_of((mm % 4) * 64 + window(mm // 4, h) * 16, 16), 16)
        return tgrad.at[pl.ds(6 * ch, 6), rows, :]

    def kept(ch, h):
        return blk.at[ch, :, pl.ds(16 * h, 16), :]

    def pair(ch, h):
        return remote(kept(ch, h), piece(ch, h, m), psend.at[ch, h], precv.at[ch, h], f, mz)

    def ring(ch, r, src, mm, h, n, to):
        return remote(src, piece(ch, h, mm), rsend.at[ch, r, n], rrecv.at[ch, r, n], f, to)

    def own_out(ch, h):
        return pltpu.make_async_copy(kept(ch, h), piece(ch, h, m), oloc.at[ch, h])

    def gather_own(ch):
        keep_back(ch).wait()

        def received(k, _):
            slot = (me + k) % 16
            remote(sret.at[ch, 0], rret.at[ch, slot], csend.at[ch, k], crecv.at[ch, slot], f, m).wait_recv()
            return 0

        lax.fori_loop(1, 16, received, 0)
        for gh in range(2):
            block = rret[ch, 8 * gh : 8 * gh + 8].reshape(384, 256)
            rows = jnp.dot(unpack_p[...], block, preferred_element_type=F32).astype(BF).reshape(4, 6, 16, 256)
            for h in range(4):
                blk[ch, :, 16 * gh : 16 * gh + 16, 256 * h : 256 * h + 256] = rows[h]
        pair(ch, 0).start()
        pair(ch, 1).start()
        ring(ch, 0, kept(ch, 0), m, 0, 0, mr).start()
        ring(ch, 0, kept(ch, 1), m, 1, 2, ml).start()
        ring(ch, 0, kept(ch, 1), m, 1, 1, mr).start()
        ring(ch, 0, kept(ch, 0), m, 0, 3, ml).start()
        own_out(ch, 0).start()
        own_out(ch, 1).start()

    def gather_pair(ch):
        def arrived(h):
            remote(kept(ch, h), piece(ch, h, mz), psend.at[ch, h], precv.at[ch, h], f, mz).wait_recv()

        arrived(0)
        ring(ch, 1, piece(ch, 0, mz), mz, 0, 0, mr).start()
        ring(ch, 1, piece(ch, 0, mz), mz, 0, 3, ml).start()
        arrived(1)
        ring(ch, 1, piece(ch, 1, mz), mz, 1, 2, ml).start()
        ring(ch, 1, piece(ch, 1, mz), mz, 1, 1, mr).start()

    def base(r):
        return (z if r == 0 else 1 - z) * 4

    def arrived(ch, r, mm, h, n):
        ring(ch, r, piece(ch, h, base(r) + mm), base(r) + mm, h, n, mr).wait_recv()

    def gather_relay(ch, r):
        arrived(ch, r, xl, 0, 0)
        ring(ch, r, piece(ch, 0, base(r) + xl), base(r) + xl, 0, 4, mr).start()
        arrived(ch, r, xr, 1, 2)
        ring(ch, r, piece(ch, 1, base(r) + xr), base(r) + xr, 1, 5, ml).start()

    def weights(i):
        j = shard_of(i)

        def block(a, _):
            rows = pl.ds(pl.multiple_of(a * 256, 256), 256)
            left = jnp.dot(norm_t[rows, :], back[i], preferred_element_type=F32).astype(BF)
            grads[j, a, :, :, :, 0:384] = left.reshape(4, 2, 32, 384)
            left = jnp.dot(og_t[rows, :], ao[i], preferred_element_type=F32).astype(BF)
            grads[j, a, :, :, :, 384:512] = left.reshape(4, 2, 32, 128)
            return 0

        lax.fori_loop(0, 4, block, 0)
        y_far(i, 0).start()
        y_far(i, 1).start()

    def y_far(i, h):
        src = grads.at[shard_of(i), pl.ds(2 * h, 2), yf]
        return remote(src, gf.at[i, h], y1send.at[i, h], y1recv.at[i, h], fr if h == 0 else fl, m)

    def y_near(i, h):
        src = grads.at[shard_of(i), :, yr if h == 0 else yl]
        return remote(src, gn.at[i, h], y2send.at[i, h], y2recv.at[i, h], fr if h == 0 else fl, m)

    def y_step(i, _):
        j = shard_of(i)
        for h in range(2):
            y_far(i, h).wait_recv()
            to = yr if h == 0 else yl
            for a in range(2):
                total = grads[j, 2 * h + a, to].astype(F32) + gf[i, h, a].astype(F32)
                grads[j, 2 * h + a, to] = total.astype(BF)
            y_near(i, h).start()
        return 0

    def z_copy(i, n):
        to = ((n // 2) * 4 + y) * 2 + n % 2
        return remote(gz.at[i, n], gzr.at[i, zi], zsend.at[i, n], zrecv.at[i, zi], to, c * 4 + x)

    def zg_copy(n):
        to = ((n // 2) * 4 + y) * 2 + n % 2
        return remote(gzg.at[n], gzgr.at[zi], zsend.at[4, n], zrecv.at[4, zi], to, c * 4 + x)

    def z_self(n):
        return jnp.logical_and(n == zh * 2 + c, own)

    def own_z(i):
        return pltpu.make_async_copy(gz.at[i, zh * 2 + c], gzr.at[i, zi], zloc.at[i])

    def own_zg():
        return pltpu.make_async_copy(gzg.at[zh * 2 + c], gzgr.at[zi], zloc.at[4])

    def z_step(i, _):
        j = shard_of(i)
        for h in range(2):
            y_near(i, h).wait_recv()
        for a in range(4):
            total = grads[j, a, y].astype(F32) + (gn[i, 0, a].astype(F32) + gn[i, 1, a].astype(F32))
            gz[i, 2 * a : 2 * a + 2] = total.astype(BF)

        def z_send(n, _):
            @pl.when(jnp.logical_not(z_self(n)))
            def _():
                z_copy(i, n).start()

            return 0

        lax.fori_loop(0, 8, z_send, 0)

        @pl.when(own)
        def _():
            own_z(i).start()

        return 0

    def z_wait(i, src, dst):
        def wait(n, _):
            @pl.when(jnp.logical_not(jnp.logical_and(n == zi, own)))
            def _():
                remote(src, dst(n), zsend.at[i, 0], zrecv.at[i, n], f, m).wait_recv()

            return 0

        lax.fori_loop(0, 8, wait, 0)

    def sum8(terms):
        while len(terms) > 1:
            terms = [a + b for a, b in zip(terms[::2], terms[1::2])]
        return terms[0]

    def x_copy(i):
        return remote(gxs.at[i], gxr.at[i], xsend.at[i], xrecv.at[i], f, z * 4 + shard_of(i))

    def x_step(i, _):
        z_wait(i, gz.at[0, 0], lambda n: gzr.at[i, n])

        @pl.when(own)
        def _():
            own_z(i).wait()

        gxs[i] = sum8([gzr[i, k].astype(F32) for k in range(8)]).astype(BF)

        @pl.when(i > 0)
        def _():
            x_copy(i).start()

        return 0

    def gain_y(k):
        yk = (y + k) % 4
        return remote(gcol.at[:, yk], ggr.at[k], gsend.at[k], grecv.at[k], (zh * 4 + yk) * 2 + c, m)

    own_gain = pltpu.make_async_copy(gcol.at[:, y], ggr.at[0], gloc)

    def gain_x(k):
        return remote(gxg, gxgr.at[k], hsend.at[k], hrecv.at[k], f, z * 4 + (x + k) % 4)

    to_sib_gain = remote(gvec, gvecr, vsend, vrecv, sib, m)

    tokens_arrived(0)
    prepare(0)

    @pl.when(own)
    def _():
        own_w.wait()

    def first_heads(i, _):
        @pl.when(i == 3)
        def _():
            relay_tokens(1)

        @pl.when(i > 0)
        def _():
            slot = shard_of(i)
            for h in range(2):
                waited = jnp.logical_and(i < 3, h == i - 1)

                @pl.when(jnp.logical_not(waited))
                def _():
                    remote(wown.at[half[h]], wout.at[slot, half[h]], wsend.at[0], wrecv.at[i, h], f, mr).wait_recv()

        heads(0, i)
        return 0

    lax.fori_loop(0, 4, first_heads, 0)
    partial(0)
    token_gradient(0)

    tokens_arrived(1)
    prepare(1)

    def second_heads(i, _):
        @pl.when(i == 2)
        def _():
            gather_own(0)

        heads(1, i)
        return 0

    lax.fori_loop(0, 4, second_heads, 0)
    gather_pair(0)

    def all_weights(i, _):
        weights(i)
        return 0

    lax.fori_loop(0, 4, all_weights, 0)
    lax.fori_loop(0, 2, y_step, 0)
    partial(1)
    gather_relay(0, 0)
    lax.fori_loop(2, 4, y_step, 0)
    token_gradient(1)
    gvec[...] = jnp.broadcast_to(jnp.sum(gacc[...], axis=0, keepdims=True), (8, D))
    to_sib_gain.start()
    gather_relay(0, 1)
    to_sib_gain.wait_recv()
    gcol[...] = jnp.broadcast_to(gvec[0:1] + gvecr[0:1], (128, D)).T.astype(BF).reshape(4, 4, 2, 32, 128)
    for k in range(1, 4):
        gain_y(k).start()
    own_gain.start()
    lax.fori_loop(0, 2, z_step, 0)
    gather_own(1)
    lax.fori_loop(2, 4, z_step, 0)
    gather_pair(1)
    gather_relay(1, 0)

    own_gain.wait()
    for k in range(1, 4):
        remote(ggr.at[0], ggr.at[k], gsend.at[k], grecv.at[k], f, m).wait_recv()
    total = sum8([ggr[k].astype(F32) for k in range(4)])
    gzg[...] = total.astype(BF).reshape(8, 32, 128)

    def zg_send(n, _):
        @pl.when(jnp.logical_not(z_self(n)))
        def _():
            zg_copy(n).start()

        return 0

    lax.fori_loop(0, 8, zg_send, 0)

    @pl.when(own)
    def _():
        own_zg().start()

    lax.fori_loop(0, 4, x_step, 0)
    z_wait(4, gzg.at[0], lambda n: gzgr.at[n])

    @pl.when(own)
    def _():
        own_zg().wait()

    gxg[...] = sum8([gzgr[k].astype(F32) for k in range(8)]).astype(BF)
    for k in range(1, 4):
        gain_x(k).start()
    gather_relay(1, 1)

    for i in range(1, 4):
        x_copy(i).wait_recv()
    total = sum8([gxs[0].astype(F32)] + [gxr[i].astype(F32) for i in range(1, 4)])
    for j in range(3):
        gq[j] = total[:, 128 * j : 128 * j + 128]
    go[...] = total[:, 384:512]
    for k in range(1, 4):
        gain_x(k).wait_recv()
    total = sum8([gxg[...].astype(F32)] + [gxgr[k].astype(F32) for k in range(1, 4)])
    gg[...] = jnp.broadcast_to(total[0:32, 0:1], (32, 128))

    for ch in range(2):
        for r in range(2):
            arrived(ch, r, xl, 1, 1)
            arrived(ch, r, xr, 0, 3)
            arrived(ch, r, xf, 0, 4)
            arrived(ch, r, xf, 1, 5)
            for n, (mm, h) in enumerate(((x, 0), (x, 1), (x, 1), (x, 0), (xl, 0), (xr, 1))):
                ring(ch, r, piece(ch, h, base(r) + mm), base(r) + mm, h, n, mr).wait_send()
        pair(ch, 0).wait_send()
        pair(ch, 1).wait_send()
        own_out(ch, 0).wait()
        own_out(ch, 1).wait()
        to_sibling(ch).wait_send()

        def sent(k, _, ch=ch):
            a2a(ch, k).wait_send()
            back_to(ch, k).wait_send()
            forward(ch, k, recv.at[ch, c, (g + 16 - k) % 16]).wait_send()
            return 0

        lax.fori_loop(1, 16, sent, 0)
        forward(ch, 0, sbuf.at[ch, me]).wait_send()
    to_sib_gain.wait_send()
    for n in range(6):
        i, h = w_pairs[n]
        w_ring(wown.at[half[h]], x, n, mr).wait_send()

    @pl.when(jnp.logical_not(own))
    def _():
        swap(0).wait_send()
        swap(1).wait_send()

    for k in range(1, 4):
        gain_y(k).wait_send()
        gain_x(k).wait_send()
        x_copy(k).wait_send()

    def y_sent(i, _):
        for h in range(2):
            y_far(i, h).wait_send()
            y_near(i, h).wait_send()
        return 0

    lax.fori_loop(0, 4, y_sent, 0)

    def z_sent(n, _):
        @pl.when(jnp.logical_not(z_self(n)))
        def _():
            for i in range(4):
                z_copy(i, n).wait_send()
            zg_copy(n).wait_send()

        return 0

    lax.fori_loop(0, 8, z_sent, 0)


def sublayer(tok, og, qkvw, outw, gain):
    vm = pl.BlockSpec(memory_space=pltpu.VMEM)
    hbm = pl.BlockSpec(memory_space=pltpu.HBM)
    dma = pltpu.SemaphoreType.DMA
    perms = [jnp.asarray(p, BF) for p in (PACK, GROUP, REPACK, UNPACK)]
    bf = lambda *shape: pltpu.VMEM(shape, BF)
    return pl.pallas_call(
        sublayer_kernel,
        out_shape=(
            jax.ShapeDtypeStruct((12, 256, D), BF),
            jax.ShapeDtypeStruct((3, 32, 128), F32),
            jax.ShapeDtypeStruct((32, 128), F32),
            jax.ShapeDtypeStruct((32, 128), F32),
        ),
        in_specs=[hbm] * 4 + [vm] * 5,
        out_specs=(hbm, vm, vm, vm),
        scratch_shapes=[
            bf(2, 2, 6, 32, D),
            bf(2, 16, 48, 512),
            bf(2, 2, 16, 48, 512),
            bf(D, 512),
            bf(4, D, 512),
            bf(4, 384, D),
            bf(128, D),
            bf(2, 2, 6, 2, 32, D),
            bf(768, D),
            bf(D, 768),
            bf(D, 768),
            bf(384, 512),
            bf(4, 768, 384),
            bf(4, 768, 128),
            pltpu.VMEM((6, 2, 32, D), F32),
            bf(2, 6, 32, D),
            bf(2, 6, 32, D),
            bf(6, 32, D),
            pltpu.VMEM((8, D), F32),
            pltpu.VMEM((8, D), F32),
            pltpu.VMEM((8, D), F32),
            bf(4, 4, 2, 32, 128),
            bf(2, 16, 48, 256),
            bf(2, 16, 48, 256),
            bf(2, 6, 32, D),
            bf(4, 4, 4, 2, 32, 512),
            bf(4, 2, 2, 2, 32, 512),
            bf(4, 2, 4, 2, 32, 512),
            bf(4, 4, 2, 32, 128),
            bf(4, 8, 32, 512),
            bf(4, 8, 32, 512),
            bf(8, 32, 128),
            bf(8, 32, 128),
            bf(4, 32, 512),
            bf(4, 32, 512),
            bf(32, 128),
            bf(4, 32, 128),
            dma((12,)),
            dma((4,)),
            dma,
            dma((2, 2)),
            dma((5,)),
            dma,
            dma((2, 16)),
            dma((2, 16)),
            dma((2, 16)),
            dma((2, 16)),
            dma((2,)),
            dma((2,)),
            dma((6,)),
            dma((4, 2)),
            dma((2,)),
            dma((2,)),
            dma,
            dma,
            dma((2, 16)),
            dma((2, 16)),
            dma((2, 2)),
            dma((2, 2)),
            dma((2, 2, 6)),
            dma((2, 2, 6)),
            dma((4, 2)),
            dma((4, 2)),
            dma((4, 2)),
            dma((4, 2)),
            dma((4,)),
            dma((4,)),
            dma((5, 8)),
            dma((5, 8)),
            dma((4,)),
            dma((4,)),
            dma((4,)),
            dma((4,)),
        ],
        compiler_params=pltpu.CompilerParams(
            collective_id=0, has_side_effects=True, vmem_limit_bytes=57 * 2**20
        ),
        name="sublayer",
    )(tok, og, qkvw, outw, gain, *perms)


def shards(tokens, output_gradient, gain, qkv_weight, out_weight):
    clips, frames, patches, width = tokens.shape
    tgrad, gq, go, gg = sublayer(
        tokens.reshape(12, 256, D),
        output_gradient.reshape(12, 256, D),
        jnp.transpose(qkv_weight, (1, 0, 2)),
        out_weight,
        gain.reshape(1, D),
    )
    return (
        tgrad.reshape(clips, frames, patches, width),
        jnp.transpose(gq, (1, 0, 2)),
        go.T,
        gg[:, 0],
    )


def solution(mesh):
    in_specs = (
        P(None, "frame", None, None),
        P(None, "frame", None, None),
        P(),
        P(None, None, "mlp"),
        P("mlp", None),
    )
    out_specs = (
        P(None, "frame", None, None),
        P("frame", None, "mlp"),
        P("mlp", "frame"),
        P("frame"),
    )
    return jax.shard_map(shards, mesh=mesh, in_specs=in_specs, out_specs=out_specs, check_vma=False)
```

```python
import numpy as np

import jax
import jax.numpy as jnp
from jax import lax
from jax.experimental import pallas as pl
from jax.experimental.pallas import tpu as pltpu
from jax.sharding import PartitionSpec as P

MESH = pl.DeviceIdType.MESH
BF = jnp.bfloat16
F32 = jnp.float32
D = 1024
FACTOR = 64 ** (-0.5)
NEG = -1e30


def one_hot(shape, perm):
    index = np.arange(384).reshape(shape).transpose(perm).reshape(-1)
    return np.eye(384, dtype=np.float32)[index]


PACK = one_hot((2, 2, 6, 8, 2), (3, 0, 1, 4, 2))
GROUP = one_hot((8, 2, 2, 6, 2), (1, 2, 3, 0, 4))
REPACK = one_hot((4, 6, 8, 2), (2, 0, 1, 3))
UNPACK = one_hot((8, 4, 2, 6), (1, 3, 0, 2))


def remote(src, dst, send, recv, f, m):
    return pltpu.make_async_remote_copy(
        src_ref=src, dst_ref=dst, send_sem=send, recv_sem=recv, device_id=(f, m), device_id_type=MESH
    )


def greet(barrier, f, m):
    pl.semaphore_signal(barrier, inc=1, device_id=(f, m), device_id_type=MESH)


def standardize(values):
    centered = values - jnp.mean(values, axis=-1, keepdims=True)
    rstd = lax.rsqrt(jnp.mean(centered * centered, axis=-1, keepdims=True) + 1e-05)
    return centered * rstd, rstd


def dot_t(a, b):
    return lax.dot_general(a, b, (((1,), (1,)), ((), ())), preferred_element_type=F32)


def t_dot(a, b):
    return lax.dot_general(a, b, (((0,), (0,)), ((), ())), preferred_element_type=F32)


def attend(q, k, v, d, allowed, first):
    zero = jnp.zeros_like(k)
    k2 = jnp.concatenate([jnp.where(first, k, zero), jnp.where(first, zero, k)], axis=0)
    v2 = jnp.concatenate([jnp.where(first, v, zero), jnp.where(first, zero, v)], axis=0)
    scores = dot_t(q, k2) * FACTOR
    dprob = dot_t(d, v2)
    probs, dscore = [], []
    for h in range(2):
        s = jnp.where(allowed, scores[:, 128 * h : 128 * h + 128], NEG)
        e = jnp.exp(s - jnp.max(s, axis=-1, keepdims=True))
        p = e * (1.0 / jnp.sum(e, axis=-1, keepdims=True))
        dp = dprob[:, 128 * h : 128 * h + 128]
        delta = jnp.sum(p * dp, axis=-1, keepdims=True)
        probs.append(p.astype(BF))
        dscore.append((p * (dp - delta) * FACTOR).astype(BF))
    probs = jnp.concatenate(probs, axis=1)
    dscore = jnp.concatenate(dscore, axis=1)
    out = jnp.dot(probs, v2, preferred_element_type=F32)
    dq = jnp.dot(dscore, k2, preferred_element_type=F32)
    dv = t_dot(probs, d)
    dk = t_dot(dscore, q)
    dv = jnp.where(first, dv[:128], dv[128:])
    dk = jnp.where(first, dk[:128], dk[128:])
    return out, dq, dk, dv


def sublayer_kernel(
    tok, og, qkvw, outw, gain, pack_p, group_p, repack_p, unpack_p,
    tgrad, gq, go, gg,
    xin, sbuf, recv, wown, wout, wt, ow, xs, normed, norm_t, og_t, proj, back, ao, part, other, rsib,
    tg, gacc, gvec, gvecr, gcol, sret, rret, blk, grads, gf, gn, ggr, gz, gzr, gzg, gzgr, gxs, gxr, gxg, gxgr,
    loc, kloc, wloc, oloc, zloc, gloc,
    asend, arecv, fsend, frecv, ssend, srecv, wsend, wrecv, bsend, brecv, vsend, vrecv,
    csend, crecv, psend, precv, rsend, rrecv, y1send, y1recv, y2send, y2recv, gsend, grecv,
    zsend, zrecv, xsend, xrecv, hsend, hrecv,
):
    f, m = lax.axis_index("frame"), lax.axis_index("mlp")
    g, c, z, x = f // 2, f % 2, m // 4, m % 4
    zh, y = f // 8, (f // 2) % 4
    zi = zh * 2 + z
    sib = g * 2 + 1 - c
    mz = (1 - z) * 4 + x
    xl, xr, xf = (x + 3) % 4, (x + 1) % 4, (x + 2) % 4
    mr, ml = z * 4 + xr, z * 4 + xl
    yl, yr, yf = (y + 3) % 4, (y + 1) % 4, (y + 2) % 4
    fr, fl = (zh * 4 + yr) * 2 + c, (zh * 4 + yl) * 2 + c
    own = c == z
    start = (zi + 5 + 3 * z) % 8
    me = (3 - 3 * z) * 4 + y

    def window(lo, h):
        return (zh + 3 - 2 * lo + h) % 4

    def owner(slot):
        to = (start + slot // 4) % 8
        return ((to // 2) * 4 + slot % 4) * 2 + c, (to % 2) * 4 + x

    def source(n):
        there = n // 4
        d = (there + 4 - zh) % 4
        lo = (d % 2) * (d // 2) + (1 - d % 2) * ((d // 2) * (1 - z) + (1 - d // 2) * z)
        place = (zi + 16 - (there * 2 + lo + 5 + 3 * lo)) % 8
        return n * 2 + c, lo * 4 + x, place * 4 + y

    w_in = [pltpu.make_async_copy(qkvw.at[j], wown.at[:, pl.ds(128 * j, 128)], loc.at[j]) for j in range(3)]
    w_in.append(pltpu.make_async_copy(outw, ow, loc.at[3]))
    for copy in w_in:
        copy.start()
    x_in = []
    for ch in range(2):
        for t, ref in enumerate((tok, og)):
            for h in range(2):
                rows = pl.ds(pl.multiple_of(x * 64 + window(z, h) * 16, 16), 16)
                x_in.append(
                    pltpu.make_async_copy(
                        ref.at[pl.ds(6 * ch, 6), rows, :],
                        xin.at[ch, t, :, pl.ds(16 * h, 16), :],
                        loc.at[4 + 4 * ch + 2 * t + h],
                    )
                )
                x_in[-1].start()

    barrier = pltpu.get_barrier_semaphore()

    def hello_plane(k, _):
        n = (zi * 4 + y + k) % 32
        greet(barrier, ((n // 8) * 4 + n % 4) * 2 + c, ((n // 4) % 2) * 4 + x)
        return 0

    def hello_other(k, _):
        greet(barrier, ((k // 2) * 4 + y) * 2 + 1 - c, (k % 2) * 4 + x)
        return 0

    lax.fori_loop(1, 32, hello_plane, 0)
    lax.fori_loop(0, 8, hello_other, 0)
    for k in range(1, 4):
        greet(barrier, f, z * 4 + (x + k) % 4)

    for copy in w_in:
        copy.wait()
    wown[:, 384:512] = ow[...].T
    pl.semaphore_wait(barrier, 42)

    half = (pl.ds(0, 512), pl.ds(512, 512))
    w_pairs = ((1, 0), (1, 1), (2, 1), (2, 0), (3, 0), (3, 1))

    def w_ring(src, slot, n, to):
        i, h = w_pairs[n]
        return remote(src, wout.at[slot, half[h]], wsend.at[n], wrecv.at[i, h], f, to)

    def w_spread(src, h):
        if h == 0:
            w_ring(src.at[half[0]], x, 0, mr).start()
            w_ring(src.at[half[0]], x, 3, ml).start()
        else:
            w_ring(src.at[half[1]], x, 2, ml).start()
            w_ring(src.at[half[1]], x, 1, mr).start()

    far = (zi + 7 + 2 * z) % 8
    near_id = (g * 2 + 1 - c, mz)
    far_id = (((far // 2) * 4 + y) * 2 + 1 - c, (far % 2) * 4 + x)

    def swap(h):
        return remote(
            wown.at[half[h]], wout.at[x, half[h]], ssend.at[h], srecv.at[h], *(near_id if h == 0 else far_id)
        )

    own_w = pltpu.make_async_copy(wown, wout.at[x], wloc)

    @pl.when(own)
    def _():
        w_spread(wown, 0)
        w_spread(wown, 1)
        own_w.start()

    @pl.when(jnp.logical_not(own))
    def _():
        swap(0).start()
        swap(1).start()

    def a2a(ch, k):
        slot = (me + k) % 16
        return remote(sbuf.at[ch, slot], recv.at[ch, c, g], asend.at[ch, k], arecv.at[ch, g], *owner(slot))

    def forward(ch, k, src):
        slot = (g + 16 - k) % 16
        return remote(src, recv.at[ch, c, slot], fsend.at[ch, k], frecv.at[ch, k], sib, m)

    def keep(ch):
        return pltpu.make_async_copy(sbuf.at[ch, me], recv.at[ch, c, g], kloc.at[ch])

    for ch in range(2):
        for copy in x_in[4 * ch : 4 * ch + 4]:
            copy.wait()
        for gh in range(2):
            rows = slice(16 * gh, 16 * gh + 16)
            parts = [xin[ch, t, :, rows, 512 * h : 512 * h + 512].reshape(96, 512) for h in range(2) for t in range(2)]
            packed = jnp.dot(pack_p[...], jnp.concatenate(parts, axis=0), preferred_element_type=F32)
            sbuf[ch, 8 * gh : 8 * gh + 8] = packed.astype(BF).reshape(8, 48, 512)

        def send(k, _, ch=ch):
            a2a(ch, k).start()
            return 0

        lax.fori_loop(1, 16, send, 0)
        keep(ch).start()
        forward(ch, 0, sbuf.at[ch, me]).start()

    @pl.when(jnp.logical_not(own))
    def _():
        swap(0).wait_recv()
        w_spread(wout.at[x], 0)
        swap(1).wait_recv()
        w_spread(wout.at[x], 1)

    def w_arrived(n):
        i, h = w_pairs[n]
        slot = (x, xl, xr, xf)[i]
        remote(wown.at[half[h]], wout.at[slot, half[h]], wsend.at[n], wrecv.at[i, h], f, mr).wait_recv()

    def relay_tokens(ch):
        def relay(k, _):
            slot = (g + 16 - k) % 16
            remote(sbuf.at[ch, 0], recv.at[ch, c, slot], asend.at[ch, k], arecv.at[ch, slot], f, m).wait_recv()
            forward(ch, k, recv.at[ch, c, slot]).start()
            return 0

        lax.fori_loop(1, 16, relay, 0)

    def tokens_arrived(ch):
        keep(ch).wait()

        def wait(k, _):
            slot = (g + 16 - k) % 16
            remote(sbuf.at[ch, 0], recv.at[ch, 1 - c, slot], fsend.at[ch, k], frecv.at[ch, k], f, m).wait_recv()
            return 0

        lax.fori_loop(0, 16, wait, 0)

    relay_tokens(0)
    w_arrived(0)
    w_ring(wout.at[xl, half[0]], xl, 4, mr).start()
    w_arrived(2)
    w_ring(wout.at[xr, half[1]], xr, 5, ml).start()

    lane = lax.broadcasted_iota(jnp.int32, (128, 128), 1)
    line = lax.broadcasted_iota(jnp.int32, (128, 128), 0)
    first = lane < 64
    allowed = (lane < 64) == (line < 64)

    def shard_of(i):
        return (x + (i % 2) * 3 + (i // 2) * (1 + (i % 2) * 2)) % 4

    def prepare(ch):
        for s in range(2):
            for gh in range(2):
                block = recv[ch, s, 8 * gh : 8 * gh + 8].reshape(384, 512)
                rows = jnp.dot(group_p[...], block, preferred_element_type=F32).astype(BF).reshape(2, 2, 6, 16, 512)
                for h in range(2):
                    xs[ch, :, :, s, 16 * gh : 16 * gh + 16, 512 * h : 512 * h + 512] = rows[h]

        def norm(u, _):
            xhat, _ = standardize(xs[ch, 0, u].reshape(64, D).astype(F32))
            normed[pl.ds(pl.multiple_of(ch * 384 + u * 64, 64), 64), :] = (xhat * gain[...]).astype(BF)
            return 0

        lax.fori_loop(0, 6, norm, 0)
        for i in range(3):
            at = 384 * ch + 128 * i
            norm_t[:, at : at + 128] = normed[at : at + 128, :].T
            og_t[:, at : at + 128] = xs[ch, 1, 2 * i : 2 * i + 2].reshape(128, D).T

    def heads(ch, i):
        j = shard_of(i)
        at = 384 * ch
        if ch == 0:
            wt[i] = wout[j, :, 0:384].T
        proj[:, 0:384] = jnp.dot(normed[at : at + 384, :], wout[j, :, 0:384], preferred_element_type=F32).astype(BF)
        proj[:, 384:512] = jnp.dot(
            xs[ch, 1].reshape(384, D), wout[j, :, 384:512], preferred_element_type=F32
        ).astype(BF)
        for n in range(3):
            rows = slice(128 * n, 128 * n + 128)
            out, dq, dk, dv = attend(
                proj[rows, 0:128], proj[rows, 128:256], proj[rows, 256:384], proj[rows, 384:512], allowed, first
            )
            rows = slice(at + 128 * n, at + 128 * n + 128)
            back[i, rows, 0:128] = dq.astype(BF)
            back[i, rows, 128:256] = dk.astype(BF)
            back[i, rows, 256:384] = dv.astype(BF)
            ao[i, rows, :] = out.astype(BF)

    def to_sibling(ch):
        return remote(other.at[ch], rsib.at[ch], bsend.at[ch], brecv.at[ch], sib, m)

    def partial(ch):
        for n in range(3):
            rows = slice(384 * ch + 128 * n, 384 * ch + 128 * n + 128)
            term = jnp.dot(back[0, rows, :], wt[0], preferred_element_type=F32)
            for i in range(1, 4):
                term += jnp.dot(back[i, rows, :], wt[i], preferred_element_type=F32)
            part[2 * n : 2 * n + 2] = term.reshape(2, 2, 32, D)
        other[ch] = part[:, 1 - c].astype(BF)
        to_sibling(ch).start()

    def back_to(ch, k):
        n = (g + k) % 16
        fs, ms, slot = source(n)
        return remote(sret.at[ch, n], rret.at[ch, slot], csend.at[ch, k], crecv.at[ch, slot], fs, ms)

    def keep_back(ch):
        return pltpu.make_async_copy(sret.at[ch, g], rret.at[ch, me], kloc.at[2 + ch])

    def token_gradient(ch):
        to_sibling(ch).wait_recv()

        def token(u, total):
            xhat, rstd = standardize(xs[ch, 0, u, c].astype(F32))
            dn = part[u, c] + rsib[ch, u].astype(F32)
            bp = dn * gain[...]
            inner = bp - jnp.mean(bp, axis=-1, keepdims=True) - xhat * jnp.mean(bp * xhat, axis=-1, keepdims=True)
            tg[u] = (xs[ch, 1, u, c].astype(F32) + rstd * inner).astype(BF)
            return total + jnp.sum((dn * xhat).reshape(4, 8, D), axis=0)

        total = lax.fori_loop(0, 6, token, jnp.zeros((8, D), F32))
        if ch == 0:
            gacc[...] = total
        else:
            gacc[...] += total
        for gh in range(2):
            rows = slice(16 * gh, 16 * gh + 16)
            parts = [tg[:, rows, 256 * h : 256 * h + 256].reshape(96, 256) for h in range(4)]
            packed = jnp.dot(repack_p[...], jnp.concatenate(parts, axis=0), preferred_element_type=F32)
            sret[ch, 8 * gh : 8 * gh + 8] = packed.astype(BF).reshape(8, 48, 256)

        def send(k, _):
            back_to(ch, k).start()
            return 0

        lax.fori_loop(1, 16, send, 0)
        keep_back(ch).start()

    def piece(ch, h, mm):
        rows = pl.ds(pl.multiple_of((mm % 4) * 64 + window(mm // 4, h) * 16, 16), 16)
        return tgrad.at[pl.ds(6 * ch, 6), rows, :]

    def kept(ch, h):
        return blk.at[ch, :, pl.ds(16 * h, 16), :]

    def pair(ch, h):
        return remote(kept(ch, h), piece(ch, h, m), psend.at[ch, h], precv.at[ch, h], f, mz)

    def ring(ch, r, src, mm, h, n, to):
        return remote(src, piece(ch, h, mm), rsend.at[ch, r, n], rrecv.at[ch, r, n], f, to)

    def own_out(ch, h):
        return pltpu.make_async_copy(kept(ch, h), piece(ch, h, m), oloc.at[ch, h])

    def gather_own(ch):
        keep_back(ch).wait()

        def received(k, _):
            slot = (me + k) % 16
            remote(sret.at[ch, 0], rret.at[ch, slot], csend.at[ch, k], crecv.at[ch, slot], f, m).wait_recv()
            return 0

        lax.fori_loop(1, 16, received, 0)
        for gh in range(2):
            block = rret[ch, 8 * gh : 8 * gh + 8].reshape(384, 256)
            rows = jnp.dot(unpack_p[...], block, preferred_element_type=F32).astype(BF).reshape(4, 6, 16, 256)
            for h in range(4):
                blk[ch, :, 16 * gh : 16 * gh + 16, 256 * h : 256 * h + 256] = rows[h]
        pair(ch, 0).start()
        pair(ch, 1).start()
        ring(ch, 0, kept(ch, 0), m, 0, 0, mr).start()
        ring(ch, 0, kept(ch, 1), m, 1, 2, ml).start()
        ring(ch, 0, kept(ch, 1), m, 1, 1, mr).start()
        ring(ch, 0, kept(ch, 0), m, 0, 3, ml).start()
        own_out(ch, 0).start()
        own_out(ch, 1).start()

    def gather_pair(ch):
        def arrived(h):
            remote(kept(ch, h), piece(ch, h, mz), psend.at[ch, h], precv.at[ch, h], f, mz).wait_recv()

        arrived(0)
        ring(ch, 1, piece(ch, 0, mz), mz, 0, 0, mr).start()
        ring(ch, 1, piece(ch, 0, mz), mz, 0, 3, ml).start()
        arrived(1)
        ring(ch, 1, piece(ch, 1, mz), mz, 1, 2, ml).start()
        ring(ch, 1, piece(ch, 1, mz), mz, 1, 1, mr).start()

    def base(r):
        return (z if r == 0 else 1 - z) * 4

    def arrived(ch, r, mm, h, n):
        ring(ch, r, piece(ch, h, base(r) + mm), base(r) + mm, h, n, mr).wait_recv()

    def gather_relay(ch, r):
        arrived(ch, r, xl, 0, 0)
        ring(ch, r, piece(ch, 0, base(r) + xl), base(r) + xl, 0, 4, mr).start()
        arrived(ch, r, xr, 1, 2)
        ring(ch, r, piece(ch, 1, base(r) + xr), base(r) + xr, 1, 5, ml).start()

    def weights(i):
        j = shard_of(i)

        def block(a, _):
            rows = pl.ds(pl.multiple_of(a * 256, 256), 256)
            left = jnp.dot(norm_t[rows, :], back[i], preferred_element_type=F32).astype(BF)
            grads[j, a, :, :, :, 0:384] = left.reshape(4, 2, 32, 384)
            left = jnp.dot(og_t[rows, :], ao[i], preferred_element_type=F32).astype(BF)
            grads[j, a, :, :, :, 384:512] = left.reshape(4, 2, 32, 128)
            return 0

        lax.fori_loop(0, 4, block, 0)
        y_far(i, 0).start()
        y_far(i, 1).start()

    def y_far(i, h):
        src = grads.at[shard_of(i), pl.ds(2 * h, 2), yf]
        return remote(src, gf.at[i, h], y1send.at[i, h], y1recv.at[i, h], fr if h == 0 else fl, m)

    def y_near(i, h):
        src = grads.at[shard_of(i), :, yr if h == 0 else yl]
        return remote(src, gn.at[i, h], y2send.at[i, h], y2recv.at[i, h], fr if h == 0 else fl, m)

    def y_step(i, _):
        j = shard_of(i)
        for h in range(2):
            y_far(i, h).wait_recv()
            to = yr if h == 0 else yl
            for a in range(2):
                total = grads[j, 2 * h + a, to].astype(F32) + gf[i, h, a].astype(F32)
                grads[j, 2 * h + a, to] = total.astype(BF)
            y_near(i, h).start()
        return 0

    def z_copy(i, n):
        to = ((n // 2) * 4 + y) * 2 + n % 2
        return remote(gz.at[i, n], gzr.at[i, zi], zsend.at[i, n], zrecv.at[i, zi], to, c * 4 + x)

    def zg_copy(n):
        to = ((n // 2) * 4 + y) * 2 + n % 2
        return remote(gzg.at[n], gzgr.at[zi], zsend.at[4, n], zrecv.at[4, zi], to, c * 4 + x)

    def z_self(n):
        return jnp.logical_and(n == zh * 2 + c, own)

    def own_z(i):
        return pltpu.make_async_copy(gz.at[i, zh * 2 + c], gzr.at[i, zi], zloc.at[i])

    def own_zg():
        return pltpu.make_async_copy(gzg.at[zh * 2 + c], gzgr.at[zi], zloc.at[4])

    def z_step(i, _):
        j = shard_of(i)
        for h in range(2):
            y_near(i, h).wait_recv()
        for a in range(4):
            total = grads[j, a, y].astype(F32) + (gn[i, 0, a].astype(F32) + gn[i, 1, a].astype(F32))
            gz[i, 2 * a : 2 * a + 2] = total.astype(BF)

        def z_send(n, _):
            @pl.when(jnp.logical_not(z_self(n)))
            def _():
                z_copy(i, n).start()

            return 0

        lax.fori_loop(0, 8, z_send, 0)

        @pl.when(own)
        def _():
            own_z(i).start()

        return 0

    def z_wait(i, src, dst):
        def wait(n, _):
            @pl.when(jnp.logical_not(jnp.logical_and(n == zi, own)))
            def _():
                remote(src, dst(n), zsend.at[i, 0], zrecv.at[i, n], f, m).wait_recv()

            return 0

        lax.fori_loop(0, 8, wait, 0)

    def sum8(terms):
        while len(terms) > 1:
            terms = [a + b for a, b in zip(terms[::2], terms[1::2])]
        return terms[0]

    def x_copy(i):
        return remote(gxs.at[i], gxr.at[i], xsend.at[i], xrecv.at[i], f, z * 4 + shard_of(i))

    def x_step(i, _):
        z_wait(i, gz.at[0, 0], lambda n: gzr.at[i, n])

        @pl.when(own)
        def _():
            own_z(i).wait()

        gxs[i] = sum8([gzr[i, k].astype(F32) for k in range(8)]).astype(BF)

        @pl.when(i > 0)
        def _():
            x_copy(i).start()

        return 0

    def gain_y(k):
        yk = (y + k) % 4
        return remote(gcol.at[:, yk], ggr.at[k], gsend.at[k], grecv.at[k], (zh * 4 + yk) * 2 + c, m)

    own_gain = pltpu.make_async_copy(gcol.at[:, y], ggr.at[0], gloc)

    def gain_x(k):
        return remote(gxg, gxgr.at[k], hsend.at[k], hrecv.at[k], f, z * 4 + (x + k) % 4)

    to_sib_gain = remote(gvec, gvecr, vsend, vrecv, sib, m)

    tokens_arrived(0)
    prepare(0)

    @pl.when(own)
    def _():
        own_w.wait()

    def shard_arrived(i):
        for h in range(2):
            waited = jnp.logical_or(i == 0, jnp.logical_and(i < 3, h == i - 1))

            @pl.when(jnp.logical_not(waited))
            def _():
                slot = shard_of(i)
                remote(wown.at[half[h]], wout.at[slot, half[h]], wsend.at[0], wrecv.at[i, h], f, mr).wait_recv()

    def first_heads(i, _):
        shard_arrived(i)
        heads(0, i)
        return 0

    def second_heads(i, _):
        heads(1, i)
        return 0

    def both_heads(i, _):
        shard_arrived(i)
        heads(0, i)

        @pl.when(i == 3)
        def _():
            partial(0)

        heads(1, i)
        return 0

    def all_weights(i, _):
        weights(i)
        return 0

    lax.fori_loop(0, 2, first_heads, 0)
    relay_tokens(1)
    tokens_arrived(1)
    prepare(1)
    lax.fori_loop(0, 2, second_heads, 0)
    lax.fori_loop(2, 4, both_heads, 0)
    token_gradient(0)
    lax.fori_loop(0, 2, all_weights, 0)
    gather_own(0)
    lax.fori_loop(2, 4, all_weights, 0)
    partial(1)
    y_step(0, 0)
    gather_pair(0)
    token_gradient(1)
    gvec[...] = jnp.broadcast_to(jnp.sum(gacc[...], axis=0, keepdims=True), (8, D))
    to_sib_gain.start()
    lax.fori_loop(1, 3, y_step, 0)
    gather_relay(0, 0)
    y_step(3, 0)
    to_sib_gain.wait_recv()
    gcol[...] = jnp.broadcast_to(gvec[0:1] + gvecr[0:1], (128, D)).T.astype(BF).reshape(4, 4, 2, 32, 128)
    for k in range(1, 4):
        gain_y(k).start()
    own_gain.start()
    gather_own(1)
    z_step(0, 0)
    gather_relay(0, 1)
    z_step(1, 0)
    gather_pair(1)
    z_step(2, 0)
    gather_relay(1, 0)
    z_step(3, 0)

    own_gain.wait()
    for k in range(1, 4):
        remote(ggr.at[0], ggr.at[k], gsend.at[k], grecv.at[k], f, m).wait_recv()
    total = sum8([ggr[k].astype(F32) for k in range(4)])
    gzg[...] = total.astype(BF).reshape(8, 32, 128)

    def zg_send(n, _):
        @pl.when(jnp.logical_not(z_self(n)))
        def _():
            zg_copy(n).start()

        return 0

    lax.fori_loop(0, 8, zg_send, 0)

    @pl.when(own)
    def _():
        own_zg().start()

    lax.fori_loop(0, 4, x_step, 0)
    z_wait(4, gzg.at[0], lambda n: gzgr.at[n])

    @pl.when(own)
    def _():
        own_zg().wait()

    gxg[...] = sum8([gzgr[k].astype(F32) for k in range(8)]).astype(BF)
    for k in range(1, 4):
        gain_x(k).start()
    gather_relay(1, 1)

    for i in range(1, 4):
        x_copy(i).wait_recv()
    total = sum8([gxs[0].astype(F32)] + [gxr[i].astype(F32) for i in range(1, 4)])
    for j in range(3):
        gq[j] = total[:, 128 * j : 128 * j + 128]
    go[...] = total[:, 384:512]
    for k in range(1, 4):
        gain_x(k).wait_recv()
    total = sum8([gxg[...].astype(F32)] + [gxgr[k].astype(F32) for k in range(1, 4)])
    gg[...] = jnp.broadcast_to(total[0:32, 0:1], (32, 128))

    for ch in range(2):
        for r in range(2):
            arrived(ch, r, xl, 1, 1)
            arrived(ch, r, xr, 0, 3)
            arrived(ch, r, xf, 0, 4)
            arrived(ch, r, xf, 1, 5)
            for n, (mm, h) in enumerate(((x, 0), (x, 1), (x, 1), (x, 0), (xl, 0), (xr, 1))):
                ring(ch, r, piece(ch, h, base(r) + mm), base(r) + mm, h, n, mr).wait_send()
        pair(ch, 0).wait_send()
        pair(ch, 1).wait_send()
        own_out(ch, 0).wait()
        own_out(ch, 1).wait()
        to_sibling(ch).wait_send()

        def sent(k, _, ch=ch):
            a2a(ch, k).wait_send()
            back_to(ch, k).wait_send()
            forward(ch, k, recv.at[ch, c, (g + 16 - k) % 16]).wait_send()
            return 0

        lax.fori_loop(1, 16, sent, 0)
        forward(ch, 0, sbuf.at[ch, me]).wait_send()
    to_sib_gain.wait_send()
    for n in range(6):
        i, h = w_pairs[n]
        w_ring(wown.at[half[h]], x, n, mr).wait_send()

    @pl.when(jnp.logical_not(own))
    def _():
        swap(0).wait_send()
        swap(1).wait_send()

    for k in range(1, 4):
        gain_y(k).wait_send()
        gain_x(k).wait_send()
        x_copy(k).wait_send()

    def y_sent(i, _):
        for h in range(2):
            y_far(i, h).wait_send()
            y_near(i, h).wait_send()
        return 0

    lax.fori_loop(0, 4, y_sent, 0)

    def z_sent(n, _):
        @pl.when(jnp.logical_not(z_self(n)))
        def _():
            for i in range(4):
                z_copy(i, n).wait_send()
            zg_copy(n).wait_send()

        return 0

    lax.fori_loop(0, 8, z_sent, 0)


def sublayer(tok, og, qkvw, outw, gain):
    vm = pl.BlockSpec(memory_space=pltpu.VMEM)
    hbm = pl.BlockSpec(memory_space=pltpu.HBM)
    dma = pltpu.SemaphoreType.DMA
    perms = [jnp.asarray(p, BF) for p in (PACK, GROUP, REPACK, UNPACK)]
    bf = lambda *shape: pltpu.VMEM(shape, BF)
    return pl.pallas_call(
        sublayer_kernel,
        out_shape=(
            jax.ShapeDtypeStruct((12, 256, D), BF),
            jax.ShapeDtypeStruct((3, 32, 128), F32),
            jax.ShapeDtypeStruct((32, 128), F32),
            jax.ShapeDtypeStruct((32, 128), F32),
        ),
        in_specs=[hbm] * 4 + [vm] * 5,
        out_specs=(pl.BlockSpec(memory_space=pl.ANY), vm, vm, vm),
        scratch_shapes=[
            bf(2, 2, 6, 32, D),
            bf(2, 16, 48, 512),
            bf(2, 2, 16, 48, 512),
            bf(D, 512),
            bf(4, D, 512),
            bf(4, 384, D),
            bf(128, D),
            bf(2, 2, 6, 2, 32, D),
            bf(768, D),
            bf(D, 768),
            bf(D, 768),
            bf(384, 512),
            bf(4, 768, 384),
            bf(4, 768, 128),
            pltpu.VMEM((6, 2, 32, D), F32),
            bf(2, 6, 32, D),
            bf(2, 6, 32, D),
            bf(6, 32, D),
            pltpu.VMEM((8, D), F32),
            pltpu.VMEM((8, D), F32),
            pltpu.VMEM((8, D), F32),
            bf(4, 4, 2, 32, 128),
            bf(2, 16, 48, 256),
            bf(2, 16, 48, 256),
            bf(2, 6, 32, D),
            bf(4, 4, 4, 2, 32, 512),
            bf(4, 2, 2, 2, 32, 512),
            bf(4, 2, 4, 2, 32, 512),
            bf(4, 4, 2, 32, 128),
            bf(4, 8, 32, 512),
            bf(4, 8, 32, 512),
            bf(8, 32, 128),
            bf(8, 32, 128),
            bf(4, 32, 512),
            bf(4, 32, 512),
            bf(32, 128),
            bf(4, 32, 128),
            dma((12,)),
            dma((4,)),
            dma,
            dma((2, 2)),
            dma((5,)),
            dma,
            dma((2, 16)),
            dma((2, 16)),
            dma((2, 16)),
            dma((2, 16)),
            dma((2,)),
            dma((2,)),
            dma((6,)),
            dma((4, 2)),
            dma((2,)),
            dma((2,)),
            dma,
            dma,
            dma((2, 16)),
            dma((2, 16)),
            dma((2, 2)),
            dma((2, 2)),
            dma((2, 2, 6)),
            dma((2, 2, 6)),
            dma((4, 2)),
            dma((4, 2)),
            dma((4, 2)),
            dma((4, 2)),
            dma((4,)),
            dma((4,)),
            dma((5, 8)),
            dma((5, 8)),
            dma((4,)),
            dma((4,)),
            dma((4,)),
            dma((4,)),
        ],
        compiler_params=pltpu.CompilerParams(
            collective_id=0, has_side_effects=True, vmem_limit_bytes=46 * 2**20
        ),
        name="sublayer",
    )(tok, og, qkvw, outw, gain, *perms)


def shards(tokens, output_gradient, gain, qkv_weight, out_weight):
    clips, frames, patches, width = tokens.shape
    tgrad, gq, go, gg = sublayer(
        tokens.reshape(12, 256, D),
        output_gradient.reshape(12, 256, D),
        jnp.transpose(qkv_weight, (1, 0, 2)),
        out_weight,
        gain.reshape(1, D),
    )
    return (
        tgrad.reshape(clips, frames, patches, width),
        jnp.transpose(gq, (1, 0, 2)),
        go.T,
        gg[:, 0],
    )


def solution(mesh):
    in_specs = (
        P(None, "frame", None, None),
        P(None, "frame", None, None),
        P(),
        P(None, None, "mlp"),
        P("mlp", None),
    )
    out_specs = (
        P(None, "frame", None, None),
        P("frame", None, "mlp"),
        P("mlp", "frame"),
        P("frame"),
    )
    return jax.shard_map(shards, mesh=mesh, in_specs=in_specs, out_specs=out_specs, check_vma=False)
```

```python
import numpy as np

import jax
import jax.numpy as jnp
from jax import lax
from jax.experimental import pallas as pl
from jax.experimental.pallas import tpu as pltpu
from jax.sharding import PartitionSpec as P

MESH = pl.DeviceIdType.MESH
BF = jnp.bfloat16
F32 = jnp.float32
D = 1024
FACTOR = 64 ** (-0.5)
NEG = -1e30


def one_hot(shape, perm):
    index = np.arange(384).reshape(shape).transpose(perm).reshape(-1)
    return np.eye(384, dtype=np.float32)[index]


PACK = one_hot((2, 2, 6, 8, 2), (3, 0, 1, 4, 2))
GROUP = one_hot((8, 2, 2, 6, 2), (1, 2, 3, 0, 4))
REPACK = one_hot((4, 6, 8, 2), (2, 0, 1, 3))
UNPACK = one_hot((8, 4, 2, 6), (1, 3, 0, 2))


def remote(src, dst, send, recv, f, m):
    return pltpu.make_async_remote_copy(
        src_ref=src, dst_ref=dst, send_sem=send, recv_sem=recv, device_id=(f, m), device_id_type=MESH
    )


def greet(barrier, f, m):
    pl.semaphore_signal(barrier, inc=1, device_id=(f, m), device_id_type=MESH)


def standardize(values):
    centered = values - jnp.mean(values, axis=-1, keepdims=True)
    rstd = lax.rsqrt(jnp.mean(centered * centered, axis=-1, keepdims=True) + 1e-05)
    return centered * rstd, rstd


def dot_t(a, b):
    return lax.dot_general(a, b, (((1,), (1,)), ((), ())), preferred_element_type=F32)


def turned(a):
    return jnp.concatenate([a[:, :128].T, a[:, 128:].T], axis=1)


def attend(q, k, v, d, allowed, first):
    zero = jnp.zeros_like(k)
    k2 = jnp.concatenate([jnp.where(first, k, zero), jnp.where(first, zero, k)], axis=0)
    v2 = jnp.concatenate([jnp.where(first, v, zero), jnp.where(first, zero, v)], axis=0)
    scores = dot_t(q, k2) * FACTOR
    dprob = dot_t(d, v2)
    probs, dscore = [], []
    for h in range(2):
        s = jnp.where(allowed, scores[:, 128 * h : 128 * h + 128], NEG)
        e = jnp.exp(s - jnp.max(s, axis=-1, keepdims=True))
        p = e * (1.0 / jnp.sum(e, axis=-1, keepdims=True))
        dp = dprob[:, 128 * h : 128 * h + 128]
        delta = jnp.sum(p * dp, axis=-1, keepdims=True)
        probs.append(p.astype(BF))
        dscore.append((p * (dp - delta) * FACTOR).astype(BF))
    probs = jnp.concatenate(probs, axis=1)
    dscore = jnp.concatenate(dscore, axis=1)
    out = jnp.dot(probs, v2, preferred_element_type=F32)
    dq = jnp.dot(dscore, k2, preferred_element_type=F32)
    d2 = jnp.concatenate([jnp.where(first, d, zero), jnp.where(first, zero, d)], axis=0)
    q2 = jnp.concatenate([jnp.where(first, q, zero), jnp.where(first, zero, q)], axis=0)
    dv = jnp.dot(turned(probs), d2, preferred_element_type=F32)
    dk = jnp.dot(turned(dscore), q2, preferred_element_type=F32)
    return out, dq, dk, dv


def sublayer_kernel(
    tok, og, qkvw, outw, gain, perms,
    tgrad, gq, go, gg,
    order, xin, sbuf, recv, wown, wout, wt, ow, xs, normed, norm_t, og_t, proj, back, ao, part, other, rsib,
    tg, gacc, gvec, gvecr, gcol, sret, rret, blk, grads, gf, gn, ggr, gz, gzr, gzg, gzgr, gxs, gxr, gxg, gxgr,
    loc, ploc, kloc, wloc, oloc, zloc, gloc,
    asend, arecv, fsend, frecv, ssend, srecv, wsend, wrecv, bsend, brecv, vsend, vrecv,
    csend, crecv, psend, precv, rsend, rrecv, y1send, y1recv, y2send, y2recv, gsend, grecv,
    zsend, zrecv, xsend, xrecv, hsend, hrecv,
):
    f, m = lax.axis_index("frame"), lax.axis_index("mlp")
    g, c, z, x = f // 2, f % 2, m // 4, m % 4
    zh, y = f // 8, (f // 2) % 4
    zi = zh * 2 + z
    sib = g * 2 + 1 - c
    mz = (1 - z) * 4 + x
    xl, xr, xf = (x + 3) % 4, (x + 1) % 4, (x + 2) % 4
    mr, ml = z * 4 + xr, z * 4 + xl
    yl, yr, yf = (y + 3) % 4, (y + 1) % 4, (y + 2) % 4
    fr, fl = (zh * 4 + yr) * 2 + c, (zh * 4 + yl) * 2 + c
    own = c == z
    start = (zi + 5 + 3 * z) % 8
    me = (3 - 3 * z) * 4 + y

    def window(lo, h):
        return (zh + 3 - 2 * lo + h) % 4

    def owner(slot):
        to = (start + slot // 4) % 8
        return ((to // 2) * 4 + slot % 4) * 2 + c, (to % 2) * 4 + x

    def source(n):
        there = n // 4
        d = (there + 4 - zh) % 4
        lo = (d % 2) * (d // 2) + (1 - d % 2) * ((d // 2) * (1 - z) + (1 - d // 2) * z)
        place = (zi + 16 - (there * 2 + lo + 5 + 3 * lo)) % 8
        return n * 2 + c, lo * 4 + x, place * 4 + y

    p_in = [pltpu.make_async_copy(perms.at[pl.ds(0, 1)], order.at[pl.ds(0, 1)], ploc.at[0])]
    p_in.append(pltpu.make_async_copy(perms.at[pl.ds(1, 3)], order.at[pl.ds(1, 3)], ploc.at[1]))
    p_in[0].start()
    w_in = [pltpu.make_async_copy(qkvw.at[j], wown.at[:, pl.ds(128 * j, 128)], loc.at[j]) for j in range(3)]
    w_in.append(pltpu.make_async_copy(outw, ow, loc.at[3]))
    for copy in w_in:
        copy.start()
    x_in = []
    for ch in range(2):
        for t, ref in enumerate((tok, og)):
            for h in range(2):
                rows = pl.ds(pl.multiple_of(x * 64 + window(z, h) * 16, 16), 16)
                x_in.append(
                    pltpu.make_async_copy(
                        ref.at[pl.ds(6 * ch, 6), rows, :],
                        xin.at[ch, t, :, pl.ds(16 * h, 16), :],
                        loc.at[4 + 4 * ch + 2 * t + h],
                    )
                )
                x_in[-1].start()

    p_in[1].start()
    barrier = pltpu.get_barrier_semaphore()

    def hello_plane(k, _):
        n = (zi * 4 + y + k) % 32
        greet(barrier, ((n // 8) * 4 + n % 4) * 2 + c, ((n // 4) % 2) * 4 + x)
        return 0

    def hello_other(k, _):
        greet(barrier, ((k // 2) * 4 + y) * 2 + 1 - c, (k % 2) * 4 + x)
        return 0

    lax.fori_loop(1, 32, hello_plane, 0)
    lax.fori_loop(0, 8, hello_other, 0)
    for k in range(1, 4):
        greet(barrier, f, z * 4 + (x + k) % 4)

    for copy in w_in:
        copy.wait()
    wown[:, 384:512] = ow[...].T
    p_in[0].wait()

    def pack(ch):
        for copy in x_in[4 * ch : 4 * ch + 4]:
            copy.wait()
        for gh in range(2):
            rows = slice(16 * gh, 16 * gh + 16)
            parts = [xin[ch, t, :, rows, 512 * h : 512 * h + 512].reshape(96, 512) for h in range(2) for t in range(2)]
            packed = jnp.dot(order[0], jnp.concatenate(parts, axis=0), preferred_element_type=F32)
            sbuf[ch, 8 * gh : 8 * gh + 8] = packed.astype(BF).reshape(8, 48, 512)

    pack(0)
    pl.semaphore_wait(barrier, 42)

    half = (pl.ds(0, 512), pl.ds(512, 512))
    w_pairs = ((1, 0), (1, 1), (2, 1), (2, 0), (3, 0), (3, 1))

    def w_ring(src, slot, n, to):
        i, h = w_pairs[n]
        return remote(src, wout.at[slot, half[h]], wsend.at[n], wrecv.at[i, h], f, to)

    def w_spread(src, h):
        if h == 0:
            w_ring(src.at[half[0]], x, 0, mr).start()
            w_ring(src.at[half[0]], x, 3, ml).start()
        else:
            w_ring(src.at[half[1]], x, 2, ml).start()
            w_ring(src.at[half[1]], x, 1, mr).start()

    def swap(h):
        return remote(wown.at[half[h]], wout.at[x, half[h]], ssend.at[h], srecv.at[h], g * 2 + 1 - c, mz)

    own_w = pltpu.make_async_copy(wown, wout.at[x], wloc)

    @pl.when(own)
    def _():
        w_spread(wown, 0)
        w_spread(wown, 1)
        own_w.start()

    @pl.when(jnp.logical_not(own))
    def _():
        swap(0).start()
        swap(1).start()

    def a2a(ch, k):
        slot = (me + k) % 16
        return remote(sbuf.at[ch, slot], recv.at[ch, c, g], asend.at[ch, k], arecv.at[ch, g], *owner(slot))

    def forward(ch, k, src):
        slot = (g + 16 - k) % 16
        return remote(src, recv.at[ch, c, slot], fsend.at[ch, k], frecv.at[ch, k], sib, m)

    def keep(ch):
        return pltpu.make_async_copy(sbuf.at[ch, me], recv.at[ch, c, g], kloc.at[ch])

    for ch in range(2):
        if ch:
            pack(ch)

        def send(k, _, ch=ch):
            a2a(ch, k).start()
            return 0

        lax.fori_loop(1, 16, send, 0)
        keep(ch).start()
        forward(ch, 0, sbuf.at[ch, me]).start()

    @pl.when(jnp.logical_not(own))
    def _():
        swap(0).wait_recv()
        w_spread(wout.at[x], 0)
        swap(1).wait_recv()
        w_spread(wout.at[x], 1)

    def w_arrived(n):
        i, h = w_pairs[n]
        slot = (x, xl, xr, xf)[i]
        remote(wown.at[half[h]], wout.at[slot, half[h]], wsend.at[n], wrecv.at[i, h], f, mr).wait_recv()

    def relay_tokens(ch):
        def relay(k, _):
            slot = (g + 16 - k) % 16
            remote(sbuf.at[ch, 0], recv.at[ch, c, slot], asend.at[ch, k], arecv.at[ch, slot], f, m).wait_recv()
            forward(ch, k, recv.at[ch, c, slot]).start()
            return 0

        lax.fori_loop(1, 16, relay, 0)

    def tokens_arrived(ch):
        keep(ch).wait()

        def wait(k, _):
            slot = (g + 16 - k) % 16
            remote(sbuf.at[ch, 0], recv.at[ch, 1 - c, slot], fsend.at[ch, k], frecv.at[ch, k], f, m).wait_recv()
            return 0

        lax.fori_loop(0, 16, wait, 0)

    relay_tokens(0)
    w_arrived(0)
    w_ring(wout.at[xl, half[0]], xl, 4, mr).start()
    w_arrived(2)
    w_ring(wout.at[xr, half[1]], xr, 5, ml).start()

    lane = lax.broadcasted_iota(jnp.int32, (128, 128), 1)
    line = lax.broadcasted_iota(jnp.int32, (128, 128), 0)
    first = lane < 64
    allowed = (lane < 64) == (line < 64)

    def shard_of(i):
        return (x + (i % 2) * 3 + (i // 2) * (1 + (i % 2) * 2)) % 4

    def prepare(ch):
        for s in range(2):
            for gh in range(2):
                block = recv[ch, s, 8 * gh : 8 * gh + 8].reshape(384, 512)
                rows = jnp.dot(order[1], block, preferred_element_type=F32).astype(BF).reshape(2, 2, 6, 16, 512)
                for h in range(2):
                    xs[ch, :, :, s, 16 * gh : 16 * gh + 16, 512 * h : 512 * h + 512] = rows[h]

        def norm(u, _):
            xhat, _ = standardize(xs[ch, 0, u].reshape(64, D).astype(F32))
            normed[pl.ds(pl.multiple_of(ch * 384 + u * 64, 64), 64), :] = (xhat * gain[...]).astype(BF)
            return 0

        lax.fori_loop(0, 6, norm, 0)
        for i in range(3):
            at = 384 * ch + 128 * i
            norm_t[:, at : at + 128] = normed[at : at + 128, :].T
            og_t[:, at : at + 128] = xs[ch, 1, 2 * i : 2 * i + 2].reshape(128, D).T

    def heads(ch, i):
        j = shard_of(i)
        at = 384 * ch
        if ch == 0:
            wt[i] = wout[j, :, 0:384].T
        proj[:, 0:384] = jnp.dot(normed[at : at + 384, :], wout[j, :, 0:384], preferred_element_type=F32).astype(BF)
        proj[:, 384:512] = jnp.dot(
            xs[ch, 1].reshape(384, D), wout[j, :, 384:512], preferred_element_type=F32
        ).astype(BF)
        for n in range(3):
            rows = slice(128 * n, 128 * n + 128)
            out, dq, dk, dv = attend(
                proj[rows, 0:128], proj[rows, 128:256], proj[rows, 256:384], proj[rows, 384:512], allowed, first
            )
            rows = slice(at + 128 * n, at + 128 * n + 128)
            back[i, rows, 0:128] = dq.astype(BF)
            back[i, rows, 128:256] = dk.astype(BF)
            back[i, rows, 256:384] = dv.astype(BF)
            ao[i, rows, :] = out.astype(BF)

    def to_sibling(ch):
        return remote(other.at[ch], rsib.at[ch], bsend.at[ch], brecv.at[ch], sib, m)

    def partial(ch):
        for n in range(3):
            rows = slice(384 * ch + 128 * n, 384 * ch + 128 * n + 128)
            term = jnp.dot(back[0, rows, :], wt[0], preferred_element_type=F32)
            for i in range(1, 4):
                term += jnp.dot(back[i, rows, :], wt[i], preferred_element_type=F32)
            part[2 * n : 2 * n + 2] = term.reshape(2, 2, 32, D)
        other[ch] = part[:, 1 - c].astype(BF)
        to_sibling(ch).start()

    def back_to(ch, k):
        n = (g + k) % 16
        fs, ms, slot = source(n)
        return remote(sret.at[ch, n], rret.at[ch, slot], csend.at[ch, k], crecv.at[ch, slot], fs, ms)

    def keep_back(ch):
        return pltpu.make_async_copy(sret.at[ch, g], rret.at[ch, me], kloc.at[2 + ch])

    def token_gradient(ch):
        to_sibling(ch).wait_recv()

        def token(u, total):
            xhat, rstd = standardize(xs[ch, 0, u, c].astype(F32))
            dn = part[u, c] + rsib[ch, u].astype(F32)
            bp = dn * gain[...]
            inner = bp - jnp.mean(bp, axis=-1, keepdims=True) - xhat * jnp.mean(bp * xhat, axis=-1, keepdims=True)
            tg[u] = (xs[ch, 1, u, c].astype(F32) + rstd * inner).astype(BF)
            return total + jnp.sum((dn * xhat).reshape(4, 8, D), axis=0)

        total = lax.fori_loop(0, 6, token, jnp.zeros((8, D), F32))
        if ch == 0:
            gacc[...] = total
        else:
            gacc[...] += total
        for gh in range(2):
            rows = slice(16 * gh, 16 * gh + 16)
            parts = [tg[:, rows, 256 * h : 256 * h + 256].reshape(96, 256) for h in range(4)]
            packed = jnp.dot(order[2], jnp.concatenate(parts, axis=0), preferred_element_type=F32)
            sret[ch, 8 * gh : 8 * gh + 8] = packed.astype(BF).reshape(8, 48, 256)

        def send(k, _):
            back_to(ch, k).start()
            return 0

        lax.fori_loop(1, 16, send, 0)
        keep_back(ch).start()

    def piece(ch, h, mm):
        rows = pl.ds(pl.multiple_of((mm % 4) * 64 + window(mm // 4, h) * 16, 16), 16)
        return tgrad.at[pl.ds(6 * ch, 6), rows, :]

    def kept(ch, h):
        return blk.at[ch, :, pl.ds(16 * h, 16), :]

    def pair(ch, h):
        return remote(kept(ch, h), piece(ch, h, m), psend.at[ch, h], precv.at[ch, h], f, mz)

    def ring(ch, r, src, mm, h, n, to):
        return remote(src, piece(ch, h, mm), rsend.at[ch, r, n], rrecv.at[ch, r, n], f, to)

    def own_out(ch, h):
        return pltpu.make_async_copy(kept(ch, h), piece(ch, h, m), oloc.at[ch, h])

    def gather_own(ch):
        keep_back(ch).wait()

        def received(k, _):
            slot = (me + k) % 16
            remote(sret.at[ch, 0], rret.at[ch, slot], csend.at[ch, k], crecv.at[ch, slot], f, m).wait_recv()
            return 0

        lax.fori_loop(1, 16, received, 0)
        for gh in range(2):
            block = rret[ch, 8 * gh : 8 * gh + 8].reshape(384, 256)
            rows = jnp.dot(order[3], block, preferred_element_type=F32).astype(BF).reshape(4, 6, 16, 256)
            for h in range(4):
                blk[ch, :, 16 * gh : 16 * gh + 16, 256 * h : 256 * h + 256] = rows[h]
        pair(ch, 0).start()
        pair(ch, 1).start()
        ring(ch, 0, kept(ch, 0), m, 0, 0, mr).start()
        ring(ch, 0, kept(ch, 1), m, 1, 2, ml).start()
        ring(ch, 0, kept(ch, 1), m, 1, 1, mr).start()
        ring(ch, 0, kept(ch, 0), m, 0, 3, ml).start()
        own_out(ch, 0).start()
        own_out(ch, 1).start()

    def gather_pair(ch):
        def arrived(h):
            remote(kept(ch, h), piece(ch, h, mz), psend.at[ch, h], precv.at[ch, h], f, mz).wait_recv()

        arrived(0)
        ring(ch, 1, piece(ch, 0, mz), mz, 0, 0, mr).start()
        ring(ch, 1, piece(ch, 0, mz), mz, 0, 3, ml).start()
        arrived(1)
        ring(ch, 1, piece(ch, 1, mz), mz, 1, 2, ml).start()
        ring(ch, 1, piece(ch, 1, mz), mz, 1, 1, mr).start()

    def base(r):
        return (z if r == 0 else 1 - z) * 4

    def arrived(ch, r, mm, h, n):
        ring(ch, r, piece(ch, h, base(r) + mm), base(r) + mm, h, n, mr).wait_recv()

    def gather_relay(ch, r):
        arrived(ch, r, xl, 0, 0)
        ring(ch, r, piece(ch, 0, base(r) + xl), base(r) + xl, 0, 4, mr).start()
        arrived(ch, r, xr, 1, 2)
        ring(ch, r, piece(ch, 1, base(r) + xr), base(r) + xr, 1, 5, ml).start()

    def weights(i):
        j = shard_of(i)

        def block(a, _):
            rows = pl.ds(pl.multiple_of(a * 256, 256), 256)
            left = jnp.dot(norm_t[rows, :], back[i], preferred_element_type=F32).astype(BF)
            grads[j, a, :, :, :, 0:384] = left.reshape(4, 2, 32, 384)
            left = jnp.dot(og_t[rows, :], ao[i], preferred_element_type=F32).astype(BF)
            grads[j, a, :, :, :, 384:512] = left.reshape(4, 2, 32, 128)
            return 0

        lax.fori_loop(0, 4, block, 0)
        y_far(i, 0).start()
        y_far(i, 1).start()

    def y_far(i, h):
        src = grads.at[shard_of(i), pl.ds(2 * h, 2), yf]
        return remote(src, gf.at[i, h], y1send.at[i, h], y1recv.at[i, h], fr if h == 0 else fl, m)

    def y_near(i, h):
        src = grads.at[shard_of(i), :, yr if h == 0 else yl]
        return remote(src, gn.at[i, h], y2send.at[i, h], y2recv.at[i, h], fr if h == 0 else fl, m)

    def y_step(i, _):
        j = shard_of(i)
        for h in range(2):
            y_far(i, h).wait_recv()
            to = yr if h == 0 else yl
            for a in range(2):
                total = grads[j, 2 * h + a, to].astype(F32) + gf[i, h, a].astype(F32)
                grads[j, 2 * h + a, to] = total.astype(BF)
            y_near(i, h).start()
        return 0

    def z_copy(i, n):
        to = ((n // 2) * 4 + y) * 2 + n % 2
        return remote(gz.at[i, n], gzr.at[i, zi], zsend.at[i, n], zrecv.at[i, zi], to, c * 4 + x)

    def zg_copy(n):
        to = ((n // 2) * 4 + y) * 2 + n % 2
        return remote(gzg.at[n], gzgr.at[zi], zsend.at[4, n], zrecv.at[4, zi], to, c * 4 + x)

    def z_self(n):
        return jnp.logical_and(n == zh * 2 + c, own)

    def own_z(i):
        return pltpu.make_async_copy(gz.at[i, zh * 2 + c], gzr.at[i, zi], zloc.at[i])

    def own_zg():
        return pltpu.make_async_copy(gzg.at[zh * 2 + c], gzgr.at[zi], zloc.at[4])

    def z_step(i, _):
        j = shard_of(i)
        for h in range(2):
            y_near(i, h).wait_recv()
        for a in range(4):
            total = grads[j, a, y].astype(F32) + (gn[i, 0, a].astype(F32) + gn[i, 1, a].astype(F32))
            gz[i, 2 * a : 2 * a + 2] = total.astype(BF)

        def z_send(n, _):
            @pl.when(jnp.logical_not(z_self(n)))
            def _():
                z_copy(i, n).start()

            return 0

        lax.fori_loop(0, 8, z_send, 0)

        @pl.when(own)
        def _():
            own_z(i).start()

        return 0

    def z_wait(i, src, dst):
        def wait(n, _):
            @pl.when(jnp.logical_not(jnp.logical_and(n == zi, own)))
            def _():
                remote(src, dst(n), zsend.at[i, 0], zrecv.at[i, n], f, m).wait_recv()

            return 0

        lax.fori_loop(0, 8, wait, 0)

    def sum8(terms):
        while len(terms) > 1:
            terms = [a + b for a, b in zip(terms[::2], terms[1::2])]
        return terms[0]

    def x_copy(i):
        return remote(gxs.at[i], gxr.at[i], xsend.at[i], xrecv.at[i], f, z * 4 + shard_of(i))

    def x_step(i, _):
        z_wait(i, gz.at[0, 0], lambda n: gzr.at[i, n])

        @pl.when(own)
        def _():
            own_z(i).wait()

        gxs[i] = sum8([gzr[i, k].astype(F32) for k in range(8)]).astype(BF)

        @pl.when(i > 0)
        def _():
            x_copy(i).start()

        return 0

    def gain_y(k):
        yk = (y + k) % 4
        return remote(gcol.at[:, yk], ggr.at[k], gsend.at[k], grecv.at[k], (zh * 4 + yk) * 2 + c, m)

    own_gain = pltpu.make_async_copy(gcol.at[:, y], ggr.at[0], gloc)

    def gain_x(k):
        return remote(gxg, gxgr.at[k], hsend.at[k], hrecv.at[k], f, z * 4 + (x + k) % 4)

    to_sib_gain = remote(gvec, gvecr, vsend, vrecv, sib, m)

    def sent_early():
        for ch in range(2):
            pair(ch, 0).wait_send()
            pair(ch, 1).wait_send()
            own_out(ch, 0).wait()
            own_out(ch, 1).wait()
            to_sibling(ch).wait_send()

            def sent(k, _, ch=ch):
                a2a(ch, k).wait_send()
                back_to(ch, k).wait_send()
                forward(ch, k, recv.at[ch, c, (g + 16 - k) % 16]).wait_send()
                return 0

            lax.fori_loop(1, 16, sent, 0)
            forward(ch, 0, sbuf.at[ch, me]).wait_send()
        to_sib_gain.wait_send()
        for n in range(6):
            i, h = w_pairs[n]
            w_ring(wown.at[half[h]], x, n, mr).wait_send()

        @pl.when(jnp.logical_not(own))
        def _():
            swap(0).wait_send()
            swap(1).wait_send()

        for k in range(1, 4):
            gain_y(k).wait_send()

        def y_sent(i, _):
            for h in range(2):
                y_far(i, h).wait_send()
                y_near(i, h).wait_send()
            return 0

        lax.fori_loop(0, 4, y_sent, 0)

        def z_sent(n, _):
            @pl.when(jnp.logical_not(z_self(n)))
            def _():
                for i in range(4):
                    z_copy(i, n).wait_send()
                zg_copy(n).wait_send()

            return 0

        lax.fori_loop(0, 8, z_sent, 0)

    p_in[1].wait()
    tokens_arrived(0)
    prepare(0)

    @pl.when(own)
    def _():
        own_w.wait()

    def shard_arrived(i):
        for h in range(2):
            waited = jnp.logical_or(i == 0, jnp.logical_and(i < 3, h == i - 1))

            @pl.when(jnp.logical_not(waited))
            def _():
                slot = shard_of(i)
                remote(wown.at[half[h]], wout.at[slot, half[h]], wsend.at[0], wrecv.at[i, h], f, mr).wait_recv()

    def first_heads(i, _):
        shard_arrived(i)
        heads(0, i)

        @pl.when(i == 2)
        def _():
            relay_tokens(1)
            tokens_arrived(1)
            prepare(1)
            heads(1, 0)

        return 0

    def second_heads(i, _):
        heads(1, i)

        @pl.when(i == 1)
        def _():
            token_gradient(0)

        return 0

    def all_weights(i, _):
        weights(i)
        return 0

    lax.fori_loop(0, 4, first_heads, 0)
    partial(0)
    lax.fori_loop(1, 4, second_heads, 0)
    lax.fori_loop(0, 1, all_weights, 0)
    gather_own(0)
    lax.fori_loop(1, 4, all_weights, 0)
    partial(1)
    y_step(0, 0)
    gather_pair(0)
    token_gradient(1)
    gvec[...] = jnp.broadcast_to(jnp.sum(gacc[...], axis=0, keepdims=True), (8, D))
    to_sib_gain.start()
    lax.fori_loop(1, 3, y_step, 0)
    gather_relay(0, 0)
    y_step(3, 0)
    to_sib_gain.wait_recv()
    gcol[...] = jnp.broadcast_to(gvec[0:1] + gvecr[0:1], (128, D)).T.astype(BF).reshape(4, 4, 2, 32, 128)
    for k in range(1, 4):
        gain_y(k).start()
    own_gain.start()
    gather_own(1)
    z_step(0, 0)
    gather_relay(0, 1)
    z_step(1, 0)
    gather_pair(1)
    z_step(2, 0)
    gather_relay(1, 0)
    z_step(3, 0)

    own_gain.wait()
    for k in range(1, 4):
        remote(ggr.at[0], ggr.at[k], gsend.at[k], grecv.at[k], f, m).wait_recv()
    total = sum8([ggr[k].astype(F32) for k in range(4)])
    gzg[...] = total.astype(BF).reshape(8, 32, 128)

    def zg_send(n, _):
        @pl.when(jnp.logical_not(z_self(n)))
        def _():
            zg_copy(n).start()

        return 0

    lax.fori_loop(0, 8, zg_send, 0)

    @pl.when(own)
    def _():
        own_zg().start()

    lax.fori_loop(0, 4, x_step, 0)
    z_wait(4, gzg.at[0], lambda n: gzgr.at[n])

    @pl.when(own)
    def _():
        own_zg().wait()

    gxg[...] = sum8([gzgr[k].astype(F32) for k in range(8)]).astype(BF)
    for k in range(1, 4):
        gain_x(k).start()
    sent_early()
    gather_relay(1, 1)

    for i in range(1, 4):
        x_copy(i).wait_recv()
    total = sum8([gxs[0].astype(F32)] + [gxr[i].astype(F32) for i in range(1, 4)])
    for j in range(3):
        gq[j] = total[:, 128 * j : 128 * j + 128]
    go[...] = total[:, 384:512]
    for k in range(1, 4):
        gain_x(k).wait_recv()
    total = sum8([gxg[...].astype(F32)] + [gxgr[k].astype(F32) for k in range(1, 4)])
    gg[...] = jnp.broadcast_to(total[0:32, 0:1], (32, 128))

    for ch in range(2):
        for r in range(2):
            arrived(ch, r, xl, 1, 1)
            arrived(ch, r, xr, 0, 3)
            arrived(ch, r, xf, 0, 4)
            arrived(ch, r, xf, 1, 5)
            for n, (mm, h) in enumerate(((x, 0), (x, 1), (x, 1), (x, 0), (xl, 0), (xr, 1))):
                ring(ch, r, piece(ch, h, base(r) + mm), base(r) + mm, h, n, mr).wait_send()
    for k in range(1, 4):
        gain_x(k).wait_send()
        x_copy(k).wait_send()


def sublayer(tok, og, qkvw, outw, gain):
    vm = pl.BlockSpec(memory_space=pltpu.VMEM)
    hbm = pl.BlockSpec(memory_space=pltpu.HBM)
    dma = pltpu.SemaphoreType.DMA
    perms = jnp.asarray(np.stack([PACK, GROUP, REPACK, UNPACK]), BF)
    bf = lambda *shape: pltpu.VMEM(shape, BF)
    return pl.pallas_call(
        sublayer_kernel,
        out_shape=(
            jax.ShapeDtypeStruct((12, 256, D), BF),
            jax.ShapeDtypeStruct((3, 32, 128), F32),
            jax.ShapeDtypeStruct((32, 128), F32),
            jax.ShapeDtypeStruct((32, 128), F32),
        ),
        in_specs=[hbm] * 4 + [vm, hbm],
        out_specs=(hbm, vm, vm, vm),
        scratch_shapes=[
            bf(4, 384, 384),
            bf(2, 2, 6, 32, D),
            bf(2, 16, 48, 512),
            bf(2, 2, 16, 48, 512),
            bf(D, 512),
            bf(4, D, 512),
            bf(4, 384, D),
            bf(128, D),
            bf(2, 2, 6, 2, 32, D),
            bf(768, D),
            bf(D, 768),
            bf(D, 768),
            bf(384, 512),
            bf(4, 768, 384),
            bf(4, 768, 128),
            pltpu.VMEM((6, 2, 32, D), F32),
            bf(2, 6, 32, D),
            bf(2, 6, 32, D),
            bf(6, 32, D),
            pltpu.VMEM((8, D), F32),
            pltpu.VMEM((8, D), F32),
            pltpu.VMEM((8, D), F32),
            bf(4, 4, 2, 32, 128),
            bf(2, 16, 48, 256),
            bf(2, 16, 48, 256),
            bf(2, 6, 32, D),
            bf(4, 4, 4, 2, 32, 512),
            bf(4, 2, 2, 2, 32, 512),
            bf(4, 2, 4, 2, 32, 512),
            bf(4, 4, 2, 32, 128),
            bf(4, 8, 32, 512),
            bf(4, 8, 32, 512),
            bf(8, 32, 128),
            bf(8, 32, 128),
            bf(4, 32, 512),
            bf(4, 32, 512),
            bf(32, 128),
            bf(4, 32, 128),
            dma((12,)),
            dma((2,)),
            dma((4,)),
            dma,
            dma((2, 2)),
            dma((5,)),
            dma,
            dma((2, 16)),
            dma((2, 16)),
            dma((2, 16)),
            dma((2, 16)),
            dma((2,)),
            dma((2,)),
            dma((6,)),
            dma((4, 2)),
            dma((2,)),
            dma((2,)),
            dma,
            dma,
            dma((2, 16)),
            dma((2, 16)),
            dma((2, 2)),
            dma((2, 2)),
            dma((2, 2, 6)),
            dma((2, 2, 6)),
            dma((4, 2)),
            dma((4, 2)),
            dma((4, 2)),
            dma((4, 2)),
            dma((4,)),
            dma((4,)),
            dma((5, 8)),
            dma((5, 8)),
            dma((4,)),
            dma((4,)),
            dma((4,)),
            dma((4,)),
        ],
        compiler_params=pltpu.CompilerParams(
            collective_id=0, has_side_effects=True, vmem_limit_bytes=58 * 2**20
        ),
        name="sublayer",
    )(tok, og, qkvw, outw, gain, perms)


def shards(tokens, output_gradient, gain, qkv_weight, out_weight):
    clips, frames, patches, width = tokens.shape
    tgrad, gq, go, gg = sublayer(
        tokens.reshape(12, 256, D),
        output_gradient.reshape(12, 256, D),
        jnp.transpose(qkv_weight, (1, 0, 2)),
        out_weight,
        gain.reshape(1, D),
    )
    return (
        tgrad.reshape(clips, frames, patches, width),
        jnp.transpose(gq, (1, 0, 2)),
        go.T,
        gg[:, 0],
    )


def solution(mesh):
    in_specs = (
        P(None, "frame", None, None),
        P(None, "frame", None, None),
        P(),
        P(None, None, "mlp"),
        P("mlp", None),
    )
    out_specs = (
        P(None, "frame", None, None),
        P("frame", None, "mlp"),
        P("mlp", "frame"),
        P("frame"),
    )
    return jax.shard_map(shards, mesh=mesh, in_specs=in_specs, out_specs=out_specs, check_vma=False)
```

```python
import numpy as np

import jax
import jax.numpy as jnp
from jax import lax
from jax.experimental import pallas as pl
from jax.experimental.pallas import tpu as pltpu
from jax.sharding import PartitionSpec as P

MESH = pl.DeviceIdType.MESH
BF = jnp.bfloat16
F32 = jnp.float32
D = 1024
FACTOR = 64 ** (-0.5)
NEG = -1e30


def one_hot(shape, perm):
    index = np.arange(384).reshape(shape).transpose(perm).reshape(-1)
    return np.eye(384, dtype=np.float32)[index]


PACK = one_hot((2, 2, 6, 8, 2), (3, 0, 1, 4, 2))
GROUP = one_hot((8, 2, 2, 6, 2), (1, 2, 3, 0, 4))
REPACK = one_hot((4, 6, 8, 2), (2, 0, 1, 3))
UNPACK = one_hot((8, 4, 2, 6), (1, 3, 0, 2))


def remote(src, dst, send, recv, f, m):
    return pltpu.make_async_remote_copy(
        src_ref=src, dst_ref=dst, send_sem=send, recv_sem=recv, device_id=(f, m), device_id_type=MESH
    )


def greet(barrier, f, m):
    pl.semaphore_signal(barrier, inc=1, device_id=(f, m), device_id_type=MESH)


def standardize(values):
    centered = values - jnp.mean(values, axis=-1, keepdims=True)
    rstd = lax.rsqrt(jnp.mean(centered * centered, axis=-1, keepdims=True) + 1e-05)
    return centered * rstd, rstd


def dot_t(a, b):
    return lax.dot_general(a, b, (((1,), (1,)), ((), ())), preferred_element_type=F32)


def turned(a):
    return jnp.concatenate([a[:, :128].T, a[:, 128:].T], axis=1)


def attend(q, k, v, d, allowed, first):
    zero = jnp.zeros_like(k)
    k2 = jnp.concatenate([jnp.where(first, k, zero), jnp.where(first, zero, k)], axis=0)
    v2 = jnp.concatenate([jnp.where(first, v, zero), jnp.where(first, zero, v)], axis=0)
    scores = dot_t(q, k2) * FACTOR
    dprob = dot_t(d, v2)
    probs, dscore = [], []
    for h in range(2):
        s = jnp.where(allowed, scores[:, 128 * h : 128 * h + 128], NEG)
        e = jnp.exp(s - jnp.max(s, axis=-1, keepdims=True))
        p = e * (1.0 / jnp.sum(e, axis=-1, keepdims=True))
        dp = dprob[:, 128 * h : 128 * h + 128]
        delta = jnp.sum(p * dp, axis=-1, keepdims=True)
        probs.append(p.astype(BF))
        dscore.append((p * (dp - delta) * FACTOR).astype(BF))
    probs = jnp.concatenate(probs, axis=1)
    dscore = jnp.concatenate(dscore, axis=1)
    out = jnp.dot(probs, v2, preferred_element_type=F32)
    dq = jnp.dot(dscore, k2, preferred_element_type=F32)
    d2 = jnp.concatenate([jnp.where(first, d, zero), jnp.where(first, zero, d)], axis=0)
    q2 = jnp.concatenate([jnp.where(first, q, zero), jnp.where(first, zero, q)], axis=0)
    dv = jnp.dot(turned(probs), d2, preferred_element_type=F32)
    dk = jnp.dot(turned(dscore), q2, preferred_element_type=F32)
    return out, dq, dk, dv


def sublayer_kernel(
    tok, og, qkvw, outw, gain, perms,
    tgrad, gq, go, gg,
    order, xin, sbuf, recv, wown, wout, wt, ow, xs, normed, norm_t, og_t, proj, back, ao, part, other, rsib,
    tg, gacc, gvec, gvecr, gcol, sret, rret, blk, grads, gf, gn, ggr, gz, gzr, gzg, gzgr, gxs, gxr, gxg, gxgr,
    loc, ploc, kloc, wloc, oloc, zloc, gloc,
    asend, arecv, fsend, frecv, ssend, srecv, qsend, qrecv, usend, urecv, wsend, wrecv, bsend, brecv, vsend, vrecv,
    csend, crecv, psend, precv, rsend, rrecv, y1send, y1recv, y2send, y2recv, gsend, grecv,
    zsend, zrecv, xsend, xrecv, hsend, hrecv,
):
    f, m = lax.axis_index("frame"), lax.axis_index("mlp")
    g, c, z, x = f // 2, f % 2, m // 4, m % 4
    zh, y = f // 8, (f // 2) % 4
    zi = zh * 2 + z
    sib = g * 2 + 1 - c
    mz = (1 - z) * 4 + x
    xl, xr, xf = (x + 3) % 4, (x + 1) % 4, (x + 2) % 4
    mr, ml = z * 4 + xr, z * 4 + xl
    yl, yr, yf = (y + 3) % 4, (y + 1) % 4, (y + 2) % 4
    fr, fl = (zh * 4 + yr) * 2 + c, (zh * 4 + yl) * 2 + c
    own = c == z
    start = (zi + 5 + 3 * z) % 8
    me = (3 - 3 * z) * 4 + y

    def window(lo, h):
        return (zh + 3 - 2 * lo + h) % 4

    def owner(slot):
        to = (start + slot // 4) % 8
        return ((to // 2) * 4 + slot % 4) * 2 + c, (to % 2) * 4 + x

    def source(n):
        there = n // 4
        d = (there + 4 - zh) % 4
        lo = (d % 2) * (d // 2) + (1 - d % 2) * ((d // 2) * (1 - z) + (1 - d // 2) * z)
        place = (zi + 16 - (there * 2 + lo + 5 + 3 * lo)) % 8
        return n * 2 + c, lo * 4 + x, place * 4 + y

    p_in = [pltpu.make_async_copy(perms.at[pl.ds(0, 1)], order.at[pl.ds(0, 1)], ploc.at[0])]
    p_in.append(pltpu.make_async_copy(perms.at[pl.ds(1, 3)], order.at[pl.ds(1, 3)], ploc.at[1]))
    p_in[0].start()
    w_in = [pltpu.make_async_copy(qkvw.at[j], wown.at[:, pl.ds(128 * j, 128)], loc.at[j]) for j in range(3)]
    w_in.append(pltpu.make_async_copy(outw, ow, loc.at[3]))
    for copy in w_in:
        copy.start()
    x_in = []
    for ch in range(2):
        for t, ref in enumerate((tok, og)):
            for h in range(2):
                rows = pl.ds(pl.multiple_of(x * 64 + window(z, h) * 16, 16), 16)
                x_in.append(
                    pltpu.make_async_copy(
                        ref.at[pl.ds(6 * ch, 6), rows, :],
                        xin.at[ch, t, :, pl.ds(16 * h, 16), :],
                        loc.at[4 + 4 * ch + 2 * t + h],
                    )
                )
                x_in[-1].start()

    p_in[1].start()
    barrier = pltpu.get_barrier_semaphore()

    def hello_plane(k, _):
        n = (zi * 4 + y + k) % 32
        greet(barrier, ((n // 8) * 4 + n % 4) * 2 + c, ((n // 4) % 2) * 4 + x)
        return 0

    def hello_other(k, _):
        greet(barrier, ((k // 2) * 4 + y) * 2 + 1 - c, (k % 2) * 4 + x)
        return 0

    lax.fori_loop(1, 32, hello_plane, 0)
    lax.fori_loop(0, 8, hello_other, 0)
    for k in range(1, 4):
        greet(barrier, f, z * 4 + (x + k) % 4)

    for copy in w_in:
        copy.wait()
    wown[:, 384:512] = ow[...].T
    p_in[0].wait()

    def pack(ch):
        for copy in x_in[4 * ch : 4 * ch + 4]:
            copy.wait()
        for gh in range(2):
            rows = slice(16 * gh, 16 * gh + 16)
            parts = [xin[ch, t, :, rows, 512 * h : 512 * h + 512].reshape(96, 512) for h in range(2) for t in range(2)]
            packed = jnp.dot(order[0], jnp.concatenate(parts, axis=0), preferred_element_type=F32)
            sbuf[ch, 8 * gh : 8 * gh + 8] = packed.astype(BF).reshape(8, 48, 512)

    pack(0)
    pl.semaphore_wait(barrier, 42)

    half = (pl.ds(0, 384), pl.ds(384, 384))
    strip = pl.ds(pl.multiple_of(768 + 64 * y, 64), 64)
    w_pairs = ((1, 0), (1, 1), (2, 1), (2, 0), (3, 0), (3, 1))

    def w_ring(src, slot, n, to):
        i, h = w_pairs[n]
        return remote(src, wout.at[slot, half[h]], wsend.at[n], wrecv.at[i, h], f, to)

    def w_spread(src, h):
        if h == 0:
            w_ring(src.at[half[0]], x, 0, mr).start()
            w_ring(src.at[half[0]], x, 3, ml).start()
        else:
            w_ring(src.at[half[1]], x, 2, ml).start()
            w_ring(src.at[half[1]], x, 1, mr).start()

    def swap(h):
        rows = (half[0], half[1], strip)[h]
        return remote(wown.at[rows], wout.at[x, rows], ssend.at[h], srecv.at[h], g * 2 + 1 - c, mz)

    def strip_x(src, k):
        return remote(src.at[strip], wout.at[x, strip], qsend.at[k], qrecv.at[k], f, z * 4 + (x + k) % 4)

    def strip_y(k):
        to = (zh * 4 + (y + k) % 4) * 2 + c
        return remote(wout.at[:, strip], wout.at[:, strip], usend.at[k], urecv.at[k], to, m)

    own_w = [
        pltpu.make_async_copy(wown.at[pl.ds(0, 768)], wout.at[x, pl.ds(0, 768)], wloc.at[0]),
        pltpu.make_async_copy(wown.at[strip], wout.at[x, strip], wloc.at[1]),
    ]

    @pl.when(own)
    def _():
        own_w[1].start()
        for k in range(1, 4):
            strip_x(wown, k).start()
        w_spread(wown, 0)
        w_spread(wown, 1)
        own_w[0].start()

    @pl.when(jnp.logical_not(own))
    def _():
        swap(2).start()
        swap(0).start()
        swap(1).start()

    def a2a(ch, k):
        slot = (me + k) % 16
        return remote(sbuf.at[ch, slot], recv.at[ch, c, g], asend.at[ch, k], arecv.at[ch, g], *owner(slot))

    def forward(ch, k, src):
        slot = (g + 16 - k) % 16
        return remote(src, recv.at[ch, c, slot], fsend.at[ch, k], frecv.at[ch, k], sib, m)

    def keep(ch):
        return pltpu.make_async_copy(sbuf.at[ch, me], recv.at[ch, c, g], kloc.at[ch])

    for ch in range(2):
        if ch:
            pack(ch)

        def send(k, _, ch=ch):
            a2a(ch, k).start()
            return 0

        lax.fori_loop(1, 16, send, 0)
        keep(ch).start()
        forward(ch, 0, sbuf.at[ch, me]).start()

        if ch == 0:

            @pl.when(jnp.logical_not(own))
            def _():
                swap(2).wait_recv()
                for k in range(1, 4):
                    strip_x(wout.at[x], k).start()

    @pl.when(own)
    def _():
        own_w[1].wait()

    for k in range(1, 4):
        remote(wown.at[strip], wout.at[(x + 4 - k) % 4, strip], qsend.at[k], qrecv.at[k], f, m).wait_recv()
    for k in range(1, 4):
        strip_y(k).start()

    @pl.when(jnp.logical_not(own))
    def _():
        swap(0).wait_recv()
        w_spread(wout.at[x], 0)
        swap(1).wait_recv()
        w_spread(wout.at[x], 1)

    def w_arrived(n):
        i, h = w_pairs[n]
        slot = (x, xl, xr, xf)[i]
        remote(wown.at[half[h]], wout.at[slot, half[h]], wsend.at[n], wrecv.at[i, h], f, mr).wait_recv()

    def relay_tokens(ch):
        def relay(k, _):
            slot = (g + 16 - k) % 16
            remote(sbuf.at[ch, 0], recv.at[ch, c, slot], asend.at[ch, k], arecv.at[ch, slot], f, m).wait_recv()
            forward(ch, k, recv.at[ch, c, slot]).start()
            return 0

        lax.fori_loop(1, 16, relay, 0)

    def tokens_arrived(ch):
        keep(ch).wait()

        def wait(k, _):
            slot = (g + 16 - k) % 16
            remote(sbuf.at[ch, 0], recv.at[ch, 1 - c, slot], fsend.at[ch, k], frecv.at[ch, k], f, m).wait_recv()
            return 0

        lax.fori_loop(0, 16, wait, 0)

    relay_tokens(0)
    w_arrived(0)
    w_ring(wout.at[xl, half[0]], xl, 4, mr).start()
    w_arrived(2)
    w_ring(wout.at[xr, half[1]], xr, 5, ml).start()

    lane = lax.broadcasted_iota(jnp.int32, (128, 128), 1)
    line = lax.broadcasted_iota(jnp.int32, (128, 128), 0)
    first = lane < 64
    allowed = (lane < 64) == (line < 64)

    def shard_of(i):
        return (x + (i % 2) * 3 + (i // 2) * (1 + (i % 2) * 2)) % 4

    def prepare(ch):
        for s in range(2):
            for gh in range(2):
                block = recv[ch, s, 8 * gh : 8 * gh + 8].reshape(384, 512)
                rows = jnp.dot(order[1], block, preferred_element_type=F32).astype(BF).reshape(2, 2, 6, 16, 512)
                for h in range(2):
                    xs[ch, :, :, s, 16 * gh : 16 * gh + 16, 512 * h : 512 * h + 512] = rows[h]

        def norm(u, _):
            xhat, _ = standardize(xs[ch, 0, u].reshape(64, D).astype(F32))
            normed[pl.ds(pl.multiple_of(ch * 384 + u * 64, 64), 64), :] = (xhat * gain[...]).astype(BF)
            return 0

        lax.fori_loop(0, 6, norm, 0)
        for i in range(3):
            at = 384 * ch + 128 * i
            norm_t[:, at : at + 128] = normed[at : at + 128, :].T
            og_t[:, at : at + 128] = xs[ch, 1, 2 * i : 2 * i + 2].reshape(128, D).T

    def heads(ch, i):
        j = shard_of(i)
        at = 384 * ch
        if ch == 0:
            wt[i] = wout[j, :, 0:384].T
        proj[:, 0:384] = jnp.dot(normed[at : at + 384, :], wout[j, :, 0:384], preferred_element_type=F32).astype(BF)
        proj[:, 384:512] = jnp.dot(
            xs[ch, 1].reshape(384, D), wout[j, :, 384:512], preferred_element_type=F32
        ).astype(BF)
        for n in range(3):
            rows = slice(128 * n, 128 * n + 128)
            out, dq, dk, dv = attend(
                proj[rows, 0:128], proj[rows, 128:256], proj[rows, 256:384], proj[rows, 384:512], allowed, first
            )
            rows = slice(at + 128 * n, at + 128 * n + 128)
            back[i, rows, 0:128] = dq.astype(BF)
            back[i, rows, 128:256] = dk.astype(BF)
            back[i, rows, 256:384] = dv.astype(BF)
            ao[i, rows, :] = out.astype(BF)

    def to_sibling(ch):
        return remote(other.at[ch], rsib.at[ch], bsend.at[ch], brecv.at[ch], sib, m)

    def partial(ch):
        for n in range(3):
            rows = slice(384 * ch + 128 * n, 384 * ch + 128 * n + 128)
            term = jnp.dot(back[0, rows, :], wt[0], preferred_element_type=F32)
            for i in range(1, 4):
                term += jnp.dot(back[i, rows, :], wt[i], preferred_element_type=F32)
            part[2 * n : 2 * n + 2] = term.reshape(2, 2, 32, D)
        other[ch] = part[:, 1 - c].astype(BF)
        to_sibling(ch).start()

    def back_to(ch, k):
        n = (g + k) % 16
        fs, ms, slot = source(n)
        return remote(sret.at[ch, n], rret.at[ch, slot], csend.at[ch, k], crecv.at[ch, slot], fs, ms)

    def keep_back(ch):
        return pltpu.make_async_copy(sret.at[ch, g], rret.at[ch, me], kloc.at[2 + ch])

    def token_gradient(ch):
        to_sibling(ch).wait_recv()

        def token(u, total):
            xhat, rstd = standardize(xs[ch, 0, u, c].astype(F32))
            dn = part[u, c] + rsib[ch, u].astype(F32)
            bp = dn * gain[...]
            inner = bp - jnp.mean(bp, axis=-1, keepdims=True) - xhat * jnp.mean(bp * xhat, axis=-1, keepdims=True)
            tg[u] = (xs[ch, 1, u, c].astype(F32) + rstd * inner).astype(BF)
            return total + jnp.sum((dn * xhat).reshape(4, 8, D), axis=0)

        total = lax.fori_loop(0, 6, token, jnp.zeros((8, D), F32))
        if ch == 0:
            gacc[...] = total
        else:
            gacc[...] += total
        for gh in range(2):
            rows = slice(16 * gh, 16 * gh + 16)
            parts = [tg[:, rows, 256 * h : 256 * h + 256].reshape(96, 256) for h in range(4)]
            packed = jnp.dot(order[2], jnp.concatenate(parts, axis=0), preferred_element_type=F32)
            sret[ch, 8 * gh : 8 * gh + 8] = packed.astype(BF).reshape(8, 48, 256)

        def send(k, _):
            back_to(ch, k).start()
            return 0

        lax.fori_loop(1, 16, send, 0)
        keep_back(ch).start()

    def piece(ch, h, mm):
        rows = pl.ds(pl.multiple_of((mm % 4) * 64 + window(mm // 4, h) * 16, 16), 16)
        return tgrad.at[pl.ds(6 * ch, 6), rows, :]

    def kept(ch, h):
        return blk.at[ch, :, pl.ds(16 * h, 16), :]

    def pair(ch, h):
        return remote(kept(ch, h), piece(ch, h, m), psend.at[ch, h], precv.at[ch, h], f, mz)

    def ring(ch, r, src, mm, h, n, to):
        return remote(src, piece(ch, h, mm), rsend.at[ch, r, n], rrecv.at[ch, r, n], f, to)

    def own_out(ch, h):
        return pltpu.make_async_copy(kept(ch, h), piece(ch, h, m), oloc.at[ch, h])

    def gather_own(ch):
        keep_back(ch).wait()

        def received(k, _):
            slot = (me + k) % 16
            remote(sret.at[ch, 0], rret.at[ch, slot], csend.at[ch, k], crecv.at[ch, slot], f, m).wait_recv()
            return 0

        lax.fori_loop(1, 16, received, 0)
        for gh in range(2):
            block = rret[ch, 8 * gh : 8 * gh + 8].reshape(384, 256)
            rows = jnp.dot(order[3], block, preferred_element_type=F32).astype(BF).reshape(4, 6, 16, 256)
            for h in range(4):
                blk[ch, :, 16 * gh : 16 * gh + 16, 256 * h : 256 * h + 256] = rows[h]
        pair(ch, 0).start()
        pair(ch, 1).start()
        ring(ch, 0, kept(ch, 0), m, 0, 0, mr).start()
        ring(ch, 0, kept(ch, 1), m, 1, 2, ml).start()
        ring(ch, 0, kept(ch, 1), m, 1, 1, mr).start()
        ring(ch, 0, kept(ch, 0), m, 0, 3, ml).start()
        own_out(ch, 0).start()
        own_out(ch, 1).start()

    def gather_pair(ch):
        def arrived(h):
            remote(kept(ch, h), piece(ch, h, mz), psend.at[ch, h], precv.at[ch, h], f, mz).wait_recv()

        arrived(0)
        ring(ch, 1, piece(ch, 0, mz), mz, 0, 0, mr).start()
        ring(ch, 1, piece(ch, 0, mz), mz, 0, 3, ml).start()
        arrived(1)
        ring(ch, 1, piece(ch, 1, mz), mz, 1, 2, ml).start()
        ring(ch, 1, piece(ch, 1, mz), mz, 1, 1, mr).start()

    def base(r):
        return (z if r == 0 else 1 - z) * 4

    def arrived(ch, r, mm, h, n):
        ring(ch, r, piece(ch, h, base(r) + mm), base(r) + mm, h, n, mr).wait_recv()

    def gather_relay(ch, r):
        arrived(ch, r, xl, 0, 0)
        ring(ch, r, piece(ch, 0, base(r) + xl), base(r) + xl, 0, 4, mr).start()
        arrived(ch, r, xr, 1, 2)
        ring(ch, r, piece(ch, 1, base(r) + xr), base(r) + xr, 1, 5, ml).start()

    def weights(i):
        j = shard_of(i)

        def block(a, _):
            rows = pl.ds(pl.multiple_of(a * 256, 256), 256)
            left = jnp.dot(norm_t[rows, :], back[i], preferred_element_type=F32).astype(BF)
            grads[j, a, :, :, :, 0:384] = left.reshape(4, 2, 32, 384)
            left = jnp.dot(og_t[rows, :], ao[i], preferred_element_type=F32).astype(BF)
            grads[j, a, :, :, :, 384:512] = left.reshape(4, 2, 32, 128)
            return 0

        lax.fori_loop(0, 4, block, 0)
        y_far(i, 0).start()
        y_far(i, 1).start()

    def y_far(i, h):
        src = grads.at[shard_of(i), pl.ds(2 * h, 2), yf]
        return remote(src, gf.at[i, h], y1send.at[i, h], y1recv.at[i, h], fr if h == 0 else fl, m)

    def y_near(i, h):
        src = grads.at[shard_of(i), :, yr if h == 0 else yl]
        return remote(src, gn.at[i, h], y2send.at[i, h], y2recv.at[i, h], fr if h == 0 else fl, m)

    def y_step(i, _):
        j = shard_of(i)
        for h in range(2):
            y_far(i, h).wait_recv()
            to = yr if h == 0 else yl
            for a in range(2):
                total = grads[j, 2 * h + a, to].astype(F32) + gf[i, h, a].astype(F32)
                grads[j, 2 * h + a, to] = total.astype(BF)
            y_near(i, h).start()
        return 0

    def z_copy(i, n):
        to = ((n // 2) * 4 + y) * 2 + n % 2
        return remote(gz.at[i, n], gzr.at[i, zi], zsend.at[i, n], zrecv.at[i, zi], to, c * 4 + x)

    def zg_copy(n):
        to = ((n // 2) * 4 + y) * 2 + n % 2
        return remote(gzg.at[n], gzgr.at[zi], zsend.at[4, n], zrecv.at[4, zi], to, c * 4 + x)

    def z_self(n):
        return jnp.logical_and(n == zh * 2 + c, own)

    def own_z(i):
        return pltpu.make_async_copy(gz.at[i, zh * 2 + c], gzr.at[i, zi], zloc.at[i])

    def own_zg():
        return pltpu.make_async_copy(gzg.at[zh * 2 + c], gzgr.at[zi], zloc.at[4])

    def z_step(i, _):
        j = shard_of(i)
        for h in range(2):
            y_near(i, h).wait_recv()
        for a in range(4):
            total = grads[j, a, y].astype(F32) + (gn[i, 0, a].astype(F32) + gn[i, 1, a].astype(F32))
            gz[i, 2 * a : 2 * a + 2] = total.astype(BF)

        def z_send(n, _):
            @pl.when(jnp.logical_not(z_self(n)))
            def _():
                z_copy(i, n).start()

            return 0

        lax.fori_loop(0, 8, z_send, 0)

        @pl.when(own)
        def _():
            own_z(i).start()

        return 0

    def z_wait(i, src, dst):
        def wait(n, _):
            @pl.when(jnp.logical_not(jnp.logical_and(n == zi, own)))
            def _():
                remote(src, dst(n), zsend.at[i, 0], zrecv.at[i, n], f, m).wait_recv()

            return 0

        lax.fori_loop(0, 8, wait, 0)

    def sum8(terms):
        while len(terms) > 1:
            terms = [a + b for a, b in zip(terms[::2], terms[1::2])]
        return terms[0]

    def x_copy(i):
        return remote(gxs.at[i], gxr.at[i], xsend.at[i], xrecv.at[i], f, z * 4 + shard_of(i))

    def x_step(i, _):
        z_wait(i, gz.at[0, 0], lambda n: gzr.at[i, n])

        @pl.when(own)
        def _():
            own_z(i).wait()

        gxs[i] = sum8([gzr[i, k].astype(F32) for k in range(8)]).astype(BF)

        @pl.when(i > 0)
        def _():
            x_copy(i).start()

        return 0

    def gain_y(k):
        yk = (y + k) % 4
        return remote(gcol.at[:, yk], ggr.at[k], gsend.at[k], grecv.at[k], (zh * 4 + yk) * 2 + c, m)

    own_gain = pltpu.make_async_copy(gcol.at[:, y], ggr.at[0], gloc)

    def gain_x(k):
        return remote(gxg, gxgr.at[k], hsend.at[k], hrecv.at[k], f, z * 4 + (x + k) % 4)

    to_sib_gain = remote(gvec, gvecr, vsend, vrecv, sib, m)

    def sent_early():
        for ch in range(2):
            pair(ch, 0).wait_send()
            pair(ch, 1).wait_send()
            own_out(ch, 0).wait()
            own_out(ch, 1).wait()
            to_sibling(ch).wait_send()

            def sent(k, _, ch=ch):
                a2a(ch, k).wait_send()
                back_to(ch, k).wait_send()
                forward(ch, k, recv.at[ch, c, (g + 16 - k) % 16]).wait_send()
                return 0

            lax.fori_loop(1, 16, sent, 0)
            forward(ch, 0, sbuf.at[ch, me]).wait_send()
        to_sib_gain.wait_send()
        for n in range(6):
            i, h = w_pairs[n]
            w_ring(wown.at[half[h]], x, n, mr).wait_send()

        @pl.when(jnp.logical_not(own))
        def _():
            for h in range(3):
                swap(h).wait_send()

        for k in range(1, 4):
            gain_y(k).wait_send()
            strip_x(wown, k).wait_send()
            strip_y(k).wait_send()

        def y_sent(i, _):
            for h in range(2):
                y_far(i, h).wait_send()
                y_near(i, h).wait_send()
            return 0

        lax.fori_loop(0, 4, y_sent, 0)

        def z_sent(n, _):
            @pl.when(jnp.logical_not(z_self(n)))
            def _():
                for i in range(4):
                    z_copy(i, n).wait_send()
                zg_copy(n).wait_send()

            return 0

        lax.fori_loop(0, 8, z_sent, 0)

    p_in[1].wait()
    tokens_arrived(0)
    prepare(0)

    @pl.when(own)
    def _():
        own_w[0].wait()

    for k in range(1, 4):
        rows = pl.ds(pl.multiple_of(768 + 64 * ((y + 4 - k) % 4), 64), 64)
        remote(wout.at[:, rows], wout.at[:, rows], usend.at[k], urecv.at[k], f, m).wait_recv()

    def shard_arrived(i):
        for h in range(2):
            waited = jnp.logical_or(i == 0, jnp.logical_and(i < 3, h == i - 1))

            @pl.when(jnp.logical_not(waited))
            def _():
                slot = shard_of(i)
                remote(wown.at[half[h]], wout.at[slot, half[h]], wsend.at[0], wrecv.at[i, h], f, mr).wait_recv()

    def first_heads(i, _):
        shard_arrived(i)
        heads(0, i)

        @pl.when(i == 2)
        def _():
            relay_tokens(1)
            tokens_arrived(1)
            prepare(1)
            heads(1, 0)

        return 0

    def second_heads(i, _):
        heads(1, i)

        @pl.when(i == 1)
        def _():
            token_gradient(0)

        return 0

    def all_weights(i, _):
        weights(i)
        return 0

    lax.fori_loop(0, 4, first_heads, 0)
    partial(0)
    lax.fori_loop(1, 4, second_heads, 0)
    partial(1)
    lax.fori_loop(0, 1, all_weights, 0)
    token_gradient(1)
    gvec[...] = jnp.broadcast_to(jnp.sum(gacc[...], axis=0, keepdims=True), (8, D))
    to_sib_gain.start()
    gather_own(0)
    lax.fori_loop(1, 4, all_weights, 0)
    gather_pair(0)
    lax.fori_loop(0, 2, y_step, 0)
    gather_relay(0, 0)
    to_sib_gain.wait_recv()
    gcol[...] = jnp.broadcast_to(gvec[0:1] + gvecr[0:1], (128, D)).T.astype(BF).reshape(4, 4, 2, 32, 128)
    for k in range(1, 4):
        gain_y(k).start()
    own_gain.start()
    gather_own(1)
    y_step(2, 0)
    gather_pair(1)
    y_step(3, 0)
    gather_relay(0, 1)
    lax.fori_loop(0, 2, z_step, 0)
    gather_relay(1, 0)
    lax.fori_loop(2, 4, z_step, 0)

    own_gain.wait()
    for k in range(1, 4):
        remote(ggr.at[0], ggr.at[k], gsend.at[k], grecv.at[k], f, m).wait_recv()
    total = sum8([ggr[k].astype(F32) for k in range(4)])
    gzg[...] = total.astype(BF).reshape(8, 32, 128)

    def zg_send(n, _):
        @pl.when(jnp.logical_not(z_self(n)))
        def _():
            zg_copy(n).start()

        return 0

    lax.fori_loop(0, 8, zg_send, 0)

    @pl.when(own)
    def _():
        own_zg().start()

    lax.fori_loop(0, 4, x_step, 0)
    z_wait(4, gzg.at[0], lambda n: gzgr.at[n])

    @pl.when(own)
    def _():
        own_zg().wait()

    gxg[...] = sum8([gzgr[k].astype(F32) for k in range(8)]).astype(BF)
    for k in range(1, 4):
        gain_x(k).start()
    sent_early()
    gather_relay(1, 1)

    for i in range(1, 4):
        x_copy(i).wait_recv()
    total = sum8([gxs[0].astype(F32)] + [gxr[i].astype(F32) for i in range(1, 4)])
    for j in range(3):
        gq[j] = total[:, 128 * j : 128 * j + 128]
    go[...] = total[:, 384:512]
    for k in range(1, 4):
        gain_x(k).wait_recv()
    total = sum8([gxg[...].astype(F32)] + [gxgr[k].astype(F32) for k in range(1, 4)])
    gg[...] = jnp.broadcast_to(total[0:32, 0:1], (32, 128))

    for ch in range(2):
        for r in range(2):
            arrived(ch, r, xl, 1, 1)
            arrived(ch, r, xr, 0, 3)
            arrived(ch, r, xf, 0, 4)
            arrived(ch, r, xf, 1, 5)
            for n, (mm, h) in enumerate(((x, 0), (x, 1), (x, 1), (x, 0), (xl, 0), (xr, 1))):
                ring(ch, r, piece(ch, h, base(r) + mm), base(r) + mm, h, n, mr).wait_send()
    for k in range(1, 4):
        gain_x(k).wait_send()
        x_copy(k).wait_send()


def sublayer(tok, og, qkvw, outw, gain):
    vm = pl.BlockSpec(memory_space=pltpu.VMEM)
    hbm = pl.BlockSpec(memory_space=pltpu.HBM)
    dma = pltpu.SemaphoreType.DMA
    perms = jnp.asarray(np.stack([PACK, GROUP, REPACK, UNPACK]), BF)
    bf = lambda *shape: pltpu.VMEM(shape, BF)
    return pl.pallas_call(
        sublayer_kernel,
        out_shape=(
            jax.ShapeDtypeStruct((12, 256, D), BF),
            jax.ShapeDtypeStruct((3, 32, 128), F32),
            jax.ShapeDtypeStruct((32, 128), F32),
            jax.ShapeDtypeStruct((32, 128), F32),
        ),
        in_specs=[hbm] * 4 + [vm, hbm],
        out_specs=(hbm, vm, vm, vm),
        scratch_shapes=[
            bf(4, 384, 384),
            bf(2, 2, 6, 32, D),
            bf(2, 16, 48, 512),
            bf(2, 2, 16, 48, 512),
            bf(D, 512),
            bf(4, D, 512),
            bf(4, 384, D),
            bf(128, D),
            bf(2, 2, 6, 2, 32, D),
            bf(768, D),
            bf(D, 768),
            bf(D, 768),
            bf(384, 512),
            bf(4, 768, 384),
            bf(4, 768, 128),
            pltpu.VMEM((6, 2, 32, D), F32),
            bf(2, 6, 32, D),
            bf(2, 6, 32, D),
            bf(6, 32, D),
            pltpu.VMEM((8, D), F32),
            pltpu.VMEM((8, D), F32),
            pltpu.VMEM((8, D), F32),
            bf(4, 4, 2, 32, 128),
            bf(2, 16, 48, 256),
            bf(2, 16, 48, 256),
            bf(2, 6, 32, D),
            bf(4, 4, 4, 2, 32, 512),
            bf(4, 2, 2, 2, 32, 512),
            bf(4, 2, 4, 2, 32, 512),
            bf(4, 4, 2, 32, 128),
            bf(4, 8, 32, 512),
            bf(4, 8, 32, 512),
            bf(8, 32, 128),
            bf(8, 32, 128),
            bf(4, 32, 512),
            bf(4, 32, 512),
            bf(32, 128),
            bf(4, 32, 128),
            dma((12,)),
            dma((2,)),
            dma((4,)),
            dma((2,)),
            dma((2, 2)),
            dma((5,)),
            dma,
            dma((2, 16)),
            dma((2, 16)),
            dma((2, 16)),
            dma((2, 16)),
            dma((3,)),
            dma((3,)),
            dma((4,)),
            dma((4,)),
            dma((4,)),
            dma((4,)),
            dma((6,)),
            dma((4, 2)),
            dma((2,)),
            dma((2,)),
            dma,
            dma,
            dma((2, 16)),
            dma((2, 16)),
            dma((2, 2)),
            dma((2, 2)),
            dma((2, 2, 6)),
            dma((2, 2, 6)),
            dma((4, 2)),
            dma((4, 2)),
            dma((4, 2)),
            dma((4, 2)),
            dma((4,)),
            dma((4,)),
            dma((5, 8)),
            dma((5, 8)),
            dma((4,)),
            dma((4,)),
            dma((4,)),
            dma((4,)),
        ],
        compiler_params=pltpu.CompilerParams(
            collective_id=0, has_side_effects=True, vmem_limit_bytes=58 * 2**20
        ),
        name="sublayer",
    )(tok, og, qkvw, outw, gain, perms)


def finish_kernel(tgrad, gq, go, gg, out, oq, oo, og, buf, insem, outsem):
    into = [pltpu.make_async_copy(tgrad.at[pl.ds(2 * n, 2)], buf.at[pl.ds(2 * n, 2)], insem.at[n]) for n in range(6)]
    away = [pltpu.make_async_copy(buf.at[pl.ds(2 * n, 2)], out.at[pl.ds(2 * n, 2)], outsem.at[n]) for n in range(6)]
    for copy in into:
        copy.start()
    oq[...] = gq[...]
    oo[...] = go[...]
    og[...] = gg[...].T[0:1, :]
    for n in range(6):
        into[n].wait()
        away[n].start()
    for copy in away:
        copy.wait()


def finish(tgrad, gq, go, gg):
    vm = pl.BlockSpec(memory_space=pltpu.VMEM)
    hbm = pl.BlockSpec(memory_space=pltpu.HBM)
    return pl.pallas_call(
        finish_kernel,
        out_shape=(
            jax.ShapeDtypeStruct((12, 256, D), BF),
            jax.ShapeDtypeStruct((3, 32, 128), F32),
            jax.ShapeDtypeStruct((32, 128), F32),
            jax.ShapeDtypeStruct((1, 32), F32),
        ),
        in_specs=[hbm, vm, vm, vm],
        out_specs=(hbm, vm, vm, vm),
        scratch_shapes=[
            pltpu.VMEM((12, 256, D), BF),
            pltpu.SemaphoreType.DMA((6,)),
            pltpu.SemaphoreType.DMA((6,)),
        ],
        compiler_params=pltpu.CompilerParams(vmem_limit_bytes=58 * 2**20),
        name="finish",
    )(tgrad, gq, go, gg)


def shards(tokens, output_gradient, gain, qkv_weight, out_weight):
    clips, frames, patches, width = tokens.shape
    results = sublayer(
        tokens.reshape(12, 256, D),
        output_gradient.reshape(12, 256, D),
        jnp.transpose(qkv_weight, (1, 0, 2)),
        out_weight,
        gain.reshape(1, D),
    )
    tgrad, gq, go, gg = finish(*results)
    return (
        tgrad.reshape(clips, frames, patches, width),
        jnp.transpose(gq, (1, 0, 2)),
        go.T,
        gg.reshape(32),
    )


def solution(mesh):
    in_specs = (
        P(None, "frame", None, None),
        P(None, "frame", None, None),
        P(),
        P(None, None, "mlp"),
        P("mlp", None),
    )
    out_specs = (
        P(None, "frame", None, None),
        P("frame", None, "mlp"),
        P("mlp", "frame"),
        P("frame"),
    )
    return jax.shard_map(shards, mesh=mesh, in_specs=in_specs, out_specs=out_specs, check_vma=False)
```

```python
import numpy as np

import jax
import jax.numpy as jnp
from jax import lax
from jax.experimental import pallas as pl
from jax.experimental.pallas import tpu as pltpu
from jax.sharding import PartitionSpec as P

MESH = pl.DeviceIdType.MESH
BF = jnp.bfloat16
F32 = jnp.float32
D = 1024
FACTOR = 64 ** (-0.5)
NEG = -1e30


def one_hot(shape, perm):
    index = np.arange(384).reshape(shape).transpose(perm).reshape(-1)
    return np.eye(384, dtype=np.float32)[index]


PACK = one_hot((2, 2, 6, 8, 2), (3, 0, 1, 4, 2))
GROUP = one_hot((8, 2, 2, 6, 2), (1, 2, 3, 0, 4))
REPACK = one_hot((4, 6, 8, 2), (2, 0, 1, 3))
UNPACK = one_hot((8, 4, 2, 6), (1, 3, 0, 2))


def remote(src, dst, send, recv, f, m):
    return pltpu.make_async_remote_copy(
        src_ref=src, dst_ref=dst, send_sem=send, recv_sem=recv, device_id=(f, m), device_id_type=MESH
    )


def greet(barrier, f, m):
    pl.semaphore_signal(barrier, inc=1, device_id=(f, m), device_id_type=MESH)


def standardize(values):
    centered = values - jnp.mean(values, axis=-1, keepdims=True)
    rstd = lax.rsqrt(jnp.mean(centered * centered, axis=-1, keepdims=True) + 1e-05)
    return centered * rstd, rstd


def dot_t(a, b):
    return lax.dot_general(a, b, (((1,), (1,)), ((), ())), preferred_element_type=F32)


def turned(a):
    return jnp.concatenate([a[:, :128].T, a[:, 128:].T], axis=1)


def attend(q, k, v, d, allowed, first):
    zero = jnp.zeros_like(k)
    k2 = jnp.concatenate([jnp.where(first, k, zero), jnp.where(first, zero, k)], axis=0)
    v2 = jnp.concatenate([jnp.where(first, v, zero), jnp.where(first, zero, v)], axis=0)
    q = q * FACTOR
    scores = dot_t(q, k2)
    dprob = dot_t(d, v2)
    probs, dscore = [], []
    for h in range(2):
        s = jnp.where(allowed, scores[:, 128 * h : 128 * h + 128], NEG)
        e = jnp.exp(s - jnp.max(s, axis=-1, keepdims=True))
        p = e * (1.0 / jnp.sum(e, axis=-1, keepdims=True))
        dp = dprob[:, 128 * h : 128 * h + 128]
        delta = jnp.sum(p * dp, axis=-1, keepdims=True)
        probs.append(p.astype(BF))
        dscore.append((p * (dp - delta)).astype(BF))
    probs = jnp.concatenate(probs, axis=1)
    dscore = jnp.concatenate(dscore, axis=1)
    out = jnp.dot(probs, v2, preferred_element_type=F32)
    dq = jnp.dot(dscore, k2, preferred_element_type=F32) * FACTOR
    d2 = jnp.concatenate([jnp.where(first, d, zero), jnp.where(first, zero, d)], axis=0)
    q2 = jnp.concatenate([jnp.where(first, q, zero), jnp.where(first, zero, q)], axis=0)
    dv = jnp.dot(turned(probs), d2, preferred_element_type=F32)
    dk = jnp.dot(turned(dscore), q2, preferred_element_type=F32)
    return out, dq, dk, dv


def sublayer_kernel(
    tok, og, qkvw, outw, gain, perms,
    tgrad, gq, go, gg,
    order, xin, sbuf, recv, wown, wout, wt, ow, xs, normed, norm_t, og_t, proj, back, ao, part, other, rsib,
    tg, gacc, gvec, gvecr, gcol, sret, rret, blk, grads, gf, gn, ggr, gz, gzr, gzg, gzgr, gxs, gxr, gxg, gxgr,
    loc, ploc, kloc, wloc, oloc, zloc, gloc,
    asend, arecv, fsend, frecv, ssend, srecv, qsend, qrecv, usend, urecv, wsend, wrecv, bsend, brecv, vsend, vrecv,
    csend, crecv, psend, precv, rsend, rrecv, y1send, y1recv, y2send, y2recv, gsend, grecv,
    zsend, zrecv, xsend, xrecv, hsend, hrecv,
):
    f, m = lax.axis_index("frame"), lax.axis_index("mlp")
    g, c, z, x = f // 2, f % 2, m // 4, m % 4
    zh, y = f // 8, (f // 2) % 4
    zi = zh * 2 + z
    sib = g * 2 + 1 - c
    mz = (1 - z) * 4 + x
    xl, xr, xf = (x + 3) % 4, (x + 1) % 4, (x + 2) % 4
    mr, ml = z * 4 + xr, z * 4 + xl
    yl, yr, yf = (y + 3) % 4, (y + 1) % 4, (y + 2) % 4
    fr, fl = (zh * 4 + yr) * 2 + c, (zh * 4 + yl) * 2 + c
    own = c == z
    start = (zi + 5 + 3 * z) % 8
    me = (3 - 3 * z) * 4 + y

    def window(lo, h):
        return (zh + 3 - 2 * lo + h) % 4

    def owner(slot):
        to = (start + slot // 4) % 8
        return ((to // 2) * 4 + slot % 4) * 2 + c, (to % 2) * 4 + x

    def source(n):
        there = n // 4
        d = (there + 4 - zh) % 4
        lo = (d % 2) * (d // 2) + (1 - d % 2) * ((d // 2) * (1 - z) + (1 - d // 2) * z)
        place = (zi + 16 - (there * 2 + lo + 5 + 3 * lo)) % 8
        return n * 2 + c, lo * 4 + x, place * 4 + y

    p_in = [pltpu.make_async_copy(perms.at[pl.ds(0, 1)], order.at[pl.ds(0, 1)], ploc.at[0])]
    p_in.append(pltpu.make_async_copy(perms.at[pl.ds(1, 3)], order.at[pl.ds(1, 3)], ploc.at[1]))
    p_in[0].start()
    w_in = [pltpu.make_async_copy(qkvw.at[j], wown.at[:, pl.ds(128 * j, 128)], loc.at[j]) for j in range(3)]
    w_in.append(pltpu.make_async_copy(outw, ow, loc.at[3]))
    for copy in w_in:
        copy.start()
    x_in = []
    for ch in range(2):
        for t, ref in enumerate((tok, og)):
            for h in range(2):
                rows = pl.ds(pl.multiple_of(x * 64 + window(z, h) * 16, 16), 16)
                x_in.append(
                    pltpu.make_async_copy(
                        ref.at[pl.ds(6 * ch, 6), rows, :],
                        xin.at[ch, t, :, pl.ds(16 * h, 16), :],
                        loc.at[4 + 4 * ch + 2 * t + h],
                    )
                )
                x_in[-1].start()

    p_in[1].start()
    barrier = pltpu.get_barrier_semaphore()

    def hello_plane(k, _):
        n = (zi * 4 + y + k) % 32
        greet(barrier, ((n // 8) * 4 + n % 4) * 2 + c, ((n // 4) % 2) * 4 + x)
        return 0

    def hello_other(k, _):
        greet(barrier, ((k // 2) * 4 + y) * 2 + 1 - c, (k % 2) * 4 + x)
        return 0

    lax.fori_loop(1, 32, hello_plane, 0)
    lax.fori_loop(0, 8, hello_other, 0)
    for k in range(1, 4):
        greet(barrier, f, z * 4 + (x + k) % 4)

    for copy in w_in:
        copy.wait()
    wown[:, 384:512] = ow[...].T
    p_in[0].wait()

    def pack(ch):
        for copy in x_in[4 * ch : 4 * ch + 4]:
            copy.wait()
        for gh in range(2):
            rows = slice(16 * gh, 16 * gh + 16)
            parts = [xin[ch, t, :, rows, 512 * h : 512 * h + 512].reshape(96, 512) for h in range(2) for t in range(2)]
            packed = jnp.dot(order[0], jnp.concatenate(parts, axis=0), preferred_element_type=F32)
            sbuf[ch, 8 * gh : 8 * gh + 8] = packed.astype(BF).reshape(8, 48, 512)

    pack(0)
    pl.semaphore_wait(barrier, 42)

    half = (pl.ds(0, 384), pl.ds(384, 384))
    strip = pl.ds(pl.multiple_of(768 + 64 * y, 64), 64)
    w_pairs = ((1, 0), (1, 1), (2, 1), (2, 0), (3, 0), (3, 1))

    def w_ring(src, slot, n, to):
        i, h = w_pairs[n]
        return remote(src, wout.at[slot, half[h]], wsend.at[n], wrecv.at[i, h], f, to)

    def w_spread(src, h):
        if h == 0:
            w_ring(src.at[half[0]], x, 0, mr).start()
            w_ring(src.at[half[0]], x, 3, ml).start()
        else:
            w_ring(src.at[half[1]], x, 2, ml).start()
            w_ring(src.at[half[1]], x, 1, mr).start()

    def swap(h):
        rows = (half[0], half[1], strip)[h]
        return remote(wown.at[rows], wout.at[x, rows], ssend.at[h], srecv.at[h], g * 2 + 1 - c, mz)

    def strip_x(src, k):
        return remote(src.at[strip], wout.at[x, strip], qsend.at[k], qrecv.at[k], f, z * 4 + (x + k) % 4)

    def strip_y(k):
        to = (zh * 4 + (y + k) % 4) * 2 + c
        return remote(wout.at[:, strip], wout.at[:, strip], usend.at[k], urecv.at[k], to, m)

    own_w = [
        pltpu.make_async_copy(wown.at[pl.ds(0, 768)], wout.at[x, pl.ds(0, 768)], wloc.at[0]),
        pltpu.make_async_copy(wown.at[strip], wout.at[x, strip], wloc.at[1]),
    ]

    @pl.when(own)
    def _():
        own_w[1].start()
        for k in range(1, 4):
            strip_x(wown, k).start()
        w_spread(wown, 0)
        w_spread(wown, 1)
        own_w[0].start()

    @pl.when(jnp.logical_not(own))
    def _():
        swap(2).start()
        swap(0).start()
        swap(1).start()

    def a2a(ch, k):
        slot = (me + k) % 16
        return remote(sbuf.at[ch, slot], recv.at[ch, c, g], asend.at[ch, k], arecv.at[ch, g], *owner(slot))

    def forward(ch, k, src):
        slot = (g + 16 - k) % 16
        return remote(src, recv.at[ch, c, slot], fsend.at[ch, k], frecv.at[ch, k], sib, m)

    def keep(ch):
        return pltpu.make_async_copy(sbuf.at[ch, me], recv.at[ch, c, g], kloc.at[ch])

    for ch in range(2):
        if ch:
            pack(ch)

        def send(k, _, ch=ch):
            a2a(ch, k).start()
            return 0

        lax.fori_loop(1, 16, send, 0)
        keep(ch).start()
        forward(ch, 0, sbuf.at[ch, me]).start()

        if ch == 0:

            @pl.when(jnp.logical_not(own))
            def _():
                swap(2).wait_recv()
                for k in range(1, 4):
                    strip_x(wout.at[x], k).start()

    @pl.when(own)
    def _():
        own_w[1].wait()

    for k in range(1, 4):
        remote(wown.at[strip], wout.at[(x + 4 - k) % 4, strip], qsend.at[k], qrecv.at[k], f, m).wait_recv()
    for k in range(1, 4):
        strip_y(k).start()

    @pl.when(jnp.logical_not(own))
    def _():
        swap(0).wait_recv()
        w_spread(wout.at[x], 0)
        swap(1).wait_recv()
        w_spread(wout.at[x], 1)

    def w_arrived(n):
        i, h = w_pairs[n]
        slot = (x, xl, xr, xf)[i]
        remote(wown.at[half[h]], wout.at[slot, half[h]], wsend.at[n], wrecv.at[i, h], f, mr).wait_recv()

    def relay_tokens(ch):
        def relay(k, _):
            slot = (g + 16 - k) % 16
            remote(sbuf.at[ch, 0], recv.at[ch, c, slot], asend.at[ch, k], arecv.at[ch, slot], f, m).wait_recv()
            forward(ch, k, recv.at[ch, c, slot]).start()
            return 0

        lax.fori_loop(1, 16, relay, 0)

    def tokens_arrived(ch):
        keep(ch).wait()

        def wait(k, _):
            slot = (g + 16 - k) % 16
            remote(sbuf.at[ch, 0], recv.at[ch, 1 - c, slot], fsend.at[ch, k], frecv.at[ch, k], f, m).wait_recv()
            return 0

        lax.fori_loop(0, 16, wait, 0)

    relay_tokens(0)
    w_arrived(0)
    w_ring(wout.at[xl, half[0]], xl, 4, mr).start()
    w_arrived(2)
    w_ring(wout.at[xr, half[1]], xr, 5, ml).start()

    lane = lax.broadcasted_iota(jnp.int32, (128, 128), 1)
    line = lax.broadcasted_iota(jnp.int32, (128, 128), 0)
    first = lane < 64
    allowed = (lane < 64) == (line < 64)

    def shard_of(i):
        return (x + (i % 2) * 3 + (i // 2) * (1 + (i % 2) * 2)) % 4

    def prepare(ch):
        for s in range(2):
            for gh in range(2):
                block = recv[ch, s, 8 * gh : 8 * gh + 8].reshape(384, 512)
                rows = jnp.dot(order[1], block, preferred_element_type=F32).astype(BF).reshape(2, 2, 6, 16, 512)
                for h in range(2):
                    xs[ch, :, :, s, 16 * gh : 16 * gh + 16, 512 * h : 512 * h + 512] = rows[h]

        def norm(u, _):
            xhat, _ = standardize(xs[ch, 0, u].reshape(64, D).astype(F32))
            normed[pl.ds(pl.multiple_of(ch * 384 + u * 64, 64), 64), :] = (xhat * gain[...]).astype(BF)
            return 0

        lax.fori_loop(0, 6, norm, 0, unroll=2)
        for i in range(3):
            at = 384 * ch + 128 * i
            norm_t[:, at : at + 128] = normed[at : at + 128, :].T
            og_t[:, at : at + 128] = xs[ch, 1, 2 * i : 2 * i + 2].reshape(128, D).T

    def heads(ch, i):
        j = shard_of(i)
        at = 384 * ch
        if ch == 0:
            wt[i] = wout[j, :, 0:384].T
        proj[:, 0:384] = jnp.dot(normed[at : at + 384, :], wout[j, :, 0:384], preferred_element_type=F32).astype(BF)
        proj[:, 384:512] = jnp.dot(
            xs[ch, 1].reshape(384, D), wout[j, :, 384:512], preferred_element_type=F32
        ).astype(BF)
        for n in range(3):
            rows = slice(128 * n, 128 * n + 128)
            out, dq, dk, dv = attend(
                proj[rows, 0:128], proj[rows, 128:256], proj[rows, 256:384], proj[rows, 384:512], allowed, first
            )
            rows = slice(at + 128 * n, at + 128 * n + 128)
            back[i, rows, 0:128] = dq.astype(BF)
            back[i, rows, 128:256] = dk.astype(BF)
            back[i, rows, 256:384] = dv.astype(BF)
            ao[i, rows, :] = out.astype(BF)

    def to_sibling(ch):
        return remote(other.at[ch], rsib.at[ch], bsend.at[ch], brecv.at[ch], sib, m)

    def partial(ch, groups):
        for n in range(3):
            rows = slice(384 * ch + 128 * n, 384 * ch + 128 * n + 128)
            term = jnp.dot(back[groups[0], rows, :], wt[groups[0]], preferred_element_type=F32)
            for i in groups[1:]:
                term += jnp.dot(back[i, rows, :], wt[i], preferred_element_type=F32)
            term = term.reshape(2, 2, 32, D)
            if groups[0] == 0:
                part[2 * n : 2 * n + 2] = term
            else:
                part[2 * n : 2 * n + 2] += term
        if groups[-1] == 3:
            other[ch] = part[:, 1 - c].astype(BF)
            to_sibling(ch).start()

    def back_to(ch, k):
        n = (g + k) % 16
        fs, ms, slot = source(n)
        return remote(sret.at[ch, n], rret.at[ch, slot], csend.at[ch, k], crecv.at[ch, slot], fs, ms)

    def keep_back(ch):
        return pltpu.make_async_copy(sret.at[ch, g], rret.at[ch, me], kloc.at[2 + ch])

    def token_gradient(ch):
        to_sibling(ch).wait_recv()

        def token(u, total):
            xhat, rstd = standardize(xs[ch, 0, u, c].astype(F32))
            dn = part[u, c] + rsib[ch, u].astype(F32)
            bp = dn * gain[...]
            inner = bp - jnp.mean(bp, axis=-1, keepdims=True) - xhat * jnp.mean(bp * xhat, axis=-1, keepdims=True)
            tg[u] = (xs[ch, 1, u, c].astype(F32) + rstd * inner).astype(BF)
            return total + jnp.sum((dn * xhat).reshape(4, 8, D), axis=0)

        total = lax.fori_loop(0, 6, token, jnp.zeros((8, D), F32), unroll=2)
        if ch == 0:
            gacc[...] = total
        else:
            gacc[...] += total
        for gh in range(2):
            rows = slice(16 * gh, 16 * gh + 16)
            parts = [tg[:, rows, 256 * h : 256 * h + 256].reshape(96, 256) for h in range(4)]
            packed = jnp.dot(order[2], jnp.concatenate(parts, axis=0), preferred_element_type=F32)
            sret[ch, 8 * gh : 8 * gh + 8] = packed.astype(BF).reshape(8, 48, 256)

        def send(k, _):
            back_to(ch, k).start()
            return 0

        lax.fori_loop(1, 16, send, 0)
        keep_back(ch).start()

    def piece(ch, h, mm):
        rows = pl.ds(pl.multiple_of((mm % 4) * 64 + window(mm // 4, h) * 16, 16), 16)
        return tgrad.at[pl.ds(6 * ch, 6), rows, :]

    def kept(ch, h):
        return blk.at[ch, :, pl.ds(16 * h, 16), :]

    def pair(ch, h):
        return remote(kept(ch, h), piece(ch, h, m), psend.at[ch, h], precv.at[ch, h], f, mz)

    def ring(ch, r, src, mm, h, n, to):
        return remote(src, piece(ch, h, mm), rsend.at[ch, r, n], rrecv.at[ch, r, n], f, to)

    def own_out(ch, h):
        return pltpu.make_async_copy(kept(ch, h), piece(ch, h, m), oloc.at[ch, h])

    def gather_own(ch):
        keep_back(ch).wait()

        def received(k, _):
            slot = (me + k) % 16
            remote(sret.at[ch, 0], rret.at[ch, slot], csend.at[ch, k], crecv.at[ch, slot], f, m).wait_recv()
            return 0

        lax.fori_loop(1, 16, received, 0)
        for gh in range(2):
            block = rret[ch, 8 * gh : 8 * gh + 8].reshape(384, 256)
            rows = jnp.dot(order[3], block, preferred_element_type=F32).astype(BF).reshape(4, 6, 16, 256)
            for h in range(4):
                blk[ch, :, 16 * gh : 16 * gh + 16, 256 * h : 256 * h + 256] = rows[h]
        pair(ch, 0).start()
        pair(ch, 1).start()
        ring(ch, 0, kept(ch, 0), m, 0, 0, mr).start()
        ring(ch, 0, kept(ch, 1), m, 1, 2, ml).start()
        ring(ch, 0, kept(ch, 1), m, 1, 1, mr).start()
        ring(ch, 0, kept(ch, 0), m, 0, 3, ml).start()
        own_out(ch, 0).start()
        own_out(ch, 1).start()

    def gather_pair(ch):
        def arrived(h):
            remote(kept(ch, h), piece(ch, h, mz), psend.at[ch, h], precv.at[ch, h], f, mz).wait_recv()

        arrived(0)
        ring(ch, 1, piece(ch, 0, mz), mz, 0, 0, mr).start()
        ring(ch, 1, piece(ch, 0, mz), mz, 0, 3, ml).start()
        arrived(1)
        ring(ch, 1, piece(ch, 1, mz), mz, 1, 2, ml).start()
        ring(ch, 1, piece(ch, 1, mz), mz, 1, 1, mr).start()

    def base(r):
        return (z if r == 0 else 1 - z) * 4

    def arrived(ch, r, mm, h, n):
        ring(ch, r, piece(ch, h, base(r) + mm), base(r) + mm, h, n, mr).wait_recv()

    def gather_relay(ch, r):
        arrived(ch, r, xl, 0, 0)
        ring(ch, r, piece(ch, 0, base(r) + xl), base(r) + xl, 0, 4, mr).start()
        arrived(ch, r, xr, 1, 2)
        ring(ch, r, piece(ch, 1, base(r) + xr), base(r) + xr, 1, 5, ml).start()

    def weights(i):
        j = shard_of(i)

        left = jnp.dot(norm_t[...], back[i], preferred_element_type=F32).astype(BF)
        grads[j, :, :, :, :, 0:384] = left.reshape(4, 4, 2, 32, 384)
        left = jnp.dot(og_t[...], ao[i], preferred_element_type=F32).astype(BF)
        grads[j, :, :, :, :, 384:512] = left.reshape(4, 4, 2, 32, 128)
        y_far(i, 0).start()
        y_far(i, 1).start()

    def y_far(i, h):
        src = grads.at[shard_of(i), pl.ds(2 * h, 2), yf]
        return remote(src, gf.at[i, h], y1send.at[i, h], y1recv.at[i, h], fr if h == 0 else fl, m)

    def y_near(i, h):
        src = grads.at[shard_of(i), :, yr if h == 0 else yl]
        return remote(src, gn.at[i, h], y2send.at[i, h], y2recv.at[i, h], fr if h == 0 else fl, m)

    def y_step(i, _):
        j = shard_of(i)
        for h in range(2):
            y_far(i, h).wait_recv()
            to = yr if h == 0 else yl
            for a in range(2):
                total = grads[j, 2 * h + a, to].astype(F32) + gf[i, h, a].astype(F32)
                grads[j, 2 * h + a, to] = total.astype(BF)
            y_near(i, h).start()
        return 0

    def z_copy(i, n):
        to = ((n // 2) * 4 + y) * 2 + n % 2
        return remote(gz.at[i, n], gzr.at[i, zi], zsend.at[i, n], zrecv.at[i, zi], to, c * 4 + x)

    def zg_copy(n):
        to = ((n // 2) * 4 + y) * 2 + n % 2
        return remote(gzg.at[n], gzgr.at[zi], zsend.at[4, n], zrecv.at[4, zi], to, c * 4 + x)

    def z_self(n):
        return jnp.logical_and(n == zh * 2 + c, own)

    def own_z(i):
        return pltpu.make_async_copy(gz.at[i, zh * 2 + c], gzr.at[i, zi], zloc.at[i])

    def own_zg():
        return pltpu.make_async_copy(gzg.at[zh * 2 + c], gzgr.at[zi], zloc.at[4])

    def z_step(i, _):
        j = shard_of(i)
        for h in range(2):
            y_near(i, h).wait_recv()
        for a in range(4):
            total = grads[j, a, y].astype(F32) + (gn[i, 0, a].astype(F32) + gn[i, 1, a].astype(F32))
            gz[i, 2 * a : 2 * a + 2] = total.astype(BF)

        def z_send(n, _):
            @pl.when(jnp.logical_not(z_self(n)))
            def _():
                z_copy(i, n).start()

            return 0

        lax.fori_loop(0, 8, z_send, 0)

        @pl.when(own)
        def _():
            own_z(i).start()

        return 0

    def z_wait(i, src, dst):
        def wait(n, _):
            @pl.when(jnp.logical_not(jnp.logical_and(n == zi, own)))
            def _():
                remote(src, dst(n), zsend.at[i, 0], zrecv.at[i, n], f, m).wait_recv()

            return 0

        lax.fori_loop(0, 8, wait, 0)

    def sum8(terms):
        while len(terms) > 1:
            terms = [a + b for a, b in zip(terms[::2], terms[1::2])]
        return terms[0]

    def x_copy(i):
        return remote(gxs.at[i], gxr.at[i], xsend.at[i], xrecv.at[i], f, z * 4 + shard_of(i))

    def x_step(i, _):
        z_wait(i, gz.at[0, 0], lambda n: gzr.at[i, n])

        @pl.when(own)
        def _():
            own_z(i).wait()

        gxs[i] = sum8([gzr[i, k].astype(F32) for k in range(8)]).astype(BF)

        @pl.when(jnp.asarray(i) > 0)
        def _():
            x_copy(i).start()

        return 0

    def gain_y(k):
        yk = (y + k) % 4
        return remote(gcol.at[:, yk], ggr.at[k], gsend.at[k], grecv.at[k], (zh * 4 + yk) * 2 + c, m)

    own_gain = pltpu.make_async_copy(gcol.at[:, y], ggr.at[0], gloc)

    def gain_x(k):
        return remote(gxg, gxgr.at[k], hsend.at[k], hrecv.at[k], f, z * 4 + (x + k) % 4)

    to_sib_gain = remote(gvec, gvecr, vsend, vrecv, sib, m)

    def sent_early():
        for ch in range(2):
            pair(ch, 0).wait_send()
            pair(ch, 1).wait_send()
            own_out(ch, 0).wait()
            own_out(ch, 1).wait()
            to_sibling(ch).wait_send()

            def sent(k, _, ch=ch):
                a2a(ch, k).wait_send()
                back_to(ch, k).wait_send()
                forward(ch, k, recv.at[ch, c, (g + 16 - k) % 16]).wait_send()
                return 0

            lax.fori_loop(1, 16, sent, 0)
            forward(ch, 0, sbuf.at[ch, me]).wait_send()
        to_sib_gain.wait_send()
        for n in range(6):
            i, h = w_pairs[n]
            w_ring(wown.at[half[h]], x, n, mr).wait_send()

        @pl.when(jnp.logical_not(own))
        def _():
            for h in range(3):
                swap(h).wait_send()

        for k in range(1, 4):
            gain_y(k).wait_send()
            strip_x(wown, k).wait_send()
            strip_y(k).wait_send()

        def y_sent(i, _):
            for h in range(2):
                y_far(i, h).wait_send()
                y_near(i, h).wait_send()
            return 0

        lax.fori_loop(0, 4, y_sent, 0)

        def z_sent(n, _):
            @pl.when(jnp.logical_not(z_self(n)))
            def _():
                for i in range(4):
                    z_copy(i, n).wait_send()
                zg_copy(n).wait_send()

            return 0

        lax.fori_loop(0, 8, z_sent, 0)

    p_in[1].wait()
    tokens_arrived(0)
    prepare(0)

    @pl.when(own)
    def _():
        own_w[0].wait()

    for k in range(1, 4):
        rows = pl.ds(pl.multiple_of(768 + 64 * ((y + 4 - k) % 4), 64), 64)
        remote(wout.at[:, rows], wout.at[:, rows], usend.at[k], urecv.at[k], f, m).wait_recv()

    def shard_arrived(i):
        for h in range(2):
            waited = jnp.logical_or(i == 0, jnp.logical_and(i < 3, h == i - 1))

            @pl.when(jnp.logical_not(waited))
            def _():
                slot = shard_of(i)
                remote(wown.at[half[h]], wout.at[slot, half[h]], wsend.at[0], wrecv.at[i, h], f, mr).wait_recv()

    def first_heads(i, _):
        shard_arrived(i)
        heads(0, i)

        @pl.when(i == 2)
        def _():
            partial(0, (0, 1, 2))
            relay_tokens(1)

        return 0

    def second_heads(i, _):
        heads(1, i)

        @pl.when(i == 0)
        def _():
            token_gradient(0)

        return 0

    def all_weights(i, _):
        weights((i + 1) % 4)
        return 0

    def y_steps(first, last):
        lax.fori_loop(first, last, lambda i, _: y_step((i + 1) % 4, 0), 0)

    def z_steps(first, last):
        lax.fori_loop(first, last, lambda i, _: z_step((i + 1) % 4, 0), 0)

    lax.fori_loop(0, 4, first_heads, 0)
    partial(0, (3,))
    tokens_arrived(1)
    prepare(1)
    lax.fori_loop(0, 4, second_heads, 0)
    partial(1, (0, 1, 2, 3))
    lax.fori_loop(0, 1, all_weights, 0)
    token_gradient(1)
    gvec[...] = jnp.broadcast_to(jnp.sum(gacc[...], axis=0, keepdims=True), (8, D))
    to_sib_gain.start()
    gather_own(0)
    lax.fori_loop(1, 4, all_weights, 0)
    gather_pair(0)
    y_steps(0, 2)
    gather_relay(0, 0)
    to_sib_gain.wait_recv()
    gcol[...] = jnp.broadcast_to(gvec[0:1] + gvecr[0:1], (128, D)).T.astype(BF).reshape(4, 4, 2, 32, 128)
    for k in range(1, 4):
        gain_y(k).start()
    own_gain.start()
    gather_own(1)
    y_steps(2, 3)
    gather_pair(1)
    y_steps(3, 4)
    gather_relay(0, 1)
    z_steps(0, 2)

    own_gain.wait()
    for k in range(1, 4):
        remote(ggr.at[0], ggr.at[k], gsend.at[k], grecv.at[k], f, m).wait_recv()
    total = sum8([ggr[k].astype(F32) for k in range(4)])
    gzg[...] = total.astype(BF).reshape(8, 32, 128)

    def zg_send(n, _):
        @pl.when(jnp.logical_not(z_self(n)))
        def _():
            zg_copy(n).start()

        return 0

    lax.fori_loop(0, 8, zg_send, 0)

    @pl.when(own)
    def _():
        own_zg().start()

    gather_relay(1, 0)
    z_steps(2, 4)
    lax.fori_loop(1, 4, x_step, 0)
    z_wait(4, gzg.at[0], lambda n: gzgr.at[n])

    @pl.when(own)
    def _():
        own_zg().wait()

    gxg[...] = sum8([gzgr[k].astype(F32) for k in range(8)]).astype(BF)
    for k in range(1, 4):
        gain_x(k).start()
    gather_relay(1, 1)
    x_step(0, 0)
    sent_early()

    for i in range(1, 4):
        x_copy(i).wait_recv()
    total = sum8([gxs[0].astype(F32)] + [gxr[i].astype(F32) for i in range(1, 4)])
    for j in range(3):
        gq[j] = total[:, 128 * j : 128 * j + 128]
    go[...] = total[:, 384:512]
    for k in range(1, 4):
        gain_x(k).wait_recv()
    total = sum8([gxg[...].astype(F32)] + [gxgr[k].astype(F32) for k in range(1, 4)])
    gg[...] = jnp.broadcast_to(total[0:32, 0:1], (32, 128))

    for ch in range(2):
        for r in range(2):
            arrived(ch, r, xl, 1, 1)
            arrived(ch, r, xr, 0, 3)
            arrived(ch, r, xf, 0, 4)
            arrived(ch, r, xf, 1, 5)
            for n, (mm, h) in enumerate(((x, 0), (x, 1), (x, 1), (x, 0), (xl, 0), (xr, 1))):
                ring(ch, r, piece(ch, h, base(r) + mm), base(r) + mm, h, n, mr).wait_send()
    for k in range(1, 4):
        gain_x(k).wait_send()
        x_copy(k).wait_send()


def sublayer(tok, og, qkvw, outw, gain):
    vm = pl.BlockSpec(memory_space=pltpu.VMEM)
    hbm = pl.BlockSpec(memory_space=pltpu.HBM)
    dma = pltpu.SemaphoreType.DMA
    perms = jnp.asarray(np.stack([PACK, GROUP, REPACK, UNPACK]), BF)
    bf = lambda *shape: pltpu.VMEM(shape, BF)
    return pl.pallas_call(
        sublayer_kernel,
        out_shape=(
            jax.ShapeDtypeStruct((12, 256, D), BF),
            jax.ShapeDtypeStruct((3, 32, 128), F32),
            jax.ShapeDtypeStruct((32, 128), F32),
            jax.ShapeDtypeStruct((32, 128), F32),
        ),
        in_specs=[hbm] * 4 + [vm, hbm],
        out_specs=(hbm, vm, vm, vm),
        scratch_shapes=[
            bf(4, 384, 384),
            bf(2, 2, 6, 32, D),
            bf(2, 16, 48, 512),
            bf(2, 2, 16, 48, 512),
            bf(D, 512),
            bf(4, D, 512),
            bf(4, 384, D),
            bf(128, D),
            bf(2, 2, 6, 2, 32, D),
            bf(768, D),
            bf(D, 768),
            bf(D, 768),
            bf(384, 512),
            bf(4, 768, 384),
            bf(4, 768, 128),
            pltpu.VMEM((6, 2, 32, D), F32),
            bf(2, 6, 32, D),
            bf(2, 6, 32, D),
            bf(6, 32, D),
            pltpu.VMEM((8, D), F32),
            pltpu.VMEM((8, D), F32),
            pltpu.VMEM((8, D), F32),
            bf(4, 4, 2, 32, 128),
            bf(2, 16, 48, 256),
            bf(2, 16, 48, 256),
            bf(2, 6, 32, D),
            bf(4, 4, 4, 2, 32, 512),
            bf(4, 2, 2, 2, 32, 512),
            bf(4, 2, 4, 2, 32, 512),
            bf(4, 4, 2, 32, 128),
            bf(4, 8, 32, 512),
            bf(4, 8, 32, 512),
            bf(8, 32, 128),
            bf(8, 32, 128),
            bf(4, 32, 512),
            bf(4, 32, 512),
            bf(32, 128),
            bf(4, 32, 128),
            dma((12,)),
            dma((2,)),
            dma((4,)),
            dma((2,)),
            dma((2, 2)),
            dma((5,)),
            dma,
            dma((2, 16)),
            dma((2, 16)),
            dma((2, 16)),
            dma((2, 16)),
            dma((3,)),
            dma((3,)),
            dma((4,)),
            dma((4,)),
            dma((4,)),
            dma((4,)),
            dma((6,)),
            dma((4, 2)),
            dma((2,)),
            dma((2,)),
            dma,
            dma,
            dma((2, 16)),
            dma((2, 16)),
            dma((2, 2)),
            dma((2, 2)),
            dma((2, 2, 6)),
            dma((2, 2, 6)),
            dma((4, 2)),
            dma((4, 2)),
            dma((4, 2)),
            dma((4, 2)),
            dma((4,)),
            dma((4,)),
            dma((5, 8)),
            dma((5, 8)),
            dma((4,)),
            dma((4,)),
            dma((4,)),
            dma((4,)),
        ],
        compiler_params=pltpu.CompilerParams(
            collective_id=0, has_side_effects=True, vmem_limit_bytes=58 * 2**20
        ),
        name="sublayer",
    )(tok, og, qkvw, outw, gain, perms)


def finish_kernel(tgrad, gq, go, gg, out, oq, oo, og, buf, insem, outsem):
    into = [pltpu.make_async_copy(tgrad.at[pl.ds(2 * n, 2)], buf.at[pl.ds(2 * n, 2)], insem.at[n]) for n in range(6)]
    away = [pltpu.make_async_copy(buf.at[pl.ds(2 * n, 2)], out.at[pl.ds(2 * n, 2)], outsem.at[n]) for n in range(6)]
    for copy in into:
        copy.start()
    oq[...] = gq[...]
    oo[...] = go[...]
    og[...] = gg[...].T[0:1, :]
    for n in range(6):
        into[n].wait()
        away[n].start()
    for copy in away:
        copy.wait()


def finish(tgrad, gq, go, gg):
    vm = pl.BlockSpec(memory_space=pltpu.VMEM)
    hbm = pl.BlockSpec(memory_space=pltpu.HBM)
    return pl.pallas_call(
        finish_kernel,
        out_shape=(
            jax.ShapeDtypeStruct((12, 256, D), BF),
            jax.ShapeDtypeStruct((3, 32, 128), F32),
            jax.ShapeDtypeStruct((32, 128), F32),
            jax.ShapeDtypeStruct((1, 32), F32),
        ),
        in_specs=[hbm, vm, vm, vm],
        out_specs=(hbm, vm, vm, vm),
        scratch_shapes=[
            pltpu.VMEM((12, 256, D), BF),
            pltpu.SemaphoreType.DMA((6,)),
            pltpu.SemaphoreType.DMA((6,)),
        ],
        compiler_params=pltpu.CompilerParams(vmem_limit_bytes=58 * 2**20),
        name="finish",
    )(tgrad, gq, go, gg)


def shards(tokens, output_gradient, gain, qkv_weight, out_weight):
    clips, frames, patches, width = tokens.shape
    results = sublayer(
        tokens.reshape(12, 256, D),
        output_gradient.reshape(12, 256, D),
        jnp.transpose(qkv_weight, (1, 0, 2)),
        out_weight,
        gain.reshape(1, D),
    )
    tgrad, gq, go, gg = finish(*results)
    return (
        tgrad.reshape(clips, frames, patches, width),
        jnp.transpose(gq, (1, 0, 2)),
        go.T,
        gg.reshape(32),
    )


def solution(mesh):
    in_specs = (
        P(None, "frame", None, None),
        P(None, "frame", None, None),
        P(),
        P(None, None, "mlp"),
        P("mlp", None),
    )
    out_specs = (
        P(None, "frame", None, None),
        P("frame", None, "mlp"),
        P("mlp", "frame"),
        P("frame"),
    )
    return jax.shard_map(shards, mesh=mesh, in_specs=in_specs, out_specs=out_specs, check_vma=False)
```

```python
import numpy as np

import jax
import jax.numpy as jnp
from jax import lax
from jax.experimental import pallas as pl
from jax.experimental.pallas import tpu as pltpu
from jax.sharding import PartitionSpec as P

MESH = pl.DeviceIdType.MESH
BF = jnp.bfloat16
F32 = jnp.float32
D = 1024
FACTOR = 64 ** (-0.5)
NEG = -1e30


def one_hot(shape, perm):
    index = np.arange(384).reshape(shape).transpose(perm).reshape(-1)
    return np.eye(384, dtype=np.float32)[index]


PACK = one_hot((2, 2, 6, 8, 2), (3, 0, 1, 4, 2))
GROUP = one_hot((8, 2, 2, 6, 2), (1, 2, 3, 0, 4))
REPACK = one_hot((4, 6, 8, 2), (2, 0, 1, 3))
UNPACK = one_hot((8, 4, 2, 6), (1, 3, 0, 2))


def remote(src, dst, send, recv, f, m):
    return pltpu.make_async_remote_copy(
        src_ref=src, dst_ref=dst, send_sem=send, recv_sem=recv, device_id=(f, m), device_id_type=MESH
    )


def greet(barrier, f, m):
    pl.semaphore_signal(barrier, inc=1, device_id=(f, m), device_id_type=MESH)


def standardize(values):
    centered = values - jnp.mean(values, axis=-1, keepdims=True)
    rstd = lax.rsqrt(jnp.mean(centered * centered, axis=-1, keepdims=True) + 1e-05)
    return centered * rstd, rstd


def dot_t(a, b):
    return lax.dot_general(a, b, (((1,), (1,)), ((), ())), preferred_element_type=F32)


def turned(a):
    return jnp.concatenate([a[:, :128].T, a[:, 128:].T], axis=1)


def attend(q, k, v, d, allowed, first):
    zero = jnp.zeros_like(k)
    k2 = jnp.concatenate([jnp.where(first, k, zero), jnp.where(first, zero, k)], axis=0)
    v2 = jnp.concatenate([jnp.where(first, v, zero), jnp.where(first, zero, v)], axis=0)
    q = q * FACTOR
    scores = dot_t(q, k2)
    dprob = dot_t(d, v2)
    probs, dscore = [], []
    for h in range(2):
        s = jnp.where(allowed, scores[:, 128 * h : 128 * h + 128], NEG)
        e = jnp.exp(s - jnp.max(s, axis=-1, keepdims=True))
        p = e * (1.0 / jnp.sum(e, axis=-1, keepdims=True))
        dp = dprob[:, 128 * h : 128 * h + 128]
        delta = jnp.sum(p * dp, axis=-1, keepdims=True)
        probs.append(p.astype(BF))
        dscore.append((p * (dp - delta)).astype(BF))
    probs = jnp.concatenate(probs, axis=1)
    dscore = jnp.concatenate(dscore, axis=1)
    out = jnp.dot(probs, v2, preferred_element_type=F32)
    dq = jnp.dot(dscore, k2, preferred_element_type=F32) * FACTOR
    d2 = jnp.concatenate([jnp.where(first, d, zero), jnp.where(first, zero, d)], axis=0)
    q2 = jnp.concatenate([jnp.where(first, q, zero), jnp.where(first, zero, q)], axis=0)
    dv = jnp.dot(turned(probs), d2, preferred_element_type=F32)
    dk = jnp.dot(turned(dscore), q2, preferred_element_type=F32)
    return out, dq, dk, dv


def sublayer_kernel(
    tok, og, qkvw, outw, gain, perms,
    tgrad, gq, go, gg,
    order, xin, sbuf, recv, wown, wout, wt, ow, xs, normed, norm_t, og_t, proj, back, ao, part, other, rsib,
    tg, gacc, gvec, gvecr, gcol, sret, rret, blk, grads, gf, gn, ggr, gz, gzr, gzg, gzgr, gxs, gxr, gxg, gxgr,
    loc, ploc, kloc, wloc, oloc, zloc, gloc,
    asend, arecv, fsend, frecv, ssend, srecv, qsend, qrecv, usend, urecv, wsend, wrecv, bsend, brecv, vsend, vrecv,
    csend, crecv, psend, precv, rsend, rrecv, y1send, y1recv, y2send, y2recv, gsend, grecv,
    zsend, zrecv, xsend, xrecv, hsend, hrecv,
):
    f, m = lax.axis_index("frame"), lax.axis_index("mlp")
    g, c, z, x = f // 2, f % 2, m // 4, m % 4
    zh, y = f // 8, (f // 2) % 4
    zi = zh * 2 + z
    sib = g * 2 + 1 - c
    mz = (1 - z) * 4 + x
    xl, xr, xf = (x + 3) % 4, (x + 1) % 4, (x + 2) % 4
    mr, ml = z * 4 + xr, z * 4 + xl
    yl, yr, yf = (y + 3) % 4, (y + 1) % 4, (y + 2) % 4
    fr, fl = (zh * 4 + yr) * 2 + c, (zh * 4 + yl) * 2 + c
    own = c == z
    start = (zi + 5 + 3 * z) % 8
    me = (3 - 3 * z) * 4 + y

    def window(lo, h):
        return (zh + 3 - 2 * lo + h) % 4

    def owner(slot):
        to = (start + slot // 4) % 8
        return ((to // 2) * 4 + slot % 4) * 2 + c, (to % 2) * 4 + x

    def source(n):
        there = n // 4
        d = (there + 4 - zh) % 4
        lo = (d % 2) * (d // 2) + (1 - d % 2) * ((d // 2) * (1 - z) + (1 - d // 2) * z)
        place = (zi + 16 - (there * 2 + lo + 5 + 3 * lo)) % 8
        return n * 2 + c, lo * 4 + x, place * 4 + y

    p_in = [pltpu.make_async_copy(perms.at[pl.ds(0, 1)], order.at[pl.ds(0, 1)], ploc.at[0])]
    p_in.append(pltpu.make_async_copy(perms.at[pl.ds(1, 3)], order.at[pl.ds(1, 3)], ploc.at[1]))
    p_in[0].start()
    w_in = [pltpu.make_async_copy(qkvw.at[j], wown.at[:, pl.ds(128 * j, 128)], loc.at[j]) for j in range(3)]
    w_in.append(pltpu.make_async_copy(outw, ow, loc.at[3]))
    for copy in w_in:
        copy.start()
    x_in = []
    for ch in range(2):
        for t, ref in enumerate((tok, og)):
            for h in range(2):
                rows = pl.ds(pl.multiple_of(x * 64 + window(z, h) * 16, 16), 16)
                x_in.append(
                    pltpu.make_async_copy(
                        ref.at[pl.ds(6 * ch, 6), rows, :],
                        xin.at[ch, t, :, pl.ds(16 * h, 16), :],
                        loc.at[4 + 4 * ch + 2 * t + h],
                    )
                )
                x_in[-1].start()

    p_in[1].start()
    barrier = pltpu.get_barrier_semaphore()

    def hello_plane(k, _):
        n = (zi * 4 + y + k) % 32
        greet(barrier, ((n // 8) * 4 + n % 4) * 2 + c, ((n // 4) % 2) * 4 + x)
        return 0

    def hello_other(k, _):
        greet(barrier, ((k // 2) * 4 + y) * 2 + 1 - c, (k % 2) * 4 + x)
        return 0

    lax.fori_loop(1, 32, hello_plane, 0)
    lax.fori_loop(0, 8, hello_other, 0)
    for k in range(1, 4):
        greet(barrier, f, z * 4 + (x + k) % 4)

    for copy in w_in:
        copy.wait()
    wown[:, 384:512] = ow[...].T
    p_in[0].wait()

    def pack(ch):
        for copy in x_in[4 * ch : 4 * ch + 4]:
            copy.wait()
        for gh in range(2):
            rows = slice(16 * gh, 16 * gh + 16)
            parts = [xin[ch, t, :, rows, 512 * h : 512 * h + 512].reshape(96, 512) for h in range(2) for t in range(2)]
            packed = jnp.dot(order[0], jnp.concatenate(parts, axis=0), preferred_element_type=F32)
            sbuf[ch, 8 * gh : 8 * gh + 8] = packed.astype(BF).reshape(8, 48, 512)

    pack(0)
    pl.semaphore_wait(barrier, 42)

    half = (pl.ds(0, 384), pl.ds(384, 384))
    strip = pl.ds(pl.multiple_of(768 + 64 * y, 64), 64)
    w_pairs = ((1, 0), (1, 1), (2, 1), (2, 0), (3, 0), (3, 1))

    def w_ring(src, slot, n, to):
        i, h = w_pairs[n]
        return remote(src, wout.at[slot, half[h]], wsend.at[n], wrecv.at[i, h], f, to)

    def w_spread(src, h):
        if h == 0:
            w_ring(src.at[half[0]], x, 0, mr).start()
            w_ring(src.at[half[0]], x, 3, ml).start()
        else:
            w_ring(src.at[half[1]], x, 2, ml).start()
            w_ring(src.at[half[1]], x, 1, mr).start()

    def swap(h):
        rows = (half[0], half[1], strip)[h]
        return remote(wown.at[rows], wout.at[x, rows], ssend.at[h], srecv.at[h], g * 2 + 1 - c, mz)

    def strip_x(src, k):
        return remote(src.at[strip], wout.at[x, strip], qsend.at[k], qrecv.at[k], f, z * 4 + (x + k) % 4)

    def strip_y(k):
        to = (zh * 4 + (y + k) % 4) * 2 + c
        return remote(wout.at[:, strip], wout.at[:, strip], usend.at[k], urecv.at[k], to, m)

    own_w = [
        pltpu.make_async_copy(wown.at[pl.ds(0, 768)], wout.at[x, pl.ds(0, 768)], wloc.at[0]),
        pltpu.make_async_copy(wown.at[strip], wout.at[x, strip], wloc.at[1]),
    ]

    @pl.when(own)
    def _():
        own_w[1].start()
        for k in range(1, 4):
            strip_x(wown, k).start()
        w_spread(wown, 0)
        w_spread(wown, 1)
        own_w[0].start()

    @pl.when(jnp.logical_not(own))
    def _():
        swap(2).start()
        swap(0).start()
        swap(1).start()

    def a2a(ch, k):
        slot = (me + k) % 16
        return remote(sbuf.at[ch, slot], recv.at[ch, c, g], asend.at[ch, k], arecv.at[ch, g], *owner(slot))

    def forward(ch, k, src):
        slot = (g + 16 - k) % 16
        return remote(src, recv.at[ch, c, slot], fsend.at[ch, k], frecv.at[ch, k], sib, m)

    def keep(ch):
        return pltpu.make_async_copy(sbuf.at[ch, me], recv.at[ch, c, g], kloc.at[ch])

    for ch in range(2):
        if ch:
            pack(ch)

        def send(k, _, ch=ch):
            a2a(ch, k).start()
            return 0

        lax.fori_loop(1, 16, send, 0)
        keep(ch).start()
        forward(ch, 0, sbuf.at[ch, me]).start()

        if ch == 0:

            @pl.when(jnp.logical_not(own))
            def _():
                swap(2).wait_recv()
                for k in range(1, 4):
                    strip_x(wout.at[x], k).start()

    @pl.when(own)
    def _():
        own_w[1].wait()

    for k in range(1, 4):
        remote(wown.at[strip], wout.at[(x + 4 - k) % 4, strip], qsend.at[k], qrecv.at[k], f, m).wait_recv()
    for k in range(1, 4):
        strip_y(k).start()

    @pl.when(jnp.logical_not(own))
    def _():
        swap(0).wait_recv()
        w_spread(wout.at[x], 0)
        swap(1).wait_recv()
        w_spread(wout.at[x], 1)

    def w_arrived(n):
        i, h = w_pairs[n]
        slot = (x, xl, xr, xf)[i]
        remote(wown.at[half[h]], wout.at[slot, half[h]], wsend.at[n], wrecv.at[i, h], f, mr).wait_recv()

    def relay_tokens(ch):
        def relay(k, _):
            slot = (g + 16 - k) % 16
            remote(sbuf.at[ch, 0], recv.at[ch, c, slot], asend.at[ch, k], arecv.at[ch, slot], f, m).wait_recv()
            forward(ch, k, recv.at[ch, c, slot]).start()
            return 0

        lax.fori_loop(1, 16, relay, 0)

    def tokens_arrived(ch):
        keep(ch).wait()

        def wait(k, _):
            slot = (g + 16 - k) % 16
            remote(sbuf.at[ch, 0], recv.at[ch, 1 - c, slot], fsend.at[ch, k], frecv.at[ch, k], f, m).wait_recv()
            return 0

        lax.fori_loop(0, 16, wait, 0)

    relay_tokens(0)
    w_arrived(0)
    w_ring(wout.at[xl, half[0]], xl, 4, mr).start()
    w_arrived(2)
    w_ring(wout.at[xr, half[1]], xr, 5, ml).start()

    lane = lax.broadcasted_iota(jnp.int32, (128, 128), 1)
    line = lax.broadcasted_iota(jnp.int32, (128, 128), 0)
    first = lane < 64
    allowed = (lane < 64) == (line < 64)

    def shard_of(i):
        return (x + (i % 2) * 3 + (i // 2) * (1 + (i % 2) * 2)) % 4

    def prepare(ch):
        for s in range(2):
            for gh in range(2):
                block = recv[ch, s, 8 * gh : 8 * gh + 8].reshape(384, 512)
                rows = jnp.dot(order[1], block, preferred_element_type=F32).astype(BF).reshape(2, 2, 6, 16, 512)
                for h in range(2):
                    xs[ch, :, :, s, 16 * gh : 16 * gh + 16, 512 * h : 512 * h + 512] = rows[h]

        def norm(u, _):
            xhat, _ = standardize(xs[ch, 0, u].reshape(64, D).astype(F32))
            normed[pl.ds(pl.multiple_of(ch * 384 + u * 64, 64), 64), :] = (xhat * gain[...]).astype(BF)
            return 0

        lax.fori_loop(0, 6, norm, 0, unroll=2)
        for i in range(3):
            at = 384 * ch + 128 * i
            norm_t[:, at : at + 128] = normed[at : at + 128, :].T
            og_t[:, at : at + 128] = xs[ch, 1, 2 * i : 2 * i + 2].reshape(128, D).T

    def heads(ch, i):
        j = shard_of(i)
        at = 384 * ch
        if ch == 0:
            wt[i] = wout[j, :, 0:384].T
        proj[:, 0:384] = jnp.dot(normed[at : at + 384, :], wout[j, :, 0:384], preferred_element_type=F32).astype(BF)
        proj[:, 384:512] = jnp.dot(
            xs[ch, 1].reshape(384, D), wout[j, :, 384:512], preferred_element_type=F32
        ).astype(BF)
        for n in range(3):
            rows = slice(128 * n, 128 * n + 128)
            out, dq, dk, dv = attend(
                proj[rows, 0:128], proj[rows, 128:256], proj[rows, 256:384], proj[rows, 384:512], allowed, first
            )
            rows = slice(at + 128 * n, at + 128 * n + 128)
            back[i, rows, 0:128] = dq.astype(BF)
            back[i, rows, 128:256] = dk.astype(BF)
            back[i, rows, 256:384] = dv.astype(BF)
            ao[i, rows, :] = out.astype(BF)

    def to_sibling(ch):
        return remote(other.at[ch], rsib.at[ch], bsend.at[ch], brecv.at[ch], sib, m)

    def partial(ch, groups):
        for n in range(3):
            rows = slice(384 * ch + 128 * n, 384 * ch + 128 * n + 128)
            term = jnp.dot(back[groups[0], rows, :], wt[groups[0]], preferred_element_type=F32)
            for i in groups[1:]:
                term += jnp.dot(back[i, rows, :], wt[i], preferred_element_type=F32)
            term = term.reshape(2, 2, 32, D)
            if groups[0] == 0:
                part[2 * n : 2 * n + 2] = term
            else:
                part[2 * n : 2 * n + 2] += term
        if groups[-1] == 3:
            other[ch] = part[:, 1 - c].astype(BF)
            to_sibling(ch).start()

    def back_to(ch, k):
        n = (g + k) % 16
        fs, ms, slot = source(n)
        return remote(sret.at[ch, n], rret.at[ch, slot], csend.at[ch, k], crecv.at[ch, slot], fs, ms)

    def keep_back(ch):
        return pltpu.make_async_copy(sret.at[ch, g], rret.at[ch, me], kloc.at[2 + ch])

    def token_gradient(ch):
        to_sibling(ch).wait_recv()

        def token(u, total):
            xhat, rstd = standardize(xs[ch, 0, u, c].astype(F32))
            dn = part[u, c] + rsib[ch, u].astype(F32)
            bp = dn * gain[...]
            inner = bp - jnp.mean(bp, axis=-1, keepdims=True) - xhat * jnp.mean(bp * xhat, axis=-1, keepdims=True)
            tg[u] = (xs[ch, 1, u, c].astype(F32) + rstd * inner).astype(BF)
            return total + jnp.sum((dn * xhat).reshape(4, 8, D), axis=0)

        total = lax.fori_loop(0, 6, token, jnp.zeros((8, D), F32), unroll=2)
        if ch == 0:
            gacc[...] = total
        else:
            gacc[...] += total
        for gh in range(2):
            rows = slice(16 * gh, 16 * gh + 16)
            parts = [tg[:, rows, 256 * h : 256 * h + 256].reshape(96, 256) for h in range(4)]
            packed = jnp.dot(order[2], jnp.concatenate(parts, axis=0), preferred_element_type=F32)
            sret[ch, 8 * gh : 8 * gh + 8] = packed.astype(BF).reshape(8, 48, 256)

        def send(k, _):
            back_to(ch, k).start()
            return 0

        lax.fori_loop(1, 16, send, 0)
        keep_back(ch).start()

    def piece(ch, h, mm):
        rows = pl.ds(pl.multiple_of((mm % 4) * 64 + window(mm // 4, h) * 16, 16), 16)
        return tgrad.at[pl.ds(6 * ch, 6), rows, :]

    def kept(ch, h):
        return blk.at[ch, :, pl.ds(16 * h, 16), :]

    def pair(ch, h):
        return remote(kept(ch, h), piece(ch, h, m), psend.at[ch, h], precv.at[ch, h], f, mz)

    def ring(ch, r, src, mm, h, n, to):
        return remote(src, piece(ch, h, mm), rsend.at[ch, r, n], rrecv.at[ch, r, n], f, to)

    def own_out(ch, h):
        return pltpu.make_async_copy(kept(ch, h), piece(ch, h, m), oloc.at[ch, h])

    def gather_own(ch):
        keep_back(ch).wait()

        def received(k, _):
            slot = (me + k) % 16
            remote(sret.at[ch, 0], rret.at[ch, slot], csend.at[ch, k], crecv.at[ch, slot], f, m).wait_recv()
            return 0

        lax.fori_loop(1, 16, received, 0)
        for gh in range(2):
            block = rret[ch, 8 * gh : 8 * gh + 8].reshape(384, 256)
            rows = jnp.dot(order[3], block, preferred_element_type=F32).astype(BF).reshape(4, 6, 16, 256)
            for h in range(4):
                blk[ch, :, 16 * gh : 16 * gh + 16, 256 * h : 256 * h + 256] = rows[h]
        pair(ch, 0).start()
        pair(ch, 1).start()
        ring(ch, 0, kept(ch, 0), m, 0, 0, mr).start()
        ring(ch, 0, kept(ch, 1), m, 1, 2, ml).start()
        ring(ch, 0, kept(ch, 1), m, 1, 1, mr).start()
        ring(ch, 0, kept(ch, 0), m, 0, 3, ml).start()
        own_out(ch, 0).start()
        own_out(ch, 1).start()

    def gather_pair(ch):
        def arrived(h):
            remote(kept(ch, h), piece(ch, h, mz), psend.at[ch, h], precv.at[ch, h], f, mz).wait_recv()

        arrived(0)
        ring(ch, 1, piece(ch, 0, mz), mz, 0, 0, mr).start()
        ring(ch, 1, piece(ch, 0, mz), mz, 0, 3, ml).start()
        arrived(1)
        ring(ch, 1, piece(ch, 1, mz), mz, 1, 2, ml).start()
        ring(ch, 1, piece(ch, 1, mz), mz, 1, 1, mr).start()

    def base(r):
        return (z if r == 0 else 1 - z) * 4

    def arrived(ch, r, mm, h, n):
        ring(ch, r, piece(ch, h, base(r) + mm), base(r) + mm, h, n, mr).wait_recv()

    def gather_relay(ch, r):
        arrived(ch, r, xl, 0, 0)
        ring(ch, r, piece(ch, 0, base(r) + xl), base(r) + xl, 0, 4, mr).start()
        arrived(ch, r, xr, 1, 2)
        ring(ch, r, piece(ch, 1, base(r) + xr), base(r) + xr, 1, 5, ml).start()

    def weights(i):
        j = shard_of(i)

        left = jnp.dot(norm_t[...], back[i], preferred_element_type=F32).astype(BF)
        grads[j, :, :, :, :, 0:384] = left.reshape(4, 4, 2, 32, 384)
        left = jnp.dot(og_t[...], ao[i], preferred_element_type=F32).astype(BF)
        grads[j, :, :, :, :, 384:512] = left.reshape(4, 4, 2, 32, 128)
        y_far(i, 0).start()
        y_far(i, 1).start()

    def y_far(i, h):
        src = grads.at[shard_of(i), pl.ds(2 * h, 2), yf]
        return remote(src, gf.at[i, h], y1send.at[i, h], y1recv.at[i, h], fr if h == 0 else fl, m)

    def y_near(i, h):
        src = grads.at[shard_of(i), :, yr if h == 0 else yl]
        return remote(src, gn.at[i, h], y2send.at[i, h], y2recv.at[i, h], fr if h == 0 else fl, m)

    def y_step(i, _):
        j = shard_of(i)
        for h in range(2):
            y_far(i, h).wait_recv()
            to = yr if h == 0 else yl
            for a in range(2):
                total = grads[j, 2 * h + a, to].astype(F32) + gf[i, h, a].astype(F32)
                grads[j, 2 * h + a, to] = total.astype(BF)
            y_near(i, h).start()
        return 0

    def z_copy(i, n):
        to = ((n // 2) * 4 + y) * 2 + n % 2
        return remote(gz.at[i, n], gzr.at[i, zi], zsend.at[i, n], zrecv.at[i, zi], to, c * 4 + x)

    def zg_copy(n):
        to = ((n // 2) * 4 + y) * 2 + n % 2
        return remote(gzg.at[n], gzgr.at[zi], zsend.at[4, n], zrecv.at[4, zi], to, c * 4 + x)

    def z_self(n):
        return jnp.logical_and(n == zh * 2 + c, own)

    def own_z(i):
        return pltpu.make_async_copy(gz.at[i, zh * 2 + c], gzr.at[i, zi], zloc.at[i])

    def own_zg():
        return pltpu.make_async_copy(gzg.at[zh * 2 + c], gzgr.at[zi], zloc.at[4])

    def z_step(i, _):
        j = shard_of(i)
        for h in range(2):
            y_near(i, h).wait_recv()
        for a in range(4):
            total = grads[j, a, y].astype(F32) + (gn[i, 0, a].astype(F32) + gn[i, 1, a].astype(F32))
            gz[i, 2 * a : 2 * a + 2] = total.astype(BF)

        def z_send(n, _):
            @pl.when(jnp.logical_not(z_self(n)))
            def _():
                z_copy(i, n).start()

            return 0

        lax.fori_loop(0, 8, z_send, 0)

        @pl.when(own)
        def _():
            own_z(i).start()

        return 0

    def z_wait(i, src, dst):
        def wait(n, _):
            @pl.when(jnp.logical_not(jnp.logical_and(n == zi, own)))
            def _():
                remote(src, dst(n), zsend.at[i, 0], zrecv.at[i, n], f, m).wait_recv()

            return 0

        lax.fori_loop(0, 8, wait, 0)

    def sum8(terms):
        while len(terms) > 1:
            terms = [a + b for a, b in zip(terms[::2], terms[1::2])]
        return terms[0]

    def x_copy(i):
        return remote(gxs.at[i], gxr.at[i], xsend.at[i], xrecv.at[i], f, z * 4 + shard_of(i))

    def x_step(i, _):
        z_wait(i, gz.at[0, 0], lambda n: gzr.at[i, n])

        @pl.when(own)
        def _():
            own_z(i).wait()

        gxs[i] = sum8([gzr[i, k].astype(F32) for k in range(8)]).astype(BF)

        @pl.when(jnp.asarray(i) > 0)
        def _():
            x_copy(i).start()

        return 0

    def gain_y(k):
        yk = (y + k) % 4
        return remote(gcol.at[:, yk], ggr.at[k], gsend.at[k], grecv.at[k], (zh * 4 + yk) * 2 + c, m)

    own_gain = pltpu.make_async_copy(gcol.at[:, y], ggr.at[0], gloc)

    def gain_x(k):
        return remote(gxg, gxgr.at[k], hsend.at[k], hrecv.at[k], f, z * 4 + (x + k) % 4)

    to_sib_gain = remote(gvec, gvecr, vsend, vrecv, sib, m)

    def sent_early():
        for ch in range(2):
            pair(ch, 0).wait_send()
            pair(ch, 1).wait_send()
            own_out(ch, 0).wait()
            own_out(ch, 1).wait()
            to_sibling(ch).wait_send()

            def sent(k, _, ch=ch):
                a2a(ch, k).wait_send()
                back_to(ch, k).wait_send()
                forward(ch, k, recv.at[ch, c, (g + 16 - k) % 16]).wait_send()
                return 0

            lax.fori_loop(1, 16, sent, 0)
            forward(ch, 0, sbuf.at[ch, me]).wait_send()
        to_sib_gain.wait_send()
        for n in range(6):
            i, h = w_pairs[n]
            w_ring(wown.at[half[h]], x, n, mr).wait_send()

        @pl.when(jnp.logical_not(own))
        def _():
            for h in range(3):
                swap(h).wait_send()

        for k in range(1, 4):
            gain_y(k).wait_send()
            strip_x(wown, k).wait_send()
            strip_y(k).wait_send()

        def y_sent(i, _):
            for h in range(2):
                y_far(i, h).wait_send()
                y_near(i, h).wait_send()
            return 0

        lax.fori_loop(0, 4, y_sent, 0)

        def z_sent(n, _):
            @pl.when(jnp.logical_not(z_self(n)))
            def _():
                for i in range(4):
                    z_copy(i, n).wait_send()
                zg_copy(n).wait_send()

            return 0

        lax.fori_loop(0, 8, z_sent, 0)

    p_in[1].wait()
    tokens_arrived(0)
    prepare(0)

    @pl.when(own)
    def _():
        own_w[0].wait()

    for k in range(1, 4):
        rows = pl.ds(pl.multiple_of(768 + 64 * ((y + 4 - k) % 4), 64), 64)
        remote(wout.at[:, rows], wout.at[:, rows], usend.at[k], urecv.at[k], f, m).wait_recv()

    def shard_arrived(i):
        for h in range(2):
            waited = jnp.logical_or(i == 0, jnp.logical_and(i < 3, h == i - 1))

            @pl.when(jnp.logical_not(waited))
            def _():
                slot = shard_of(i)
                remote(wown.at[half[h]], wout.at[slot, half[h]], wsend.at[0], wrecv.at[i, h], f, mr).wait_recv()

    def first_heads(i, _):
        shard_arrived(i)
        heads(0, i)

        @pl.when(i == 2)
        def _():
            partial(0, (0, 1, 2))
            relay_tokens(1)

        return 0

    def second_heads(i, _):
        heads(1, i)

        @pl.when(i == 0)
        def _():
            token_gradient(0)

        return 0

    def y_steps(first, last):
        lax.fori_loop(first, last, lambda i, _: y_step((i + 1) % 4, 0), 0)

    def z_steps(first, last):
        lax.fori_loop(first, last, lambda i, _: z_step((i + 1) % 4, 0), 0)

    lax.fori_loop(0, 4, first_heads, 0)
    partial(0, (3,))
    tokens_arrived(1)
    prepare(1)
    lax.fori_loop(0, 4, second_heads, 0)
    partial(1, (0, 1, 2, 3))
    weights(1)
    token_gradient(1)
    gvec[...] = jnp.broadcast_to(jnp.sum(gacc[...], axis=0, keepdims=True), (8, D))
    to_sib_gain.start()
    gather_own(0)
    weights(2)
    weights(3)
    weights(0)
    gather_pair(0)
    y_steps(0, 1)
    y_steps(1, 2)
    gather_relay(0, 0)
    to_sib_gain.wait_recv()
    gcol[...] = jnp.broadcast_to(gvec[0:1] + gvecr[0:1], (128, D)).T.astype(BF).reshape(4, 4, 2, 32, 128)
    for k in range(1, 4):
        gain_y(k).start()
    own_gain.start()
    y_steps(2, 3)
    gather_own(1)
    y_steps(3, 4)
    z_steps(0, 1)
    gather_pair(1)
    z_steps(1, 2)
    gather_relay(0, 1)
    own_gain.wait()
    for k in range(1, 4):
        remote(ggr.at[0], ggr.at[k], gsend.at[k], grecv.at[k], f, m).wait_recv()
    total = sum8([ggr[k].astype(F32) for k in range(4)])
    gzg[...] = total.astype(BF).reshape(8, 32, 128)

    def zg_send(n, _):
        @pl.when(jnp.logical_not(z_self(n)))
        def _():
            zg_copy(n).start()

        return 0

    lax.fori_loop(0, 8, zg_send, 0)

    @pl.when(own)
    def _():
        own_zg().start()

    gather_relay(1, 0)
    z_steps(2, 4)
    lax.fori_loop(1, 4, x_step, 0)
    z_wait(4, gzg.at[0], lambda n: gzgr.at[n])

    @pl.when(own)
    def _():
        own_zg().wait()

    gxg[...] = sum8([gzgr[k].astype(F32) for k in range(8)]).astype(BF)
    for k in range(1, 4):
        gain_x(k).start()
    gather_relay(1, 1)
    x_step(0, 0)
    sent_early()

    for i in range(1, 4):
        x_copy(i).wait_recv()
    total = sum8([gxs[0].astype(F32)] + [gxr[i].astype(F32) for i in range(1, 4)])
    for j in range(3):
        gq[j] = total[:, 128 * j : 128 * j + 128]
    go[...] = total[:, 384:512]
    for k in range(1, 4):
        gain_x(k).wait_recv()
    total = sum8([gxg[...].astype(F32)] + [gxgr[k].astype(F32) for k in range(1, 4)])
    gg[...] = jnp.broadcast_to(total[0:32, 0:1], (32, 128))

    for ch in range(2):
        for r in range(2):
            arrived(ch, r, xl, 1, 1)
            arrived(ch, r, xr, 0, 3)
            arrived(ch, r, xf, 0, 4)
            arrived(ch, r, xf, 1, 5)
            for n, (mm, h) in enumerate(((x, 0), (x, 1), (x, 1), (x, 0), (xl, 0), (xr, 1))):
                ring(ch, r, piece(ch, h, base(r) + mm), base(r) + mm, h, n, mr).wait_send()
    for k in range(1, 4):
        gain_x(k).wait_send()
        x_copy(k).wait_send()


def sublayer(tok, og, qkvw, outw, gain):
    vm = pl.BlockSpec(memory_space=pltpu.VMEM)
    hbm = pl.BlockSpec(memory_space=pltpu.HBM)
    dma = pltpu.SemaphoreType.DMA
    perms = jnp.asarray(np.stack([PACK, GROUP, REPACK, UNPACK]), BF)
    bf = lambda *shape: pltpu.VMEM(shape, BF)
    return pl.pallas_call(
        sublayer_kernel,
        out_shape=(
            jax.ShapeDtypeStruct((12, 256, D), BF),
            jax.ShapeDtypeStruct((3, 32, 128), F32),
            jax.ShapeDtypeStruct((32, 128), F32),
            jax.ShapeDtypeStruct((32, 128), F32),
        ),
        in_specs=[hbm] * 4 + [vm, hbm],
        out_specs=(hbm, vm, vm, vm),
        scratch_shapes=[
            bf(4, 384, 384),
            bf(2, 2, 6, 32, D),
            bf(2, 16, 48, 512),
            bf(2, 2, 16, 48, 512),
            bf(D, 512),
            bf(4, D, 512),
            bf(4, 384, D),
            bf(128, D),
            bf(2, 2, 6, 2, 32, D),
            bf(768, D),
            bf(D, 768),
            bf(D, 768),
            bf(384, 512),
            bf(4, 768, 384),
            bf(4, 768, 128),
            pltpu.VMEM((6, 2, 32, D), F32),
            bf(2, 6, 32, D),
            bf(2, 6, 32, D),
            bf(6, 32, D),
            pltpu.VMEM((8, D), F32),
            pltpu.VMEM((8, D), F32),
            pltpu.VMEM((8, D), F32),
            bf(4, 4, 2, 32, 128),
            bf(2, 16, 48, 256),
            bf(2, 16, 48, 256),
            bf(2, 6, 32, D),
            bf(4, 4, 4, 2, 32, 512),
            bf(4, 2, 2, 2, 32, 512),
            bf(4, 2, 4, 2, 32, 512),
            bf(4, 4, 2, 32, 128),
            bf(4, 8, 32, 512),
            bf(4, 8, 32, 512),
            bf(8, 32, 128),
            bf(8, 32, 128),
            bf(4, 32, 512),
            bf(4, 32, 512),
            bf(32, 128),
            bf(4, 32, 128),
            dma((12,)),
            dma((2,)),
            dma((4,)),
            dma((2,)),
            dma((2, 2)),
            dma((5,)),
            dma,
            dma((2, 16)),
            dma((2, 16)),
            dma((2, 16)),
            dma((2, 16)),
            dma((3,)),
            dma((3,)),
            dma((4,)),
            dma((4,)),
            dma((4,)),
            dma((4,)),
            dma((6,)),
            dma((4, 2)),
            dma((2,)),
            dma((2,)),
            dma,
            dma,
            dma((2, 16)),
            dma((2, 16)),
            dma((2, 2)),
            dma((2, 2)),
            dma((2, 2, 6)),
            dma((2, 2, 6)),
            dma((4, 2)),
            dma((4, 2)),
            dma((4, 2)),
            dma((4, 2)),
            dma((4,)),
            dma((4,)),
            dma((5, 8)),
            dma((5, 8)),
            dma((4,)),
            dma((4,)),
            dma((4,)),
            dma((4,)),
        ],
        compiler_params=pltpu.CompilerParams(
            collective_id=0, has_side_effects=True, vmem_limit_bytes=58 * 2**20
        ),
        name="sublayer",
    )(tok, og, qkvw, outw, gain, perms)


def finish_kernel(tgrad, gq, go, gg, out, oq, oo, og, buf, insem, outsem):
    into = [pltpu.make_async_copy(tgrad.at[pl.ds(2 * n, 2)], buf.at[pl.ds(2 * n, 2)], insem.at[n]) for n in range(6)]
    away = [pltpu.make_async_copy(buf.at[pl.ds(2 * n, 2)], out.at[pl.ds(2 * n, 2)], outsem.at[n]) for n in range(6)]
    for copy in into:
        copy.start()
    oq[...] = gq[...]
    oo[...] = go[...]
    og[...] = gg[...].T[0:1, :]
    for n in range(6):
        into[n].wait()
        away[n].start()
    for copy in away:
        copy.wait()


def finish(tgrad, gq, go, gg):
    vm = pl.BlockSpec(memory_space=pltpu.VMEM)
    hbm = pl.BlockSpec(memory_space=pltpu.HBM)
    return pl.pallas_call(
        finish_kernel,
        out_shape=(
            jax.ShapeDtypeStruct((12, 256, D), BF),
            jax.ShapeDtypeStruct((3, 32, 128), F32),
            jax.ShapeDtypeStruct((32, 128), F32),
            jax.ShapeDtypeStruct((1, 32), F32),
        ),
        in_specs=[hbm, vm, vm, vm],
        out_specs=(hbm, vm, vm, vm),
        scratch_shapes=[
            pltpu.VMEM((12, 256, D), BF),
            pltpu.SemaphoreType.DMA((6,)),
            pltpu.SemaphoreType.DMA((6,)),
        ],
        compiler_params=pltpu.CompilerParams(vmem_limit_bytes=58 * 2**20),
        name="finish",
    )(tgrad, gq, go, gg)


def shards(tokens, output_gradient, gain, qkv_weight, out_weight):
    clips, frames, patches, width = tokens.shape
    results = sublayer(
        tokens.reshape(12, 256, D),
        output_gradient.reshape(12, 256, D),
        jnp.transpose(qkv_weight, (1, 0, 2)),
        out_weight,
        gain.reshape(1, D),
    )
    tgrad, gq, go, gg = finish(*results)
    return (
        tgrad.reshape(clips, frames, patches, width),
        jnp.transpose(gq, (1, 0, 2)),
        go.T,
        gg.reshape(32),
    )


def solution(mesh):
    in_specs = (
        P(None, "frame", None, None),
        P(None, "frame", None, None),
        P(),
        P(None, None, "mlp"),
        P("mlp", None),
    )
    out_specs = (
        P(None, "frame", None, None),
        P("frame", None, "mlp"),
        P("mlp", "frame"),
        P("frame"),
    )
    return jax.shard_map(shards, mesh=mesh, in_specs=in_specs, out_specs=out_specs, check_vma=False)
```

```python
import numpy as np

import jax
import jax.numpy as jnp
from jax import lax
from jax.experimental import pallas as pl
from jax.experimental.pallas import tpu as pltpu
from jax.sharding import PartitionSpec as P

MESH = pl.DeviceIdType.MESH
BF = jnp.bfloat16
F32 = jnp.float32
D = 1024
FACTOR = 64 ** (-0.5)
NEG = -1e30


def one_hot(shape, perm):
    index = np.arange(384).reshape(shape).transpose(perm).reshape(-1)
    return np.eye(384, dtype=np.float32)[index]


PACK = one_hot((2, 2, 6, 8, 2), (3, 0, 1, 4, 2))
GROUP = one_hot((8, 2, 2, 6, 2), (1, 2, 3, 0, 4))
REPACK = one_hot((4, 6, 8, 2), (2, 0, 1, 3))
UNPACK = one_hot((8, 4, 2, 6), (1, 3, 0, 2))


def remote(src, dst, send, recv, f, m):
    return pltpu.make_async_remote_copy(
        src_ref=src, dst_ref=dst, send_sem=send, recv_sem=recv, device_id=(f, m), device_id_type=MESH
    )


def greet(barrier, f, m):
    pl.semaphore_signal(barrier, inc=1, device_id=(f, m), device_id_type=MESH)


def standardize(values):
    centered = values - jnp.mean(values, axis=-1, keepdims=True)
    rstd = lax.rsqrt(jnp.mean(centered * centered, axis=-1, keepdims=True) + 1e-05)
    return centered * rstd, rstd


def dot_t(a, b):
    return lax.dot_general(a, b, (((1,), (1,)), ((), ())), preferred_element_type=F32)


def turned(a):
    return jnp.concatenate([a[:, :128].T, a[:, 128:].T], axis=1)


def attend(q, k, v, d, allowed, first):
    zero = jnp.zeros_like(k)
    k2 = jnp.concatenate([jnp.where(first, k, zero), jnp.where(first, zero, k)], axis=0)
    v2 = jnp.concatenate([jnp.where(first, v, zero), jnp.where(first, zero, v)], axis=0)
    q = q * FACTOR
    scores = dot_t(q, k2)
    dprob = dot_t(d, v2)
    probs, dscore = [], []
    for h in range(2):
        s = jnp.where(allowed, scores[:, 128 * h : 128 * h + 128], NEG)
        e = jnp.exp(s - jnp.max(s, axis=-1, keepdims=True))
        p = e * (1.0 / jnp.sum(e, axis=-1, keepdims=True))
        dp = dprob[:, 128 * h : 128 * h + 128]
        delta = jnp.sum(p * dp, axis=-1, keepdims=True)
        probs.append(p.astype(BF))
        dscore.append((p * (dp - delta)).astype(BF))
    probs = jnp.concatenate(probs, axis=1)
    dscore = jnp.concatenate(dscore, axis=1)
    out = jnp.dot(probs, v2, preferred_element_type=F32)
    dq = jnp.dot(dscore, k2, preferred_element_type=F32) * FACTOR
    d2 = jnp.concatenate([jnp.where(first, d, zero), jnp.where(first, zero, d)], axis=0)
    q2 = jnp.concatenate([jnp.where(first, q, zero), jnp.where(first, zero, q)], axis=0)
    dv = jnp.dot(turned(probs), d2, preferred_element_type=F32)
    dk = jnp.dot(turned(dscore), q2, preferred_element_type=F32)
    return out, dq, dk, dv


def sublayer_kernel(
    tok, og, qkvw, outw, gain, perms,
    tgrad, gq, go, gg,
    order, xin, sbuf, recv, wown, wout, wt, ow, xs, normed, norm_t, og_t, proj, back, ao, part, other, rsib,
    tg, gacc, gvec, gvecr, gcol, sret, rret, blk, grads, gf, gn, ggr, gz, gzr, gzg, gzgr, gxs, gxr, gxg, gxgr,
    loc, ploc, kloc, wloc, oloc, zloc, gloc,
    asend, arecv, fsend, frecv, ssend, srecv, qsend, qrecv, usend, urecv, wsend, wrecv, bsend, brecv, vsend, vrecv,
    csend, crecv, psend, precv, rsend, rrecv, y1send, y1recv, y2send, y2recv, gsend, grecv,
    zsend, zrecv, xsend, xrecv, hsend, hrecv,
):
    f, m = lax.axis_index("frame"), lax.axis_index("mlp")
    g, c, z, x = f // 2, f % 2, m // 4, m % 4
    zh, y = f // 8, (f // 2) % 4
    zi = zh * 2 + z
    sib = g * 2 + 1 - c
    mz = (1 - z) * 4 + x
    xl, xr, xf = (x + 3) % 4, (x + 1) % 4, (x + 2) % 4
    mr, ml = z * 4 + xr, z * 4 + xl
    yl, yr, yf = (y + 3) % 4, (y + 1) % 4, (y + 2) % 4
    fr, fl = (zh * 4 + yr) * 2 + c, (zh * 4 + yl) * 2 + c
    own = c == z
    start = (zi + 5 + 3 * z) % 8
    me = (3 - 3 * z) * 4 + y

    def window(lo, h):
        return (zh + 3 - 2 * lo + h) % 4

    def owner(slot):
        to = (start + slot // 4) % 8
        return ((to // 2) * 4 + slot % 4) * 2 + c, (to % 2) * 4 + x

    def source(n):
        there = n // 4
        d = (there + 4 - zh) % 4
        lo = (d % 2) * (d // 2) + (1 - d % 2) * ((d // 2) * (1 - z) + (1 - d // 2) * z)
        place = (zi + 16 - (there * 2 + lo + 5 + 3 * lo)) % 8
        return n * 2 + c, lo * 4 + x, place * 4 + y

    p_in = [pltpu.make_async_copy(perms.at[pl.ds(0, 1)], order.at[pl.ds(0, 1)], ploc.at[0])]
    p_in.append(pltpu.make_async_copy(perms.at[pl.ds(1, 3)], order.at[pl.ds(1, 3)], ploc.at[1]))
    p_in[0].start()
    w_in = [pltpu.make_async_copy(qkvw.at[j], wown.at[:, pl.ds(128 * j, 128)], loc.at[j]) for j in range(3)]
    w_in.append(pltpu.make_async_copy(outw, ow, loc.at[3]))
    for copy in w_in:
        copy.start()
    x_in = []
    for ch in range(2):
        for t, ref in enumerate((tok, og)):
            for h in range(2):
                rows = pl.ds(pl.multiple_of(x * 64 + window(z, h) * 16, 16), 16)
                x_in.append(
                    pltpu.make_async_copy(
                        ref.at[pl.ds(6 * ch, 6), rows, :],
                        xin.at[ch, t, :, pl.ds(16 * h, 16), :],
                        loc.at[4 + 4 * ch + 2 * t + h],
                    )
                )
                x_in[-1].start()

    p_in[1].start()
    barrier = pltpu.get_barrier_semaphore()

    def hello_plane(k, _):
        n = (zi * 4 + y + k) % 32
        greet(barrier, ((n // 8) * 4 + n % 4) * 2 + c, ((n // 4) % 2) * 4 + x)
        return 0

    def hello_other(k, _):
        greet(barrier, ((k // 2) * 4 + y) * 2 + 1 - c, (k % 2) * 4 + x)
        return 0

    lax.fori_loop(1, 32, hello_plane, 0)
    lax.fori_loop(0, 8, hello_other, 0)
    for k in range(1, 4):
        greet(barrier, f, z * 4 + (x + k) % 4)

    for copy in w_in:
        copy.wait()
    wown[:, 384:512] = ow[...].T
    p_in[0].wait()

    def pack(ch):
        for copy in x_in[4 * ch : 4 * ch + 4]:
            copy.wait()
        for gh in range(2):
            rows = slice(16 * gh, 16 * gh + 16)
            parts = [xin[ch, t, :, rows, 512 * h : 512 * h + 512].reshape(96, 512) for h in range(2) for t in range(2)]
            packed = jnp.dot(order[0], jnp.concatenate(parts, axis=0), preferred_element_type=F32)
            sbuf[ch, 8 * gh : 8 * gh + 8] = packed.astype(BF).reshape(8, 48, 512)

    pack(0)
    pl.semaphore_wait(barrier, 42)

    half = (pl.ds(0, 384), pl.ds(384, 384))
    strip = pl.ds(pl.multiple_of(768 + 64 * y, 64), 64)
    w_pairs = ((1, 0), (1, 1), (2, 1), (2, 0), (3, 0), (3, 1))

    def w_ring(src, slot, n, to):
        i, h = w_pairs[n]
        return remote(src, wout.at[slot, half[h]], wsend.at[n], wrecv.at[i, h], f, to)

    def w_spread(src, h):
        if h == 0:
            w_ring(src.at[half[0]], x, 0, mr).start()
            w_ring(src.at[half[0]], x, 3, ml).start()
        else:
            w_ring(src.at[half[1]], x, 2, ml).start()
            w_ring(src.at[half[1]], x, 1, mr).start()

    def swap(h):
        rows = (half[0], half[1], strip)[h]
        return remote(wown.at[rows], wout.at[x, rows], ssend.at[h], srecv.at[h], g * 2 + 1 - c, mz)

    def strip_x(src, k):
        return remote(src.at[strip], wout.at[x, strip], qsend.at[k], qrecv.at[k], f, z * 4 + (x + k) % 4)

    def strip_y(k):
        to = (zh * 4 + (y + k) % 4) * 2 + c
        return remote(wout.at[:, strip], wout.at[:, strip], usend.at[k], urecv.at[k], to, m)

    own_w = [
        pltpu.make_async_copy(wown.at[pl.ds(0, 768)], wout.at[x, pl.ds(0, 768)], wloc.at[0]),
        pltpu.make_async_copy(wown.at[strip], wout.at[x, strip], wloc.at[1]),
    ]

    @pl.when(own)
    def _():
        own_w[1].start()
        for k in range(1, 4):
            strip_x(wown, k).start()
        w_spread(wown, 0)
        w_spread(wown, 1)
        own_w[0].start()

    @pl.when(jnp.logical_not(own))
    def _():
        swap(2).start()
        swap(0).start()
        swap(1).start()

    def a2a(ch, k):
        slot = (me + k) % 16
        return remote(sbuf.at[ch, slot], recv.at[ch, c, g], asend.at[ch, k], arecv.at[ch, g], *owner(slot))

    def forward(ch, k, src):
        slot = (g + 16 - k) % 16
        return remote(src, recv.at[ch, c, slot], fsend.at[ch, k], frecv.at[ch, k], sib, m)

    def keep(ch):
        return pltpu.make_async_copy(sbuf.at[ch, me], recv.at[ch, c, g], kloc.at[ch])

    for ch in range(2):
        if ch:
            pack(ch)

        def send(k, _, ch=ch):
            a2a(ch, k).start()
            return 0

        lax.fori_loop(1, 16, send, 0)
        keep(ch).start()
        forward(ch, 0, sbuf.at[ch, me]).start()

        if ch == 0:

            @pl.when(jnp.logical_not(own))
            def _():
                swap(2).wait_recv()
                for k in range(1, 4):
                    strip_x(wout.at[x], k).start()

    @pl.when(own)
    def _():
        own_w[1].wait()

    for k in range(1, 4):
        remote(wown.at[strip], wout.at[(x + 4 - k) % 4, strip], qsend.at[k], qrecv.at[k], f, m).wait_recv()
    for k in range(1, 4):
        strip_y(k).start()

    @pl.when(jnp.logical_not(own))
    def _():
        swap(0).wait_recv()
        w_spread(wout.at[x], 0)
        swap(1).wait_recv()
        w_spread(wout.at[x], 1)

    def w_arrived(n):
        i, h = w_pairs[n]
        slot = (x, xl, xr, xf)[i]
        remote(wown.at[half[h]], wout.at[slot, half[h]], wsend.at[n], wrecv.at[i, h], f, mr).wait_recv()

    def relay_tokens(ch):
        def relay(k, _):
            slot = (g + 16 - k) % 16
            remote(sbuf.at[ch, 0], recv.at[ch, c, slot], asend.at[ch, k], arecv.at[ch, slot], f, m).wait_recv()
            forward(ch, k, recv.at[ch, c, slot]).start()
            return 0

        lax.fori_loop(1, 16, relay, 0)

    def tokens_arrived(ch):
        keep(ch).wait()

        def wait(k, _):
            slot = (g + 16 - k) % 16
            remote(sbuf.at[ch, 0], recv.at[ch, 1 - c, slot], fsend.at[ch, k], frecv.at[ch, k], f, m).wait_recv()
            return 0

        lax.fori_loop(0, 16, wait, 0)

    relay_tokens(0)
    w_arrived(0)
    w_ring(wout.at[xl, half[0]], xl, 4, mr).start()
    w_arrived(2)
    w_ring(wout.at[xr, half[1]], xr, 5, ml).start()

    lane = lax.broadcasted_iota(jnp.int32, (128, 128), 1)
    line = lax.broadcasted_iota(jnp.int32, (128, 128), 0)
    first = lane < 64
    allowed = (lane < 64) == (line < 64)

    def shard_of(i):
        return (x + (i % 2) * 3 + (i // 2) * (1 + (i % 2) * 2)) % 4

    def prepare(ch):
        for s in range(2):
            for gh in range(2):
                block = recv[ch, s, 8 * gh : 8 * gh + 8].reshape(384, 512)
                rows = jnp.dot(order[1], block, preferred_element_type=F32).astype(BF).reshape(2, 2, 6, 16, 512)
                for h in range(2):
                    xs[ch, :, :, s, 16 * gh : 16 * gh + 16, 512 * h : 512 * h + 512] = rows[h]

        def norm(u, _):
            xhat, _ = standardize(xs[ch, 0, u].reshape(64, D).astype(F32))
            normed[pl.ds(pl.multiple_of(ch * 384 + u * 64, 64), 64), :] = (xhat * gain[...]).astype(BF)
            return 0

        lax.fori_loop(0, 6, norm, 0, unroll=2)
        for i in range(3):
            at = 384 * ch + 128 * i
            norm_t[:, at : at + 128] = normed[at : at + 128, :].T
            og_t[:, at : at + 128] = xs[ch, 1, 2 * i : 2 * i + 2].reshape(128, D).T

    def heads(ch, i):
        j = shard_of(i)
        at = 384 * ch
        if ch == 0:
            wt[i] = wout[j, :, 0:384].T
        proj[:, 0:384] = jnp.dot(normed[at : at + 384, :], wout[j, :, 0:384], preferred_element_type=F32).astype(BF)
        proj[:, 384:512] = jnp.dot(
            xs[ch, 1].reshape(384, D), wout[j, :, 384:512], preferred_element_type=F32
        ).astype(BF)
        for n in range(3):
            rows = slice(128 * n, 128 * n + 128)
            out, dq, dk, dv = attend(
                proj[rows, 0:128], proj[rows, 128:256], proj[rows, 256:384], proj[rows, 384:512], allowed, first
            )
            rows = slice(at + 128 * n, at + 128 * n + 128)
            back[i, rows, 0:128] = dq.astype(BF)
            back[i, rows, 128:256] = dk.astype(BF)
            back[i, rows, 256:384] = dv.astype(BF)
            ao[i, rows, :] = out.astype(BF)

    def to_sibling(ch):
        return remote(other.at[ch], rsib.at[ch], bsend.at[ch], brecv.at[ch], sib, m)

    def partial(ch, groups):
        for n in range(3):
            rows = slice(384 * ch + 128 * n, 384 * ch + 128 * n + 128)
            term = jnp.dot(back[groups[0], rows, :], wt[groups[0]], preferred_element_type=F32)
            for i in groups[1:]:
                term += jnp.dot(back[i, rows, :], wt[i], preferred_element_type=F32)
            term = term.reshape(2, 2, 32, D)
            if groups[0] == 0:
                part[2 * n : 2 * n + 2] = term
            else:
                part[2 * n : 2 * n + 2] += term
        if groups[-1] == 3:
            other[ch] = part[:, 1 - c].astype(BF)
            to_sibling(ch).start()

    def back_to(ch, k):
        n = (g + k) % 16
        fs, ms, slot = source(n)
        return remote(sret.at[ch, n], rret.at[ch, slot], csend.at[ch, k], crecv.at[ch, slot], fs, ms)

    def keep_back(ch):
        return pltpu.make_async_copy(sret.at[ch, g], rret.at[ch, me], kloc.at[2 + ch])

    def token_gradient(ch):
        to_sibling(ch).wait_recv()

        def token(u, total):
            xhat, rstd = standardize(xs[ch, 0, u, c].astype(F32))
            dn = part[u, c] + rsib[ch, u].astype(F32)
            bp = dn * gain[...]
            inner = bp - jnp.mean(bp, axis=-1, keepdims=True) - xhat * jnp.mean(bp * xhat, axis=-1, keepdims=True)
            tg[u] = (xs[ch, 1, u, c].astype(F32) + rstd * inner).astype(BF)
            return total + jnp.sum((dn * xhat).reshape(4, 8, D), axis=0)

        total = lax.fori_loop(0, 6, token, jnp.zeros((8, D), F32), unroll=2)
        if ch == 0:
            gacc[...] = total
        else:
            gacc[...] += total
        for gh in range(2):
            rows = slice(16 * gh, 16 * gh + 16)
            parts = [tg[:, rows, 256 * h : 256 * h + 256].reshape(96, 256) for h in range(4)]
            packed = jnp.dot(order[2], jnp.concatenate(parts, axis=0), preferred_element_type=F32)
            sret[ch, 8 * gh : 8 * gh + 8] = packed.astype(BF).reshape(8, 48, 256)

        def send(k, _):
            back_to(ch, k).start()
            return 0

        lax.fori_loop(1, 16, send, 0)
        keep_back(ch).start()

    def piece(ch, h, mm):
        rows = pl.ds(pl.multiple_of((mm % 4) * 64 + window(mm // 4, h) * 16, 16), 16)
        return tgrad.at[pl.ds(6 * ch, 6), rows, :]

    def kept(ch, h):
        return blk.at[ch, :, pl.ds(16 * h, 16), :]

    def pair(ch, h):
        return remote(kept(ch, h), piece(ch, h, m), psend.at[ch, h], precv.at[ch, h], f, mz)

    def ring(ch, r, src, mm, h, n, to):
        return remote(src, piece(ch, h, mm), rsend.at[ch, r, n], rrecv.at[ch, r, n], f, to)

    def own_out(ch, h):
        return pltpu.make_async_copy(kept(ch, h), piece(ch, h, m), oloc.at[ch, h])

    def gather_own(ch):
        keep_back(ch).wait()

        def received(k, _):
            slot = (me + k) % 16
            remote(sret.at[ch, 0], rret.at[ch, slot], csend.at[ch, k], crecv.at[ch, slot], f, m).wait_recv()
            return 0

        lax.fori_loop(1, 16, received, 0)
        for gh in range(2):
            block = rret[ch, 8 * gh : 8 * gh + 8].reshape(384, 256)
            rows = jnp.dot(order[3], block, preferred_element_type=F32).astype(BF).reshape(4, 6, 16, 256)
            for h in range(4):
                blk[ch, :, 16 * gh : 16 * gh + 16, 256 * h : 256 * h + 256] = rows[h]
        pair(ch, 0).start()
        pair(ch, 1).start()
        ring(ch, 0, kept(ch, 0), m, 0, 0, mr).start()
        ring(ch, 0, kept(ch, 1), m, 1, 2, ml).start()
        ring(ch, 0, kept(ch, 1), m, 1, 1, mr).start()
        ring(ch, 0, kept(ch, 0), m, 0, 3, ml).start()
        own_out(ch, 0).start()
        own_out(ch, 1).start()

    def gather_pair(ch):
        def arrived(h):
            remote(kept(ch, h), piece(ch, h, mz), psend.at[ch, h], precv.at[ch, h], f, mz).wait_recv()

        arrived(0)
        ring(ch, 1, piece(ch, 0, mz), mz, 0, 0, mr).start()
        ring(ch, 1, piece(ch, 0, mz), mz, 0, 3, ml).start()
        arrived(1)
        ring(ch, 1, piece(ch, 1, mz), mz, 1, 2, ml).start()
        ring(ch, 1, piece(ch, 1, mz), mz, 1, 1, mr).start()

    def base(r):
        return (z if r == 0 else 1 - z) * 4

    def arrived(ch, r, mm, h, n):
        ring(ch, r, piece(ch, h, base(r) + mm), base(r) + mm, h, n, mr).wait_recv()

    def gather_relay(ch, r):
        arrived(ch, r, xl, 0, 0)
        ring(ch, r, piece(ch, 0, base(r) + xl), base(r) + xl, 0, 4, mr).start()
        arrived(ch, r, xr, 1, 2)
        ring(ch, r, piece(ch, 1, base(r) + xr), base(r) + xr, 1, 5, ml).start()

    def weights(i):
        j = shard_of(i)

        left = jnp.dot(norm_t[...], back[i], preferred_element_type=F32).astype(BF)
        grads[j, :, :, :, :, 0:384] = left.reshape(4, 4, 2, 32, 384)
        left = jnp.dot(og_t[...], ao[i], preferred_element_type=F32).astype(BF)
        grads[j, :, :, :, :, 384:512] = left.reshape(4, 4, 2, 32, 128)
        y_far(i, 0).start()
        y_far(i, 1).start()

    def y_far(i, h):
        src = grads.at[shard_of(i), pl.ds(2 * h, 2), yf]
        return remote(src, gf.at[i, h], y1send.at[i, h], y1recv.at[i, h], fr if h == 0 else fl, m)

    def y_near(i, h):
        src = grads.at[shard_of(i), :, yr if h == 0 else yl]
        return remote(src, gn.at[i, h], y2send.at[i, h], y2recv.at[i, h], fr if h == 0 else fl, m)

    def y_step(i, _):
        j = shard_of(i)
        for h in range(2):
            y_far(i, h).wait_recv()
            to = yr if h == 0 else yl
            for a in range(2):
                total = grads[j, 2 * h + a, to].astype(F32) + gf[i, h, a].astype(F32)
                grads[j, 2 * h + a, to] = total.astype(BF)
            y_near(i, h).start()
        return 0

    def z_copy(i, n):
        to = ((n // 2) * 4 + y) * 2 + n % 2
        return remote(gz.at[i, n], gzr.at[i, zi], zsend.at[i, n], zrecv.at[i, zi], to, c * 4 + x)

    def zg_copy(n):
        to = ((n // 2) * 4 + y) * 2 + n % 2
        return remote(gzg.at[n], gzgr.at[zi], zsend.at[4, n], zrecv.at[4, zi], to, c * 4 + x)

    def z_self(n):
        return jnp.logical_and(n == zh * 2 + c, own)

    def own_z(i):
        return pltpu.make_async_copy(gz.at[i, zh * 2 + c], gzr.at[i, zi], zloc.at[i])

    def own_zg():
        return pltpu.make_async_copy(gzg.at[zh * 2 + c], gzgr.at[zi], zloc.at[4])

    def z_step(i, _):
        j = shard_of(i)
        for h in range(2):
            y_near(i, h).wait_recv()
        for a in range(4):
            total = grads[j, a, y].astype(F32) + (gn[i, 0, a].astype(F32) + gn[i, 1, a].astype(F32))
            gz[i, 2 * a : 2 * a + 2] = total.astype(BF)

        def z_send(n, _):
            @pl.when(jnp.logical_not(z_self(n)))
            def _():
                z_copy(i, n).start()

            return 0

        lax.fori_loop(0, 8, z_send, 0)

        @pl.when(own)
        def _():
            own_z(i).start()

        return 0

    def z_wait(i, src, dst):
        def wait(n, _):
            @pl.when(jnp.logical_not(jnp.logical_and(n == zi, own)))
            def _():
                remote(src, dst(n), zsend.at[i, 0], zrecv.at[i, n], f, m).wait_recv()

            return 0

        lax.fori_loop(0, 8, wait, 0)

    def sum8(terms):
        while len(terms) > 1:
            terms = [a + b for a, b in zip(terms[::2], terms[1::2])]
        return terms[0]

    def x_copy(i):
        return remote(gxs.at[i], gxr.at[i], xsend.at[i], xrecv.at[i], f, z * 4 + shard_of(i))

    def x_step(i, _):
        z_wait(i, gz.at[0, 0], lambda n: gzr.at[i, n])

        @pl.when(own)
        def _():
            own_z(i).wait()

        gxs[i] = sum8([gzr[i, k].astype(F32) for k in range(8)]).astype(BF)

        @pl.when(jnp.asarray(i) > 0)
        def _():
            x_copy(i).start()

        return 0

    def gain_y(k):
        yk = (y + k) % 4
        return remote(gcol.at[:, yk], ggr.at[k], gsend.at[k], grecv.at[k], (zh * 4 + yk) * 2 + c, m)

    own_gain = pltpu.make_async_copy(gcol.at[:, y], ggr.at[0], gloc)

    def gain_x(k):
        return remote(gxg, gxgr.at[k], hsend.at[k], hrecv.at[k], f, z * 4 + (x + k) % 4)

    to_sib_gain = remote(gvec, gvecr, vsend, vrecv, sib, m)

    def sent_early():
        for ch in range(2):
            pair(ch, 0).wait_send()
            pair(ch, 1).wait_send()
            own_out(ch, 0).wait()
            own_out(ch, 1).wait()
            to_sibling(ch).wait_send()

            def sent(k, _, ch=ch):
                a2a(ch, k).wait_send()
                back_to(ch, k).wait_send()
                forward(ch, k, recv.at[ch, c, (g + 16 - k) % 16]).wait_send()
                return 0

            lax.fori_loop(1, 16, sent, 0)
            forward(ch, 0, sbuf.at[ch, me]).wait_send()
        to_sib_gain.wait_send()
        for n in range(6):
            i, h = w_pairs[n]
            w_ring(wown.at[half[h]], x, n, mr).wait_send()

        @pl.when(jnp.logical_not(own))
        def _():
            for h in range(3):
                swap(h).wait_send()

        for k in range(1, 4):
            gain_y(k).wait_send()
            strip_x(wown, k).wait_send()
            strip_y(k).wait_send()

        def y_sent(i, _):
            for h in range(2):
                y_far(i, h).wait_send()
                y_near(i, h).wait_send()
            return 0

        lax.fori_loop(0, 4, y_sent, 0)

        def z_sent(n, _):
            @pl.when(jnp.logical_not(z_self(n)))
            def _():
                for i in range(4):
                    z_copy(i, n).wait_send()
                zg_copy(n).wait_send()

            return 0

        lax.fori_loop(0, 8, z_sent, 0)

    p_in[1].wait()
    tokens_arrived(0)
    prepare(0)

    @pl.when(own)
    def _():
        own_w[0].wait()

    for k in range(1, 4):
        rows = pl.ds(pl.multiple_of(768 + 64 * ((y + 4 - k) % 4), 64), 64)
        remote(wout.at[:, rows], wout.at[:, rows], usend.at[k], urecv.at[k], f, m).wait_recv()

    def shard_arrived(i):
        for h in range(2):
            waited = jnp.logical_or(i == 0, jnp.logical_and(i < 3, h == i - 1))

            @pl.when(jnp.logical_not(waited))
            def _():
                slot = shard_of(i)
                remote(wown.at[half[h]], wout.at[slot, half[h]], wsend.at[0], wrecv.at[i, h], f, mr).wait_recv()

    def first_heads(i, _):
        shard_arrived(i)
        heads(0, i)

        @pl.when(i == 2)
        def _():
            partial(0, (0, 1, 2))
            relay_tokens(1)

        return 0

    def second_heads(i, _):
        heads(1, i)

        @pl.when(i == 0)
        def _():
            token_gradient(0)

        return 0

    def y_steps(first, last):
        lax.fori_loop(first, last, lambda i, _: y_step((i + 1) % 4, 0), 0)

    def z_steps(first, last):
        lax.fori_loop(first, last, lambda i, _: z_step((i + 1) % 4, 0), 0)

    lax.fori_loop(0, 4, first_heads, 0)
    partial(0, (3,))
    tokens_arrived(1)
    prepare(1)
    lax.fori_loop(0, 4, second_heads, 0)
    partial(1, (0, 1, 2, 3))
    weights(1)
    weights(2)
    token_gradient(1)
    gvec[...] = jnp.broadcast_to(jnp.sum(gacc[...], axis=0, keepdims=True), (8, D))
    to_sib_gain.start()
    gather_own(0)
    weights(3)
    weights(0)
    gather_pair(0)
    y_steps(0, 1)
    y_steps(1, 2)
    gather_relay(0, 0)
    to_sib_gain.wait_recv()
    gcol[...] = jnp.broadcast_to(gvec[0:1] + gvecr[0:1], (128, D)).T.astype(BF).reshape(4, 4, 2, 32, 128)
    for k in range(1, 4):
        gain_y(k).start()
    own_gain.start()
    y_steps(2, 3)
    gather_own(1)
    y_steps(3, 4)
    z_steps(0, 1)
    gather_pair(1)
    z_steps(1, 2)
    gather_relay(0, 1)
    own_gain.wait()
    for k in range(1, 4):
        remote(ggr.at[0], ggr.at[k], gsend.at[k], grecv.at[k], f, m).wait_recv()
    total = sum8([ggr[k].astype(F32) for k in range(4)])
    gzg[...] = total.astype(BF).reshape(8, 32, 128)

    def zg_send(n, _):
        @pl.when(jnp.logical_not(z_self(n)))
        def _():
            zg_copy(n).start()

        return 0

    lax.fori_loop(0, 8, zg_send, 0)

    @pl.when(own)
    def _():
        own_zg().start()

    gather_relay(1, 0)
    z_steps(2, 4)
    lax.fori_loop(1, 4, x_step, 0)
    z_wait(4, gzg.at[0], lambda n: gzgr.at[n])

    @pl.when(own)
    def _():
        own_zg().wait()

    gxg[...] = sum8([gzgr[k].astype(F32) for k in range(8)]).astype(BF)
    for k in range(1, 4):
        gain_x(k).start()
    gather_relay(1, 1)
    x_step(0, 0)
    sent_early()

    for i in range(1, 4):
        x_copy(i).wait_recv()
    total = sum8([gxs[0].astype(F32)] + [gxr[i].astype(F32) for i in range(1, 4)])
    for j in range(3):
        gq[j] = total[:, 128 * j : 128 * j + 128]
    go[...] = total[:, 384:512]
    for k in range(1, 4):
        gain_x(k).wait_recv()
    total = sum8([gxg[...].astype(F32)] + [gxgr[k].astype(F32) for k in range(1, 4)])
    gg[...] = jnp.broadcast_to(total[0:32, 0:1], (32, 128))

    for ch in range(2):
        for r in range(2):
            arrived(ch, r, xl, 1, 1)
            arrived(ch, r, xr, 0, 3)
            arrived(ch, r, xf, 0, 4)
            arrived(ch, r, xf, 1, 5)
            for n, (mm, h) in enumerate(((x, 0), (x, 1), (x, 1), (x, 0), (xl, 0), (xr, 1))):
                ring(ch, r, piece(ch, h, base(r) + mm), base(r) + mm, h, n, mr).wait_send()
    for k in range(1, 4):
        gain_x(k).wait_send()
        x_copy(k).wait_send()


def sublayer(tok, og, qkvw, outw, gain):
    vm = pl.BlockSpec(memory_space=pltpu.VMEM)
    hbm = pl.BlockSpec(memory_space=pltpu.HBM)
    dma = pltpu.SemaphoreType.DMA
    perms = jnp.asarray(np.stack([PACK, GROUP, REPACK, UNPACK]), BF)
    bf = lambda *shape: pltpu.VMEM(shape, BF)
    return pl.pallas_call(
        sublayer_kernel,
        out_shape=(
            jax.ShapeDtypeStruct((12, 256, D), BF),
            jax.ShapeDtypeStruct((3, 32, 128), F32),
            jax.ShapeDtypeStruct((32, 128), F32),
            jax.ShapeDtypeStruct((32, 128), F32),
        ),
        in_specs=[hbm] * 4 + [vm, hbm],
        out_specs=(hbm, vm, vm, vm),
        scratch_shapes=[
            bf(4, 384, 384),
            bf(2, 2, 6, 32, D),
            bf(2, 16, 48, 512),
            bf(2, 2, 16, 48, 512),
            bf(D, 512),
            bf(4, D, 512),
            bf(4, 384, D),
            bf(128, D),
            bf(2, 2, 6, 2, 32, D),
            bf(768, D),
            bf(D, 768),
            bf(D, 768),
            bf(384, 512),
            bf(4, 768, 384),
            bf(4, 768, 128),
            pltpu.VMEM((6, 2, 32, D), F32),
            bf(2, 6, 32, D),
            bf(2, 6, 32, D),
            bf(6, 32, D),
            pltpu.VMEM((8, D), F32),
            pltpu.VMEM((8, D), F32),
            pltpu.VMEM((8, D), F32),
            bf(4, 4, 2, 32, 128),
            bf(2, 16, 48, 256),
            bf(2, 16, 48, 256),
            bf(2, 6, 32, D),
            bf(4, 4, 4, 2, 32, 512),
            bf(4, 2, 2, 2, 32, 512),
            bf(4, 2, 4, 2, 32, 512),
            bf(4, 4, 2, 32, 128),
            bf(4, 8, 32, 512),
            bf(4, 8, 32, 512),
            bf(8, 32, 128),
            bf(8, 32, 128),
            bf(4, 32, 512),
            bf(4, 32, 512),
            bf(32, 128),
            bf(4, 32, 128),
            dma((12,)),
            dma((2,)),
            dma((4,)),
            dma((2,)),
            dma((2, 2)),
            dma((5,)),
            dma,
            dma((2, 16)),
            dma((2, 16)),
            dma((2, 16)),
            dma((2, 16)),
            dma((3,)),
            dma((3,)),
            dma((4,)),
            dma((4,)),
            dma((4,)),
            dma((4,)),
            dma((6,)),
            dma((4, 2)),
            dma((2,)),
            dma((2,)),
            dma,
            dma,
            dma((2, 16)),
            dma((2, 16)),
            dma((2, 2)),
            dma((2, 2)),
            dma((2, 2, 6)),
            dma((2, 2, 6)),
            dma((4, 2)),
            dma((4, 2)),
            dma((4, 2)),
            dma((4, 2)),
            dma((4,)),
            dma((4,)),
            dma((5, 8)),
            dma((5, 8)),
            dma((4,)),
            dma((4,)),
            dma((4,)),
            dma((4,)),
        ],
        compiler_params=pltpu.CompilerParams(
            collective_id=0, has_side_effects=True, vmem_limit_bytes=58 * 2**20
        ),
        name="sublayer",
    )(tok, og, qkvw, outw, gain, perms)


def finish_kernel(tgrad, gq, go, gg, out, oq, oo, og, buf, insem, outsem):
    into = [pltpu.make_async_copy(tgrad.at[pl.ds(2 * n, 2)], buf.at[pl.ds(2 * n, 2)], insem.at[n]) for n in range(6)]
    away = [pltpu.make_async_copy(buf.at[pl.ds(2 * n, 2)], out.at[pl.ds(2 * n, 2)], outsem.at[n]) for n in range(6)]
    for copy in into:
        copy.start()
    oq[...] = gq[...]
    oo[...] = go[...]
    og[...] = gg[...].T[0:1, :]
    for n in range(6):
        into[n].wait()
        away[n].start()
    for copy in away:
        copy.wait()


def finish(tgrad, gq, go, gg):
    vm = pl.BlockSpec(memory_space=pltpu.VMEM)
    hbm = pl.BlockSpec(memory_space=pltpu.HBM)
    return pl.pallas_call(
        finish_kernel,
        out_shape=(
            jax.ShapeDtypeStruct((12, 256, D), BF),
            jax.ShapeDtypeStruct((3, 32, 128), F32),
            jax.ShapeDtypeStruct((32, 128), F32),
            jax.ShapeDtypeStruct((1, 32), F32),
        ),
        in_specs=[hbm, vm, vm, vm],
        out_specs=(hbm, vm, vm, vm),
        scratch_shapes=[
            pltpu.VMEM((12, 256, D), BF),
            pltpu.SemaphoreType.DMA((6,)),
            pltpu.SemaphoreType.DMA((6,)),
        ],
        compiler_params=pltpu.CompilerParams(vmem_limit_bytes=58 * 2**20),
        name="finish",
    )(tgrad, gq, go, gg)


def shards(tokens, output_gradient, gain, qkv_weight, out_weight):
    clips, frames, patches, width = tokens.shape
    results = sublayer(
        tokens.reshape(12, 256, D),
        output_gradient.reshape(12, 256, D),
        jnp.transpose(qkv_weight, (1, 0, 2)),
        out_weight,
        gain.reshape(1, D),
    )
    tgrad, gq, go, gg = finish(*results)
    return (
        tgrad.reshape(clips, frames, patches, width),
        jnp.transpose(gq, (1, 0, 2)),
        go.T,
        gg.reshape(32),
    )


def solution(mesh):
    in_specs = (
        P(None, "frame", None, None),
        P(None, "frame", None, None),
        P(),
        P(None, None, "mlp"),
        P("mlp", None),
    )
    out_specs = (
        P(None, "frame", None, None),
        P("frame", None, "mlp"),
        P("mlp", "frame"),
        P("frame"),
    )
    return jax.shard_map(shards, mesh=mesh, in_specs=in_specs, out_specs=out_specs, check_vma=False)
```
